32 devices in a mesh: grp: 2 (over y), psg: 8 (over z, x), qry: 2 (over core).
Axes of the slice: x: 2, y: 2, z: 4, core: 2. Of those that a mesh axis runs over, the one named last changes fastest.
Arguments:
- queries: bfloat16 [256, 32, 128], P(('grp', 'psg', 'qry')), parts along dimension 0, may hold values from -0.5 to 0.5
- passages: bfloat16 [2048, 64, 128], P(('grp', 'psg')), parts along dimension 0, may hold values from -6 to 6
- lengths: int32 [2048], P(('grp', 'psg')), parts along dimension 0, may hold values from 8 to 64
- candidates: int32 [2, 128, 32], P('qry', ('grp', 'psg')), parts along dimension 1, may hold values from 0 to 31, as said below
Outputs:
- scores: float32 [32, 8, 32, 2, 16], P(('grp', 'psg', 'qry')), parts along dimension 0
The draws below stay inside these ranges and needn't reach their ends.
There are 2 independent parts, one for each index of `grp`. The reference program is written for one: setup_inputs(seed, part) draws one part's arguments, and reference() takes and returns one part's arrays. A program takes and returns all parts, laid end to end along the dimension named above; each array names one. Nothing has to cross between parts.
Inputs may be any that keep to these rules, and one draw needn't show every extreme that they name: `candidates`: in the 8 rows of one passage shard and one half, every owner id // 4 is named exactly 32 times, always with the same id.
All inputs are finite; a program needn't handle non-finite values.
Results may differ from the reference program's by a relative error of at most 0.0003.
Values may be sent and summed in bfloat16 or wider, within the bound.
No kernel may reach another device: no remote copies, remote signals or barrier semaphores. Data moves between devices by JAX's collectives and lax.ppermute only.
A program may use at most 64 MiB of HBM per device.

```python
import jax
import jax.numpy as jnp
from jax import lax

DIM = 128
QT = 32
PT = 64
QB = 2
QBD = 4
PBS = 16
KB = 32
PBD = 8
NP = 1024
NQ = 128
N_PSG = 8
N_QRY = 2


def draw_lengths(key, part):
    key = jax.random.fold_in(key, 5)
    drawn = jax.random.randint(key, (N_PSG * PBD * PBS,), PT // 8, PT + 1)
    return drawn.at[0].set(PT).astype(jnp.int32)


def draw_candidates(key, part):
    key = jax.random.fold_in(key, 11)
    entries = PBD * KB

    def one_device(device_key):
        shuffle_key, block_key = jax.random.split(device_key)
        owners = jax.random.permutation(shuffle_key, jnp.arange(entries, dtype=jnp.int32) % N_PSG)
        chosen = jax.random.randint(block_key, (N_PSG,), 0, QBD)
        return (owners * QBD + chosen[owners]).reshape(PBD, KB)
    device_keys = jax.random.split(key, N_QRY * N_PSG)
    rows = jax.vmap(one_device)(device_keys)
    return rows.reshape(N_QRY, N_PSG * PBD, KB).astype(jnp.int32)


def block_scale(key, shape, cuts, least, high):
    level, own = 1.0, jax.random.fold_in(key, 6)
    for dim, shards_of in cuts:
        steps = jnp.exp(jax.random.uniform(jax.random.fold_in(own, dim), (shards_of,), jnp.float32, least / len(cuts), high / len(cuts)))
        level = level * jnp.repeat(steps, shape[dim] // shards_of).reshape([-1 if axis == dim else 1 for axis in range(len(shape))])
    return level


def bell_draw(stream_key, shape, spread, limit, pieces=(), held_as=jnp.bfloat16):
    level = block_scale(stream_key, shape, pieces, -0.22, 0.18) if pieces else 1.0
    values = jax.random.normal(stream_key, shape, jnp.float32) * spread * level
    return jnp.minimum(jnp.maximum(values, -limit), limit).astype(held_as)


def setup_inputs(seed: int = 0, part: int = 0) -> dict:
    seeds = jax.random.split(jax.random.key(seed), 5)
    part_keys = jax.random.split(jax.random.fold_in(seeds[4], part), 5)
    queries = bell_draw(part_keys[0], (NQ, QT, DIM), DIM ** -0.5, 0.5, ((0, 16),))
    passages = bell_draw(part_keys[1], (NP, PT, DIM), 1.0, 6.0, ((0, 8),))
    lengths = draw_lengths(jax.random.fold_in(jax.random.fold_in(seeds[4], part), 71), part)
    candidates = draw_candidates(jax.random.fold_in(jax.random.fold_in(seeds[4], part), 71), part)
    return dict(queries=queries, passages=passages, lengths=lengths, candidates=candidates)


def device_tiles(query_sel, passage_shard, length_shard):
    query_rows = query_sel.reshape(PBD, KB * QB * QT, DIM).astype(jnp.float32)
    passage_rows = passage_shard.reshape(PBD, PBS * PT, DIM).astype(jnp.float32)
    valid = jnp.arange(PT, dtype=jnp.int32)[None, None, :] < length_shard.reshape(PBD, PBS, 1)

    def one_row(items):
        left, right, keep = items
        dots = jnp.einsum("ad,bd->ab", left, right)
        dots = dots.reshape(KB * QB, QT, PBS, PT)
        dots = jnp.where(keep[None, None, :, :], dots, -jnp.inf)
        return jnp.sum(jnp.max(dots, axis=3), axis=1) * (1.0 / QT)

    tiles = lax.map(one_row, (query_rows, passage_rows, valid))
    return tiles.reshape(PBD * KB, QB, PBS)


def reference(queries, passages, lengths, candidates):
    per_owner = QB * QBD
    entries = PBD * KB
    slots = entries // N_PSG
    halves = []
    for half in range(N_QRY):
        def one_device(index):
            rows = lax.dynamic_slice_in_dim(candidates[half], index * PBD, PBD, 0).reshape(-1)
            owners = rows // QBD
            blocks = rows % QBD
            start = (owners * N_QRY + half) * per_owner + blocks * QB
            picked = start[:, None] + jnp.arange(QB, dtype=jnp.int32)[None, :]
            query_sel = queries[picked]
            passage_shard = lax.dynamic_slice_in_dim(passages, index * PBD * PBS, PBD * PBS, 0)
            length_shard = lax.dynamic_slice_in_dim(lengths, index * PBD * PBS, PBD * PBS, 0)
            tiles = device_tiles(query_sel, passage_shard, length_shard)
            order = jnp.arange(entries, dtype=jnp.int32)
            same = owners[:, None] == owners[None, :]
            earlier = order[None, :] < order[:, None]
            rank = jnp.sum(jnp.where(same & earlier, 1, 0), axis=1).astype(jnp.int32)
            buffer = jnp.zeros((N_PSG, slots, QB, PBS), jnp.float32)
            return buffer.at[owners, rank].set(tiles)

        halves.append(lax.map(one_device, jnp.arange(N_PSG, dtype=jnp.int32)))
    stacked = jnp.stack(halves)
    moved = jnp.transpose(stacked, (2, 0, 1, 3, 4, 5))
    return moved.reshape(N_PSG * N_QRY, N_PSG, slots, QB, PBS)
```

```python
import functools

import jax
import jax.numpy as jnp
from jax import lax
from jax.experimental import pallas as pl
from jax.experimental.pallas import tpu as pltpu
from jax.sharding import PartitionSpec as P

DIM = 128
QT = 32
PT = 64
QB = 2
QBD = 4
PBS = 16
KB = 32
LANES = 128
GROUP = 8


def score_kernel(first_ref, cand_ref, len_ref, q_ref, p_ref, out_ref, sel_ref, max_ref):
    shards = q_ref.shape[0]
    rows = cand_ref.shape[0]
    count = p_ref.shape[0]
    tokens = QB * QT
    cand = cand_ref[...]
    owner = cand // QBD
    block = cand - owner * QBD
    lane = lax.broadcasted_iota(jnp.int32, (rows, LANES), 1)
    sub = lax.broadcasted_iota(jnp.int32, (rows, LANES), 0)

    for o in range(shards):
        mine = owner == first_ref[0] + o
        named = jnp.max(jnp.where(mine, block, 0))
        sel_ref[o * tokens:(o + 1) * tokens, :] = q_ref[o, pl.ds(named * tokens, tokens), :]
        named_here = jnp.sum(jnp.where(mine, 1.0, 0.0), axis=1, keepdims=True)
        upto = jnp.broadcast_to(named_here, (rows, LANES))
        step = 1
        while step < rows:
            upto = upto + jnp.where(sub >= step, pltpu.roll(upto, step, 0), 0.0)
            step *= 2
        row_of_slot = jnp.sum(jnp.where(upto <= lane.astype(jnp.float32), 1.0, 0.0), axis=0, keepdims=True)
        out_ref[o, QB:QB + 1, :] = row_of_slot

    sel = sel_ref[...]
    u = lax.broadcasted_iota(jnp.int32, (PT, 1), 0)
    for g in range(count // GROUP):
        left = p_ref[g * GROUP:(g + 1) * GROUP].reshape(GROUP * PT, DIM)
        dots = lax.dot_general(left, sel, (((1,), (1,)), ((), ())), preferred_element_type=jnp.float32)
        for i in range(GROUP):
            live = u < len_ref[g * GROUP + i]
            best = jnp.where(live, dots[i * PT:(i + 1) * PT], -jnp.inf)
            max_ref[g * GROUP + i:g * GROUP + i + 1, :] = jnp.max(best, axis=0, keepdims=True)

    best = max_ref[...]
    high = best.astype(jnp.bfloat16)
    rest = best - high.astype(jnp.float32)
    mid = rest.astype(jnp.bfloat16)
    low = (rest - mid.astype(jnp.float32)).astype(jnp.bfloat16)
    query = lax.broadcasted_iota(jnp.int32, (shards * QB, shards * tokens), 0)
    token = lax.broadcasted_iota(jnp.int32, (shards * QB, shards * tokens), 1)
    ones = jnp.where(token // QT == query, 1.0, 0.0).astype(jnp.bfloat16)
    total = jnp.zeros((shards * QB, count), jnp.float32)
    for part in (low, mid, high):
        total = total + lax.dot_general(ones, part, (((1,), (1,)), ((), ())), preferred_element_type=jnp.float32)
    total = total * (1.0 / QT)
    for o in range(shards):
        out_ref[o, 0:QB, :] = total[o * QB:(o + 1) * QB]


def place_kernel(in_ref, out_ref):
    shards = in_ref.shape[0]
    slots = out_ref.shape[-1]
    m = lax.broadcasted_iota(jnp.int32, (PBS, LANES), 0)
    for j in range(shards):
        row = in_ref[j, QB:QB + 1, :].astype(jnp.int32)
        where = jnp.minimum(row * PBS, LANES - PBS) + m
        for i in range(QB):
            tile = jnp.broadcast_to(in_ref[j, i:i + 1, :], (PBS, LANES))
            out_ref[j, i] = jnp.take_along_axis(tile, where, axis=1)[:, :slots]


def per_device(queries, passages, lengths, candidates):
    shards = lax.axis_size("psg")
    count = passages.shape[0]
    rows = count // PBS
    slots = rows * KB // shards
    tokens = QB * QT
    mine = queries.reshape(1, QBD * tokens, DIM)
    gathered = lax.all_to_all(
        jnp.broadcast_to(mine, (shards, QBD * tokens, DIM)), "psg", split_axis=0, concat_axis=0, tiled=True
    )
    vmem = pl.BlockSpec(memory_space=pltpu.VMEM)
    some = min(shards, 8)
    smem = pl.BlockSpec(memory_space=pltpu.SMEM)
    score = pl.pallas_call(
        score_kernel,
        out_shape=jax.ShapeDtypeStruct((some, QB + 1, LANES), jnp.float32),
        in_specs=[smem, vmem, smem, vmem, vmem],
        out_specs=vmem,
        scratch_shapes=[
            pltpu.VMEM((some * tokens, DIM), jnp.bfloat16),
            pltpu.VMEM((count, some * tokens), jnp.float32),
        ],
        compiler_params=pltpu.CompilerParams(vmem_limit_bytes=40 * 1024 * 1024),
    )

    def score_some(items):
        first, some_queries = items
        return score(first, candidates.reshape(rows, KB), lengths, some_queries, passages)

    firsts = some * jnp.arange(shards // some, dtype=jnp.int32)[:, None]
    if shards == some:
        tiles = score_some((firsts[0], gathered))
    else:
        tiles = lax.map(score_some, (firsts, gathered.reshape(shards // some, some, QBD * tokens, DIM)))
        tiles = tiles.reshape(shards, QB + 1, LANES)
    received = lax.all_to_all(tiles, "psg", split_axis=0, concat_axis=0, tiled=True)
    placed = pl.pallas_call(
        place_kernel,
        out_shape=jax.ShapeDtypeStruct((shards, QB, PBS, slots), jnp.float32),
        in_specs=[vmem],
        out_specs=vmem,
    )(received)
    return placed.transpose(0, 3, 1, 2)[None]


def solution(mesh):
    return jax.shard_map(
        per_device,
        mesh=mesh,
        in_specs=(
            P(("grp", "psg", "qry"), None, None),
            P(("grp", "psg"), None, None),
            P(("grp", "psg")),
            P("qry", ("grp", "psg"), None),
        ),
        out_specs=P(("grp", "psg", "qry"), None, None, None, None),
        check_vma=False,
    )
```

```python
import jax
import jax.numpy as jnp
from jax import lax
from jax.experimental import pallas as pl
from jax.experimental.pallas import tpu as pltpu
from jax.sharding import PartitionSpec as P

DIM = 128
QT = 32
PT = 64
QB = 2
QBD = 4
PBS = 16
KB = 32
LANES = 128
GROUP = 8


def score_kernel(owners_ref, cand_ref, len_ref, p_ref, *refs):
    some = (len(refs) - 2) // 2
    q_refs, out_refs = refs[:some], refs[some:2 * some]
    sel_ref, max_ref = refs[2 * some:]
    rows = cand_ref.shape[0]
    count = p_ref.shape[0]
    tokens = QB * QT
    cand = cand_ref[...]
    owner = cand // QBD
    block = cand - owner * QBD
    lane = lax.broadcasted_iota(jnp.int32, (rows, LANES), 1)
    sub = lax.broadcasted_iota(jnp.int32, (rows, LANES), 0)

    for k in range(some):
        mine = owner == owners_ref[k]
        named = jnp.max(jnp.where(mine, block, 0))
        sel_ref[k * tokens:(k + 1) * tokens, :] = q_refs[k][pl.ds(named * tokens, tokens), :]
        named_here = jnp.sum(jnp.where(mine, 1.0, 0.0), axis=1, keepdims=True)
        upto = jnp.broadcast_to(named_here, (rows, LANES))
        step = 1
        while step < rows:
            upto = upto + jnp.where(sub >= step, pltpu.roll(upto, step, 0), 0.0)
            step *= 2
        row_of_slot = jnp.sum(jnp.where(upto <= lane.astype(jnp.float32), 1.0, 0.0), axis=0, keepdims=True)
        out_refs[k][QB:QB + 1, :] = row_of_slot

    sel = sel_ref[...]
    u = lax.broadcasted_iota(jnp.int32, (PT, 1), 0)
    for g in range(count // GROUP):
        left = p_ref[g * GROUP:(g + 1) * GROUP].reshape(GROUP * PT, DIM)
        dots = lax.dot_general(left, sel, (((1,), (1,)), ((), ())), preferred_element_type=jnp.float32)
        for i in range(GROUP):
            live = u < len_ref[g * GROUP + i]
            best = jnp.where(live, dots[i * PT:(i + 1) * PT], -jnp.inf)
            max_ref[g * GROUP + i:g * GROUP + i + 1, :] = jnp.max(best, axis=0, keepdims=True)

    best = max_ref[...]
    high = best.astype(jnp.bfloat16)
    rest = best - high.astype(jnp.float32)
    mid = rest.astype(jnp.bfloat16)
    low = (rest - mid.astype(jnp.float32)).astype(jnp.bfloat16)
    query = lax.broadcasted_iota(jnp.int32, (some * QB, some * tokens), 0)
    token = lax.broadcasted_iota(jnp.int32, (some * QB, some * tokens), 1)
    ones = jnp.where(token // QT == query, 1.0, 0.0).astype(jnp.bfloat16)
    total = jnp.zeros((some * QB, count), jnp.float32)
    for part in (low, mid, high):
        total = total + lax.dot_general(ones, part, (((1,), (1,)), ((), ())), preferred_element_type=jnp.float32)
    total = total * (1.0 / QT)
    for k in range(some):
        out_refs[k][0:QB, :] = total[k * QB:(k + 1) * QB]


def score(owners, candidates, lengths, passages, blocks):
    some = len(blocks)
    count = passages.shape[0]
    smem = pl.BlockSpec(memory_space=pltpu.SMEM)
    vmem = pl.BlockSpec(memory_space=pltpu.VMEM)
    return pl.pallas_call(
        score_kernel,
        out_shape=[jax.ShapeDtypeStruct((QB + 1, LANES), jnp.float32)] * some,
        in_specs=[smem, vmem, smem, vmem] + [vmem] * some,
        out_specs=[vmem] * some,
        scratch_shapes=[
            pltpu.VMEM((some * QB * QT, DIM), jnp.bfloat16),
            pltpu.VMEM((count, some * QB * QT), jnp.float32),
        ],
        compiler_params=pltpu.CompilerParams(vmem_limit_bytes=40 * 1024 * 1024),
    )(owners, candidates, lengths, passages, *blocks)


def place_kernel(shards_ref, *refs):
    in_refs, out_ref = refs[:-1], refs[-1]
    slots = out_ref.shape[-1]
    m = lax.broadcasted_iota(jnp.int32, (PBS, LANES), 0)
    for k, in_ref in enumerate(in_refs):
        row = in_ref[QB:QB + 1, :].astype(jnp.int32)
        where = jnp.minimum(row * PBS, LANES - PBS) + m
        for i in range(QB):
            tile = jnp.broadcast_to(in_ref[i:i + 1, :], (PBS, LANES))
            out_ref[shards_ref[k], i] = jnp.take_along_axis(tile, where, axis=1)[:, :slots]


def place(shards, tiles, slots):
    vmem = pl.BlockSpec(memory_space=pltpu.VMEM)
    return pl.pallas_call(
        place_kernel,
        out_shape=jax.ShapeDtypeStruct((len(tiles), QB, PBS, slots), jnp.float32),
        in_specs=[pl.BlockSpec(memory_space=pltpu.SMEM)] + [vmem] * len(tiles),
        out_specs=vmem,
    )(shards, *tiles)


def swap(x, k, shards):
    return lax.ppermute(x, "psg", [(j, j ^ k) for j in range(shards)]) if k else x


def per_device(queries, passages, lengths, candidates):
    shards = lax.axis_size("psg")
    rows = passages.shape[0] // PBS
    slots = rows * KB // shards
    cand = candidates.reshape(rows, KB)
    own = queries.reshape(QBD * QB * QT, DIM)
    if shards <= 8:
        partners = lax.axis_index("psg") ^ jnp.arange(shards, dtype=jnp.int32)
        blocks = [swap(own, k, shards) for k in range(shards)]
        tiles = score(partners, cand, lengths, passages, blocks)
        received = [swap(tiles[k], k, shards) for k in range(shards)]
        placed = place(partners, received, slots)
    else:
        gathered = lax.all_gather(own, "psg", axis=0)
        some = 8

        def score_some(items):
            first, some_blocks = items
            owners = first + jnp.arange(some, dtype=jnp.int32)
            return jnp.stack(score(owners, cand, lengths, passages, [some_blocks[k] for k in range(some)]))

        firsts = jnp.arange(0, shards, some, dtype=jnp.int32)
        tiles = lax.map(score_some, (firsts, gathered.reshape(shards // some, some, *own.shape)))
        received = lax.all_to_all(
            tiles.reshape(shards, QB + 1, LANES), "psg", split_axis=0, concat_axis=0, tiled=True
        )
        placed = jnp.concatenate([
            place(jnp.arange(some, dtype=jnp.int32), [received[j + k] for k in range(some)], slots)
            for j in range(0, shards, some)
        ])
    return placed.transpose(0, 3, 1, 2)[None]


def solution(mesh):
    return jax.shard_map(
        per_device,
        mesh=mesh,
        in_specs=(
            P(("grp", "psg", "qry"), None, None),
            P(("grp", "psg"), None, None),
            P(("grp", "psg")),
            P("qry", ("grp", "psg"), None),
        ),
        out_specs=P(("grp", "psg", "qry"), None, None, None, None),
        check_vma=False,
    )
```

```python
import functools

import jax
import jax.numpy as jnp
from jax import lax
from jax.experimental import pallas as pl
from jax.experimental.pallas import tpu as pltpu
from jax.sharding import PartitionSpec as P

DIM = 128
QT = 32
PT = 64
QB = 2
QBD = 4
PBS = 16
KB = 32
LANES = 128
GROUP = 8


def prepare_kernel(cand_ref, len_ref, p_hbm, slots_ref, picks_ref, clean_ref, raw_ref, sems):
    rows = cand_ref.shape[0]
    shards = slots_ref.shape[0]
    count = p_hbm.shape[0]

    def fetch(g):
        part = pl.ds(g * GROUP, GROUP)
        return pltpu.make_async_copy(p_hbm.at[part], raw_ref.at[part], sems.at[g])

    for g in range(count // GROUP):
        fetch(g).start()

    cand = cand_ref[...]
    owner = cand // QBD
    block = cand - owner * QBD
    lane = lax.broadcasted_iota(jnp.int32, (rows, LANES), 1).astype(jnp.float32)
    sub = lax.broadcasted_iota(jnp.int32, (rows, LANES), 0)
    for o in range(shards):
        mine = owner == o
        named_here = jnp.sum(jnp.where(mine, 1.0, 0.0), axis=1, keepdims=True)
        upto = jnp.broadcast_to(named_here, (rows, LANES))
        step = 1
        while step < rows:
            upto = upto + jnp.where(sub >= step, pltpu.roll(upto, step, 0), 0.0)
            step *= 2
        slots_ref[o:o + 1, :] = jnp.sum(jnp.where(upto <= lane, 1.0, 0.0), axis=0, keepdims=True)
        named = jnp.max(jnp.where(mine, block, 0), axis=1, keepdims=True)
        picks_ref[o:o + 1, :] = jnp.broadcast_to(jnp.max(named, axis=0, keepdims=True), (1, LANES))

    u = lax.broadcasted_iota(jnp.int32, (PT, LANES), 0)
    for g in range(count // GROUP):
        fetch(g).wait()
        for p in range(g * GROUP, (g + 1) * GROUP):
            tokens = raw_ref[p].astype(jnp.float32)
            clean_ref[p] = jnp.where(u < len_ref[p], tokens, tokens[0:1]).astype(jnp.bfloat16)


def prepare(shards, candidates, lengths, passages):
    smem = pl.BlockSpec(memory_space=pltpu.SMEM)
    vmem = pl.BlockSpec(memory_space=pltpu.VMEM)
    return pl.pallas_call(
        prepare_kernel,
        out_shape=[
            jax.ShapeDtypeStruct((shards, LANES), jnp.float32),
            jax.ShapeDtypeStruct((shards, LANES), jnp.int32),
            jax.ShapeDtypeStruct(passages.shape, passages.dtype),
        ],
        in_specs=[vmem, smem, pl.BlockSpec(memory_space=pl.ANY)],
        out_specs=[vmem] * 3,
        scratch_shapes=[
            pltpu.VMEM(passages.shape, passages.dtype),
            pltpu.SemaphoreType.DMA((passages.shape[0] // GROUP,)),
        ],
        compiler_params=pltpu.CompilerParams(vmem_limit_bytes=24 * 1024 * 1024),
        cost_estimate=pl.CostEstimate(flops=passages.size, bytes_accessed=2 * passages.size, transcendentals=0),
    )(candidates, lengths, passages)


def score_kernel(paired, slots_ref, picks_ref, p_ref, *refs):
    some = len(refs) - 3
    q_refs, (out_ref, sel_ref, max_ref) = refs[:some], refs[some:]
    count = p_ref.shape[0]
    tokens = QB * QT
    me = lax.axis_index("psg") if paired else 0

    for k in range(some):
        pick = jnp.max(picks_ref[pl.ds(me ^ k, 1), :])
        sel_ref[k * tokens:(k + 1) * tokens, :] = q_refs[k][pl.ds(pick * tokens, tokens), :]

    sel = sel_ref[...]
    for g in range(count // GROUP):
        left = p_ref[g * GROUP:(g + 1) * GROUP].reshape(GROUP * PT, DIM)
        dots = lax.dot_general(left, sel, (((1,), (1,)), ((), ())), preferred_element_type=jnp.float32)
        best = jnp.max(dots.reshape(GROUP, PT, some * tokens), axis=1)
        max_ref[g * GROUP:(g + 1) * GROUP, :] = best

    best = max_ref[...]
    high = best.astype(jnp.bfloat16)
    rest = best - high.astype(jnp.float32)
    mid = rest.astype(jnp.bfloat16)
    low = (rest - mid.astype(jnp.float32)).astype(jnp.bfloat16)
    query = lax.broadcasted_iota(jnp.int32, (some * QB, some * tokens), 0)
    token = lax.broadcasted_iota(jnp.int32, (some * QB, some * tokens), 1)
    ones = jnp.where(token // QT == query, 1.0, 0.0).astype(jnp.bfloat16)
    total = jnp.zeros((some * QB, count), jnp.float32)
    for part in (low, mid, high):
        total = total + lax.dot_general(ones, part, (((1,), (1,)), ((), ())), preferred_element_type=jnp.float32)
    total = total * (1.0 / QT)
    for k in range(some):
        out_ref[me ^ k, 0:QB, :] = total[k * QB:(k + 1) * QB]
        out_ref[k, QB:QB + 1, :] = slots_ref[k:k + 1, :]


def score(paired, slots, picks, passages, blocks):
    some = len(blocks)
    count = passages.shape[0]
    vmem = pl.BlockSpec(memory_space=pltpu.VMEM)
    return pl.pallas_call(
        functools.partial(score_kernel, paired),
        out_shape=jax.ShapeDtypeStruct((some, QB + 1, LANES), jnp.float32),
        in_specs=[vmem] * (3 + some),
        out_specs=vmem,
        scratch_shapes=[
            pltpu.VMEM((some * QB * QT, DIM), jnp.bfloat16),
            pltpu.VMEM((count, some * QB * QT), jnp.float32),
        ],
        compiler_params=pltpu.CompilerParams(vmem_limit_bytes=40 * 1024 * 1024),
    )(slots, picks, passages, *blocks)


def place_kernel(in_ref, out_ref):
    slots = out_ref.shape[-1]
    m = lax.broadcasted_iota(jnp.int32, (PBS, LANES), 0)
    for j in range(in_ref.shape[0]):
        row = in_ref[j, QB:QB + 1, :].astype(jnp.int32)
        where = jnp.minimum(row * PBS, LANES - PBS) + m
        for i in range(QB):
            tile = jnp.broadcast_to(in_ref[j, i:i + 1, :], (PBS, LANES))
            out_ref[j, i] = jnp.take_along_axis(tile, where, axis=1)[:, :slots]


def place(tiles, slots):
    vmem = pl.BlockSpec(memory_space=pltpu.VMEM)
    return pl.pallas_call(
        place_kernel,
        out_shape=jax.ShapeDtypeStruct((tiles.shape[0], QB, PBS, slots), jnp.float32),
        in_specs=[vmem],
        out_specs=vmem,
    )(tiles)


def relay(own, shards):
    blocks = {0: own}

    def swap(source, k):
        blocks[source ^ k] = lax.ppermute(blocks[source], "psg", [(j, j ^ k) for j in range(shards)])

    for source, k in ((0, 4), (0, 2), (0, 1), (4, 2), (1, 2), (4, 1), (6, 1)):
        if source ^ k < shards:
            swap(source, k)
    return [blocks[k] for k in range(shards)]


def per_device(queries, passages, lengths, candidates):
    shards = lax.axis_size("psg")
    rows = passages.shape[0] // PBS
    slots = rows * KB // shards
    own = queries.reshape(QBD * QB * QT, DIM)
    slot_rows, picks, clean = prepare(shards, candidates.reshape(rows, KB), lengths, passages)
    if shards in (2, 4, 8):
        tiles = score(True, slot_rows, picks, clean, relay(own, shards))
    else:
        gathered = lax.all_gather(own, "psg", axis=0)
        some = 8

        def score_some(items):
            some_rows, some_picks, some_blocks = items
            return score(False, some_rows, some_picks, clean, [some_blocks[k] for k in range(some)])

        parts = shards // some
        tiles = lax.map(score_some, (
            slot_rows.reshape(parts, some, LANES),
            picks.reshape(parts, some, LANES),
            gathered.reshape(parts, some, *own.shape),
        )).reshape(shards, QB + 1, LANES)
    received = lax.all_to_all(tiles, "psg", split_axis=0, concat_axis=0, tiled=True)
    return place(received, slots).transpose(0, 3, 1, 2)[None]


def solution(mesh):
    return jax.shard_map(
        per_device,
        mesh=mesh,
        in_specs=(
            P(("grp", "psg", "qry"), None, None),
            P(("grp", "psg"), None, None),
            P(("grp", "psg")),
            P("qry", ("grp", "psg"), None),
        ),
        out_specs=P(("grp", "psg", "qry"), None, None, None, None),
        check_vma=False,
    )
```

```python
import functools

import jax
import jax.numpy as jnp
from jax import lax
from jax.experimental import pallas as pl
from jax.experimental.pallas import tpu as pltpu
from jax.sharding import PartitionSpec as P

DIM = 128
QT = 32
PT = 64
QB = 2
QBD = 4
PBS = 16
KB = 32
LANES = 128
GROUP = 8


def prepare_kernel(cand_hbm, len_hbm, p_hbm, slots_ref, picks_ref, clean_ref, cand_ref, len_ref, raw_ref, sems):
    rows = cand_ref.shape[0]
    shards = slots_ref.shape[0]
    groups = p_hbm.shape[0] // GROUP

    def fetch(g):
        part = pl.ds(g * GROUP, GROUP)
        return pltpu.make_async_copy(p_hbm.at[part], raw_ref.at[part], sems.at[g])

    fetch_cand = pltpu.make_async_copy(cand_hbm, cand_ref, sems.at[groups])
    fetch_len = pltpu.make_async_copy(len_hbm, len_ref, sems.at[groups + 1])
    fetch_cand.start()
    fetch_len.start()
    for g in range(groups):
        fetch(g).start()

    fetch_cand.wait()
    cand = cand_ref[...]
    owner = cand // QBD
    block = cand - owner * QBD
    lane = lax.broadcasted_iota(jnp.int32, (rows, LANES), 1).astype(jnp.float32)
    sub = lax.broadcasted_iota(jnp.int32, (rows, LANES), 0)
    for o in range(shards):
        mine = owner == o
        named_here = jnp.sum(jnp.where(mine, 1.0, 0.0), axis=1, keepdims=True)
        upto = jnp.broadcast_to(named_here, (rows, LANES))
        step = 1
        while step < rows:
            upto = upto + jnp.where(sub >= step, pltpu.roll(upto, step, 0), 0.0)
            step *= 2
        slots_ref[o:o + 1, :] = jnp.sum(jnp.where(upto <= lane, 1.0, 0.0), axis=0, keepdims=True)
        named = jnp.max(jnp.where(mine, block, 0), axis=1, keepdims=True)
        picks_ref[o:o + 1, :] = jnp.broadcast_to(jnp.max(named, axis=0, keepdims=True), (1, LANES))

    fetch_len.wait()
    u = lax.broadcasted_iota(jnp.int32, (PT, LANES), 0)

    @pl.loop(0, groups)
    def _(g):
        fetch(g).wait()
        for i in range(GROUP):
            p = g * GROUP + i
            tokens = raw_ref[p].astype(jnp.float32)
            clean_ref[p] = jnp.where(u < len_ref[p], tokens, tokens[0:1]).astype(jnp.bfloat16)


def prepare(shards, candidates, lengths, passages):
    hbm = pl.BlockSpec(memory_space=pltpu.HBM)
    vmem = pl.BlockSpec(memory_space=pltpu.VMEM)
    return pl.pallas_call(
        prepare_kernel,
        out_shape=[
            jax.ShapeDtypeStruct((shards, LANES), jnp.float32),
            jax.ShapeDtypeStruct((shards, LANES), jnp.int32),
            jax.ShapeDtypeStruct(passages.shape, passages.dtype),
        ],
        in_specs=[hbm] * 3,
        out_specs=[vmem] * 3,
        scratch_shapes=[
            pltpu.VMEM(candidates.shape, candidates.dtype),
            pltpu.SMEM(lengths.shape, lengths.dtype),
            pltpu.VMEM(passages.shape, passages.dtype),
            pltpu.SemaphoreType.DMA((passages.shape[0] // GROUP + 2,)),
        ],
        compiler_params=pltpu.CompilerParams(vmem_limit_bytes=24 * 1024 * 1024),
        cost_estimate=pl.CostEstimate(flops=passages.size, bytes_accessed=2 * passages.size, transcendentals=0),
    )(candidates, lengths, passages)


def score_kernel(partners, shards, slots_ref, picks_ref, p_ref, *refs):
    some = len(partners)
    q_refs, (out_ref, sel_ref, max_ref) = refs[:some], refs[-3:]
    earlier_refs = refs[some:-3]
    count = p_ref.shape[0]
    tokens = QB * QT
    me = lax.axis_index("psg") if some < shards or len(earlier_refs) else 0

    for n, k in enumerate(partners):
        pick = jnp.max(picks_ref[pl.ds(me ^ k, 1), :])
        sel_ref[n * tokens:(n + 1) * tokens, :] = q_refs[n][pl.ds(pick * tokens, tokens), :]

    sel = sel_ref[...]
    for g in range(count // GROUP):
        left = p_ref[g * GROUP:(g + 1) * GROUP].reshape(GROUP * PT, DIM)
        dots = lax.dot_general(left, sel, (((1,), (1,)), ((), ())), preferred_element_type=jnp.float32)
        best = jnp.max(dots.reshape(GROUP, PT, some * tokens), axis=1)
        max_ref[g * GROUP:(g + 1) * GROUP, :] = best

    best = max_ref[...]
    high = best.astype(jnp.bfloat16)
    rest = best - high.astype(jnp.float32)
    mid = rest.astype(jnp.bfloat16)
    low = (rest - mid.astype(jnp.float32)).astype(jnp.bfloat16)
    query = lax.broadcasted_iota(jnp.int32, (some * QB, some * tokens), 0)
    token = lax.broadcasted_iota(jnp.int32, (some * QB, some * tokens), 1)
    ones = jnp.where(token // QT == query, 1.0, 0.0).astype(jnp.bfloat16)
    total = jnp.zeros((some * QB, count), jnp.float32)
    for part in (low, mid, high):
        total = total + lax.dot_general(ones, part, (((1,), (1,)), ((), ())), preferred_element_type=jnp.float32)
    total = total * (1.0 / QT)
    if earlier_refs:
        out_ref[...] = earlier_refs[0][...]
    for n, k in enumerate(partners):
        out_ref[me ^ k, 0:QB, :] = total[n * QB:(n + 1) * QB]
        out_ref[me ^ k, QB:QB + 1, :] = slots_ref[pl.ds(me ^ k, 1), :]


def score(partners, slots, picks, passages, blocks, *earlier):
    some = len(blocks)
    shards = slots.shape[0]
    count = passages.shape[0]
    vmem = pl.BlockSpec(memory_space=pltpu.VMEM)
    return pl.pallas_call(
        functools.partial(score_kernel, partners, shards),
        out_shape=jax.ShapeDtypeStruct((shards, QB + 1, LANES), jnp.float32),
        in_specs=[vmem] * (3 + some + len(earlier)),
        out_specs=vmem,
        scratch_shapes=[
            pltpu.VMEM((some * QB * QT, DIM), jnp.bfloat16),
            pltpu.VMEM((count, some * QB * QT), jnp.float32),
        ],
        compiler_params=pltpu.CompilerParams(vmem_limit_bytes=32 * 1024 * 1024),
        cost_estimate=pl.CostEstimate(
            flops=2 * passages.size * some * QB * QT, bytes_accessed=2 * passages.size, transcendentals=0
        ),
    )(slots, picks, passages, *blocks, *earlier)


def place_kernel(in_ref, out_ref):
    slots = out_ref.shape[-1]
    m = lax.broadcasted_iota(jnp.int32, (PBS, LANES), 0)
    for j in range(in_ref.shape[0]):
        row = in_ref[j, QB:QB + 1, :].astype(jnp.int32)
        where = jnp.minimum(row * PBS, LANES - PBS) + m
        for i in range(QB):
            tile = jnp.broadcast_to(in_ref[j, i:i + 1, :], (PBS, LANES))
            out_ref[j, i] = jnp.take_along_axis(tile, where, axis=1)[:, :slots]


def place(tiles, slots):
    vmem = pl.BlockSpec(memory_space=pltpu.VMEM)
    return pl.pallas_call(
        place_kernel,
        out_shape=jax.ShapeDtypeStruct((tiles.shape[0], QB, PBS, slots), jnp.float32),
        in_specs=[vmem],
        out_specs=vmem,
    )(tiles)


def relay_and_score(own, shards, candidates, lengths, passages):
    def swap(x, k):
        return lax.ppermute(x, "psg", [(j, j ^ k) for j in range(shards)])

    queries = {0: own, 4: swap(own, 4), 1: swap(own, 1), 2: swap(own, 2)}
    slots, picks, clean = prepare(shards, candidates, lengths, passages)
    queries[4], queries[1], clean = lax.optimization_barrier((queries[4], queries[1], clean))
    queries[6] = swap(queries[4], 2)
    queries[5] = swap(queries[4], 1)
    queries[3] = swap(queries[1], 2)
    first, second = (0, 1, 2, 4), (3, 5, 6, 7)
    tiles = score(first, slots, picks, clean, [queries[k] for k in first])
    queries[6], tiles = lax.optimization_barrier((queries[6], tiles))
    queries[7] = swap(queries[6], 1)
    return score(second, slots, picks, clean, [queries[k] for k in second], tiles)


def per_device(queries, passages, lengths, candidates):
    shards = lax.axis_size("psg")
    rows = passages.shape[0] // PBS
    slots = rows * KB // shards
    own = queries.reshape(QBD * QB * QT, DIM)
    candidates = candidates.reshape(rows, KB)
    if shards == 8:
        tiles = relay_and_score(own, shards, candidates, lengths, passages)
    else:
        slot_rows, picks, clean = prepare(shards, candidates, lengths, passages)
        gathered = lax.all_gather(own, "psg", axis=0)
        some = 8

        def score_some(items):
            some_rows, some_picks, some_blocks = items
            return score(range(some), some_rows, some_picks, clean, [some_blocks[k] for k in range(some)])

        parts = shards // some
        tiles = lax.map(score_some, (
            slot_rows.reshape(parts, some, LANES),
            picks.reshape(parts, some, LANES),
            gathered.reshape(parts, some, *own.shape),
        )).reshape(shards, QB + 1, LANES)
    received = lax.all_to_all(tiles, "psg", split_axis=0, concat_axis=0, tiled=True)
    return place(received, slots).transpose(0, 3, 1, 2)[None]


def solution(mesh):
    return jax.shard_map(
        per_device,
        mesh=mesh,
        in_specs=(
            P(("grp", "psg", "qry"), None, None),
            P(("grp", "psg"), None, None),
            P(("grp", "psg")),
            P("qry", ("grp", "psg"), None),
        ),
        out_specs=P(("grp", "psg", "qry"), None, None, None, None),
        check_vma=False,
    )
```

```python
import functools

import jax
import jax.numpy as jnp
from jax import lax
from jax.experimental import pallas as pl
from jax.experimental.pallas import tpu as pltpu
from jax.sharding import PartitionSpec as P

DIM = 128
QT = 32
PT = 64
QB = 2
QBD = 4
PBS = 16
KB = 32
LANES = 128
GROUP = 8


def prepare_kernel(cand_hbm, len_hbm, p_hbm, slots_ref, picks_ref, clean_ref, cand_ref, len_ref, raw_ref, sems):
    rows = cand_ref.shape[0]
    shards = slots_ref.shape[0]
    groups = p_hbm.shape[0] // GROUP

    def fetch(g):
        part = pl.ds(g * GROUP, GROUP)
        return pltpu.make_async_copy(p_hbm.at[part], raw_ref.at[part], sems.at[g])

    fetch_cand = pltpu.make_async_copy(cand_hbm, cand_ref, sems.at[groups])
    fetch_len = pltpu.make_async_copy(len_hbm, len_ref, sems.at[groups + 1])
    fetch_cand.start()
    fetch_len.start()
    for g in range(groups):
        fetch(g).start()

    fetch_cand.wait()
    cand = cand_ref[...]
    owner = cand // QBD
    block = cand - owner * QBD
    lane = lax.broadcasted_iota(jnp.int32, (rows, LANES), 1).astype(jnp.float32)
    sub = lax.broadcasted_iota(jnp.int32, (rows, LANES), 0)
    for o in range(shards):
        mine = owner == o
        named_here = jnp.sum(jnp.where(mine, 1.0, 0.0), axis=1, keepdims=True)
        upto = jnp.broadcast_to(named_here, (rows, LANES))
        step = 1
        while step < rows:
            upto = upto + jnp.where(sub >= step, pltpu.roll(upto, step, 0), 0.0)
            step *= 2
        slots_ref[o:o + 1, :] = jnp.sum(jnp.where(upto <= lane, 1.0, 0.0), axis=0, keepdims=True)
        named = jnp.max(jnp.where(mine, block, 0), axis=1, keepdims=True)
        picks_ref[o:o + 1, :] = jnp.broadcast_to(jnp.max(named, axis=0, keepdims=True), (1, LANES))

    fetch_len.wait()
    u = lax.broadcasted_iota(jnp.int32, (PT, LANES), 0)

    @pl.loop(0, groups)
    def _(g):
        fetch(g).wait()
        for i in range(GROUP):
            p = g * GROUP + i
            tokens = raw_ref[p].astype(jnp.float32)
            clean_ref[p] = jnp.where(u < len_ref[p], tokens, tokens[0:1]).astype(jnp.bfloat16)


def prepare(shards, candidates, lengths, passages):
    hbm = pl.BlockSpec(memory_space=pltpu.HBM)
    vmem = pl.BlockSpec(memory_space=pltpu.VMEM)
    operands = [pltpu.with_memory_space_constraint(x, pltpu.HBM) for x in (candidates, lengths, passages)]
    return pl.pallas_call(
        prepare_kernel,
        out_shape=[
            jax.ShapeDtypeStruct((shards, LANES), jnp.float32),
            jax.ShapeDtypeStruct((shards, LANES), jnp.int32),
            jax.ShapeDtypeStruct(passages.shape, passages.dtype),
        ],
        in_specs=[hbm] * 3,
        out_specs=[vmem] * 3,
        scratch_shapes=[
            pltpu.VMEM(candidates.shape, candidates.dtype),
            pltpu.SMEM(lengths.shape, lengths.dtype),
            pltpu.VMEM(passages.shape, passages.dtype),
            pltpu.SemaphoreType.DMA((passages.shape[0] // GROUP + 2,)),
        ],
        compiler_params=pltpu.CompilerParams(vmem_limit_bytes=24 * 1024 * 1024),
        cost_estimate=pl.CostEstimate(flops=passages.size, bytes_accessed=2 * passages.size, transcendentals=0),
    )(*operands)


def score_blocks(partners, me, slots_ref, picks_ref, p_ref, q_refs, sel_ref, max_ref):
    some = len(partners)
    count = p_ref.shape[0]
    tokens = QB * QT
    for n, k in enumerate(partners):
        pick = jnp.max(picks_ref[pl.ds(me ^ k, 1), :])
        sel_ref[n * tokens:(n + 1) * tokens, :] = q_refs[n][pl.ds(pick * tokens, tokens), :]

    sel = sel_ref[...]
    for g in range(count // GROUP):
        left = p_ref[g * GROUP:(g + 1) * GROUP].reshape(GROUP * PT, DIM)
        dots = lax.dot_general(left, sel, (((1,), (1,)), ((), ())), preferred_element_type=jnp.float32)
        best = jnp.max(dots.reshape(GROUP, PT, some * tokens), axis=1)
        max_ref[g * GROUP:(g + 1) * GROUP, :] = best

    best = max_ref[...]
    high = best.astype(jnp.bfloat16)
    rest = best - high.astype(jnp.float32)
    mid = rest.astype(jnp.bfloat16)
    low = (rest - mid.astype(jnp.float32)).astype(jnp.bfloat16)
    query = lax.broadcasted_iota(jnp.int32, (some * QB, some * tokens), 0)
    token = lax.broadcasted_iota(jnp.int32, (some * QB, some * tokens), 1)
    ones = jnp.where(token // QT == query, 1.0, 0.0).astype(jnp.bfloat16)
    total = jnp.zeros((some * QB, count), jnp.float32)
    for part in (low, mid, high):
        total = total + lax.dot_general(ones, part, (((1,), (1,)), ((), ())), preferred_element_type=jnp.float32)
    total = total * (1.0 / QT)
    return [
        jnp.concatenate([total[n * QB:(n + 1) * QB], slots_ref[pl.ds(me ^ k, 1), :]]) for n, k in enumerate(partners)
    ]


def score_kernel(partners, paired, slots_ref, picks_ref, p_ref, *refs):
    q_refs, (out_ref, sel_ref, max_ref) = refs[:-3], refs[-3:]
    me = lax.axis_index("psg") if paired else 0
    tiles = score_blocks(partners, me, slots_ref, picks_ref, p_ref, q_refs, sel_ref, max_ref)
    for n, tile in enumerate(tiles):
        out_ref[n] = tile


def join_kernel(partners, slots_ref, picks_ref, p_ref, *refs):
    some = len(partners)
    q_refs, theirs_ref, out_refs, (sel_ref, max_ref) = refs[:some], refs[some], refs[some + 1:-2], refs[-2:]
    me = lax.axis_index("psg")
    tiles = score_blocks(partners, me, slots_ref, picks_ref, p_ref, q_refs, sel_ref, max_ref)
    for n, tile in enumerate(tiles):
        out_refs[n][0] = tile
        out_refs[n][1] = theirs_ref[n]


def score(kernel, out_shape, slots, picks, passages, blocks, *more):
    some = len(blocks)
    count = passages.shape[0]
    vmem = pl.BlockSpec(memory_space=pltpu.VMEM)
    return pl.pallas_call(
        kernel,
        out_shape=out_shape,
        in_specs=[vmem] * (3 + some + len(more)),
        out_specs=jax.tree.map(lambda _: vmem, out_shape),
        scratch_shapes=[
            pltpu.VMEM((some * QB * QT, DIM), jnp.bfloat16),
            pltpu.VMEM((count, some * QB * QT), jnp.float32),
        ],
        compiler_params=pltpu.CompilerParams(vmem_limit_bytes=32 * 1024 * 1024),
        cost_estimate=pl.CostEstimate(
            flops=2 * passages.size * some * QB * QT, bytes_accessed=2 * passages.size, transcendentals=0
        ),
    )(slots, picks, passages, *blocks, *more)


def place_kernel(sources, in_refs, out_ref):
    slots = out_ref.shape[-1]
    m = lax.broadcasted_iota(jnp.int32, (PBS, LANES), 0)
    for j, tile_ref in zip(sources, in_refs):
        row = tile_ref[QB:QB + 1, :].astype(jnp.int32)
        where = jnp.minimum(row * PBS, LANES - PBS) + m
        for i in range(QB):
            tile = jnp.broadcast_to(tile_ref[i:i + 1, :], (PBS, LANES))
            out_ref[j, i] = jnp.take_along_axis(tile, where, axis=1)[:, :slots]


def place_all_kernel(in_ref, out_ref):
    shards = in_ref.shape[0]
    place_kernel(range(shards), [in_ref.at[j] for j in range(shards)], out_ref)


def place_pairs_kernel(partners, *refs):
    me = lax.axis_index("psg")
    in_refs = [ref.at[n] for ref in refs[:-1] for n in range(2)]
    place_kernel([me ^ k ^ n for k in partners for n in range(2)], in_refs, refs[-1])


def place(kernel, shards, slots, *tiles):
    vmem = pl.BlockSpec(memory_space=pltpu.VMEM)
    return pl.pallas_call(
        kernel,
        out_shape=jax.ShapeDtypeStruct((shards, QB, PBS, slots), jnp.float32),
        in_specs=[vmem] * len(tiles),
        out_specs=vmem,
    )(*tiles)


def by_partners(own, shards, slots, candidates, lengths, passages):
    def swap(x, k):
        return lax.ppermute(x, "psg", [(j, j ^ k) for j in range(shards)])

    near = list(range(0, shards, 2))
    far = [k + 1 for k in near]
    tile = (QB + 1, LANES)
    queries = {0: own} | {k: swap(own, k) for k in reversed(far)}
    rows, picks, clean = prepare(shards, candidates, lengths, passages)
    *arrived, clean = lax.optimization_barrier((*[queries[k] for k in far], clean))
    queries |= dict(zip(far, arrived))
    queries |= {k: swap(queries[k + 1], 1) for k in near[1:]}
    theirs = swap(
        score(
            functools.partial(score_kernel, far, True),
            jax.ShapeDtypeStruct((len(far), *tile), jnp.float32),
            rows, picks, clean, [queries[k] for k in far],
        ), 1,
    )
    pairs = score(
        functools.partial(join_kernel, near),
        [jax.ShapeDtypeStruct((2, *tile), jnp.float32)] * len(near),
        rows, picks, clean, [queries[k] for k in near], theirs,
    )
    pairs = [swap(pair, k) if k else pair for pair, k in zip(pairs, near)]
    return place(functools.partial(place_pairs_kernel, near), shards, slots, *pairs)


def by_collectives(own, shards, slots, candidates, lengths, passages):
    rows, picks, clean = prepare(shards, candidates, lengths, passages)
    gathered = lax.all_gather(own, "psg", axis=0)
    some = min(shards, 8)
    tile = (QB + 1, LANES)

    def score_some(items):
        some_rows, some_picks, some_blocks = items
        return score(
            functools.partial(score_kernel, range(some), False),
            jax.ShapeDtypeStruct((some, *tile), jnp.float32),
            some_rows, some_picks, clean, [some_blocks[k] for k in range(some)],
        )

    parts = shards // some
    tiles = lax.map(score_some, (
        rows.reshape(parts, some, LANES),
        picks.reshape(parts, some, LANES),
        gathered.reshape(parts, some, *own.shape),
    ))
    tiles = lax.all_to_all(tiles.reshape(shards, *tile), "psg", split_axis=0, concat_axis=0, tiled=True)
    return place(place_all_kernel, shards, slots, tiles)


def per_device(queries, passages, lengths, candidates):
    shards = lax.axis_size("psg")
    rows = passages.shape[0] // PBS
    form = by_partners if shards in (4, 8) else by_collectives
    placed = form(
        queries.reshape(QBD * QB * QT, DIM), shards, rows * KB // shards,
        candidates.reshape(rows, KB), lengths, passages,
    )
    return placed.transpose(0, 3, 1, 2)[None]


def solution(mesh):
    return jax.shard_map(
        per_device,
        mesh=mesh,
        in_specs=(
            P(("grp", "psg", "qry"), None, None),
            P(("grp", "psg"), None, None),
            P(("grp", "psg")),
            P("qry", ("grp", "psg"), None),
        ),
        out_specs=P(("grp", "psg", "qry"), None, None, None, None),
        check_vma=False,
    )
```

```python
import functools

import jax
import jax.numpy as jnp
from jax import lax
from jax.experimental import pallas as pl
from jax.experimental.pallas import tpu as pltpu
from jax.sharding import PartitionSpec as P

DIM = 128
QT = 32
PT = 64
QB = 2
QBD = 4
PBS = 16
KB = 32
LANES = 128
GROUP = 8


def prepare_kernel(*refs):
    several = (len(refs) - 8) // 2
    *cand_refs, len_hbm, p_hbm, slots_ref = refs[:several + 3]
    picks_refs = refs[several + 3:-5]
    clean_ref, len_ref, raw_ref, cand_ref, sems = refs[-5:]
    rows = cand_ref.shape[0]
    shards = slots_ref.shape[0]
    groups = p_hbm.shape[0] // GROUP

    def fetch(g):
        part = pl.ds(g * GROUP, GROUP)
        return pltpu.make_async_copy(p_hbm.at[part], raw_ref.at[part], sems.at[g])

    fetch_cand = pltpu.make_async_copy(cand_refs[0], cand_ref, sems.at[groups])
    fetch_len = pltpu.make_async_copy(len_hbm, len_ref, sems.at[groups + 1])
    fetch_cand.start()
    fetch_len.start()
    for g in range(groups):
        fetch(g).start()

    fetch_cand.wait()
    lane = lax.broadcasted_iota(jnp.int32, (rows, LANES), 1).astype(jnp.float32)
    sub = lax.broadcasted_iota(jnp.int32, (rows, LANES), 0)
    for n, picks_ref in enumerate(picks_refs):
        cand = (cand_refs[n] if n else cand_ref)[...]
        owner = cand // QBD
        block = cand - owner * QBD
        for o in range(shards):
            mine = owner == o
            named = jnp.max(jnp.where(mine, block, 0), axis=1, keepdims=True)
            picks_ref[o:o + 1, :] = jnp.broadcast_to(jnp.max(named, axis=0, keepdims=True), (1, LANES))
            if n:
                continue
            named_here = jnp.sum(jnp.where(mine, 1.0, 0.0), axis=1, keepdims=True)
            upto = jnp.broadcast_to(named_here, (rows, LANES))
            step = 1
            while step < rows:
                upto = upto + jnp.where(sub >= step, pltpu.roll(upto, step, 0), 0.0)
                step *= 2
            slots_ref[o:o + 1, :] = jnp.sum(jnp.where(upto <= lane, 1.0, 0.0), axis=0, keepdims=True)

    fetch_len.wait()
    u = lax.broadcasted_iota(jnp.int32, (PT, LANES), 0)

    @pl.loop(0, groups)
    def _(g):
        fetch(g).wait()
        for i in range(GROUP):
            p = g * GROUP + i
            tokens = raw_ref[p].astype(jnp.float32)
            clean_ref[p] = jnp.where(u < len_ref[p], tokens, tokens[0:1]).astype(jnp.bfloat16)


def prepare(shards, lengths, passages, *candidates):
    hbm = pl.BlockSpec(memory_space=pltpu.HBM)
    vmem = pl.BlockSpec(memory_space=pltpu.VMEM)
    kept = [pltpu.with_memory_space_constraint(x, pltpu.HBM) for x in (candidates[0], lengths, passages)]
    more = candidates[1:]
    return pl.pallas_call(
        prepare_kernel,
        out_shape=[
            jax.ShapeDtypeStruct((shards, LANES), jnp.float32),
            *[jax.ShapeDtypeStruct((shards, LANES), jnp.int32) for _ in candidates],
            jax.ShapeDtypeStruct(passages.shape, passages.dtype),
        ],
        in_specs=[hbm] + [vmem] * len(more) + [hbm] * 2,
        out_specs=[vmem] * (2 + len(candidates)),
        scratch_shapes=[
            pltpu.SMEM(lengths.shape, lengths.dtype),
            pltpu.VMEM(passages.shape, passages.dtype),
            pltpu.VMEM(candidates[0].shape, candidates[0].dtype),
            pltpu.SemaphoreType.DMA((passages.shape[0] // GROUP + 2,)),
        ],
        compiler_params=pltpu.CompilerParams(vmem_limit_bytes=24 * 1024 * 1024),
        cost_estimate=pl.CostEstimate(flops=passages.size, bytes_accessed=2 * passages.size, transcendentals=0),
    )(kept[0], *more, *kept[1:])


def picked(picks_ref, owner, q_ref):
    pick = jnp.max(picks_ref[pl.ds(owner, 1), :])
    return q_ref[pl.ds(pick * QB * QT, QB * QT), :]


def pack_kernel(partners, picks_ref, *refs):
    q_refs, out_ref = refs[:-1], refs[-1]
    me = lax.axis_index("psg")
    for n, k in enumerate(partners):
        out_ref[n * QB * QT:(n + 1) * QB * QT, :] = picked(picks_ref, me ^ k, q_refs[n])


def pack(partners, picks, blocks):
    vmem = pl.BlockSpec(memory_space=pltpu.VMEM)
    return pl.pallas_call(
        functools.partial(pack_kernel, partners),
        out_shape=jax.ShapeDtypeStruct((len(partners) * QB * QT, DIM), blocks[0].dtype),
        in_specs=[vmem] * (1 + len(blocks)),
        out_specs=vmem,
        compiler_params=pltpu.CompilerParams(vmem_limit_bytes=4 * 1024 * 1024),
    )(picks, *blocks)


def score_picked(sel_ref, p_ref, max_ref):
    count = p_ref.shape[0]
    sel = sel_ref[...]
    tokens = sel.shape[0]
    for g in range(count // GROUP):
        left = p_ref[g * GROUP:(g + 1) * GROUP].reshape(GROUP * PT, DIM)
        dots = lax.dot_general(left, sel, (((1,), (1,)), ((), ())), preferred_element_type=jnp.float32)
        best = jnp.max(dots.reshape(GROUP, PT, tokens), axis=1)
        max_ref[g * GROUP:(g + 1) * GROUP, :] = best

    best = max_ref[...]
    high = best.astype(jnp.bfloat16)
    rest = best - high.astype(jnp.float32)
    mid = rest.astype(jnp.bfloat16)
    low = (rest - mid.astype(jnp.float32)).astype(jnp.bfloat16)
    query = lax.broadcasted_iota(jnp.int32, (tokens // QT, tokens), 0)
    token = lax.broadcasted_iota(jnp.int32, (tokens // QT, tokens), 1)
    ones = jnp.where(token // QT == query, 1.0, 0.0).astype(jnp.bfloat16)
    total = jnp.zeros((tokens // QT, count), jnp.float32)
    for part in (low, mid, high):
        total = total + lax.dot_general(ones, part, (((1,), (1,)), ((), ())), preferred_element_type=jnp.float32)
    return total * (1.0 / QT)


def score_kernel(partners, slots_ref, picks_ref, p_ref, *refs):
    q_refs, (out_ref, sel_ref, max_ref) = refs[:-3], refs[-3:]
    me = lax.axis_index("psg")
    for n, k in enumerate(partners):
        sel_ref[n * QB * QT:(n + 1) * QB * QT, :] = picked(picks_ref, me ^ k, q_refs[n])
    total = score_picked(sel_ref, p_ref, max_ref)
    for n, k in enumerate(partners):
        out_ref[n, 0:QB, :] = total[n * QB:(n + 1) * QB]
        out_ref[n, QB:QB + 1, :] = slots_ref[pl.ds(me ^ k, 1), :]


def join_kernel(partners, slots_ref, p_ref, sel_ref, earlier_ref, out_ref, max_ref):
    me = lax.axis_index("psg")
    total = score_picked(sel_ref, p_ref, max_ref)
    for n, k in enumerate(partners):
        out_ref[me ^ k, 0:QB, :] = total[n * QB:(n + 1) * QB]
        out_ref[me ^ k, QB:QB + 1, :] = slots_ref[pl.ds(me ^ k, 1), :]
        out_ref[me ^ k ^ 1] = earlier_ref[n]


def all_kernel(slots_ref, picks_ref, p_ref, q_ref, out_ref, sel_ref, max_ref):
    some = q_ref.shape[0]
    for n in range(some):
        sel_ref[n * QB * QT:(n + 1) * QB * QT, :] = picked(picks_ref, n, q_ref.at[n])
    total = score_picked(sel_ref, p_ref, max_ref)
    for n in range(some):
        out_ref[n, 0:QB, :] = total[n * QB:(n + 1) * QB]
        out_ref[n, QB:QB + 1, :] = slots_ref[n:n + 1, :]


def score(kernel, tiles, some, selects, passages, *more):
    count = passages.shape[0]
    vmem = pl.BlockSpec(memory_space=pltpu.VMEM)
    return pl.pallas_call(
        kernel,
        out_shape=jax.ShapeDtypeStruct((tiles, QB + 1, LANES), jnp.float32),
        in_specs=[vmem] * len(more),
        out_specs=vmem,
        scratch_shapes=[pltpu.VMEM((some * QB * QT, DIM), jnp.bfloat16)] * selects + [
            pltpu.VMEM((count, some * QB * QT), jnp.float32),
        ],
        compiler_params=pltpu.CompilerParams(vmem_limit_bytes=32 * 1024 * 1024),
        cost_estimate=pl.CostEstimate(
            flops=2 * passages.size * some * QB * QT, bytes_accessed=2 * passages.size, transcendentals=0
        ),
    )(*more)


def place_kernel(in_ref, out_ref):
    slots = out_ref.shape[-1]
    m = lax.broadcasted_iota(jnp.int32, (PBS, LANES), 0)
    for j in range(in_ref.shape[0]):
        row = in_ref[j, QB:QB + 1, :].astype(jnp.int32)
        where = jnp.minimum(row * PBS, LANES - PBS) + m
        for i in range(QB):
            tile = jnp.broadcast_to(in_ref[j, i:i + 1, :], (PBS, LANES))
            out_ref[j, i] = jnp.take_along_axis(tile, where, axis=1)[:, :slots]


def place(tiles, slots):
    vmem = pl.BlockSpec(memory_space=pltpu.VMEM)
    shards = tiles.shape[0]
    return pl.pallas_call(
        place_kernel,
        out_shape=jax.ShapeDtypeStruct((shards, QB, PBS, slots), jnp.float32),
        in_specs=[vmem],
        out_specs=vmem,
        compiler_params=pltpu.CompilerParams(vmem_limit_bytes=8 * 1024 * 1024),
    )(tiles)


def by_partners(own, shards, candidates, lengths, passages):
    def swap(x, k):
        return lax.ppermute(x, "psg", [(j, j ^ k) for j in range(shards)])

    near = list(range(0, shards, 2))
    theirs = swap(candidates, 1)
    queries = {0: own} | {k: swap(own, k) for k in reversed(near[1:])}
    slots, picks, their_picks, clean = prepare(shards, lengths, passages, candidates, theirs)
    *arrived, clean = lax.optimization_barrier((*[queries[k] for k in near[1:]], clean))
    blocks = [own, *arrived]
    far = swap(pack(near, their_picks, blocks), 1)
    tiles = score(
        functools.partial(score_kernel, near), len(near), len(near), 1, clean, slots, picks, clean, *blocks
    )
    far, tiles = lax.optimization_barrier((far, tiles))
    return score(
        functools.partial(join_kernel, [k + 1 for k in near]), shards, len(near), 0, clean, slots, clean, far, tiles
    )


def by_gather(own, shards, candidates, lengths, passages):
    slots, picks, clean = prepare(shards, lengths, passages, candidates)
    gathered = lax.all_gather(own, "psg", axis=0)
    some = min(shards, 8)

    def score_some(items):
        return score(all_kernel, some, some, 1, clean, items[0], items[1], clean, items[2])

    parts = [x.reshape(shards // some, some, *x.shape[1:]) for x in (slots, picks, gathered)]
    return lax.map(score_some, parts).reshape(shards, QB + 1, LANES)


def per_device(queries, passages, lengths, candidates):
    shards = lax.axis_size("psg")
    rows = passages.shape[0] // PBS
    form = by_partners if shards in (4, 8) else by_gather
    tiles = form(
        queries.reshape(QBD * QB * QT, DIM), shards, candidates.reshape(rows, KB), lengths, passages
    )
    tiles = lax.all_to_all(tiles, "psg", split_axis=0, concat_axis=0, tiled=True)
    return place(tiles, rows * KB // shards).transpose(0, 3, 1, 2)[None]


def solution(mesh):
    return jax.shard_map(
        per_device,
        mesh=mesh,
        in_specs=(
            P(("grp", "psg", "qry"), None, None),
            P(("grp", "psg"), None, None),
            P(("grp", "psg")),
            P("qry", ("grp", "psg"), None),
        ),
        out_specs=P(("grp", "psg", "qry"), None, None, None, None),
        check_vma=False,
    )
```

```python
import functools

import jax
import jax.numpy as jnp
from jax import lax
from jax.experimental import pallas as pl
from jax.experimental.pallas import tpu as pltpu
from jax.sharding import PartitionSpec as P

DIM = 128
QT = 32
PT = 64
QB = 2
QBD = 4
PBS = 16
KB = 32
LANES = 128
GROUP = 8


def prepare_kernel(
    cand_hbm, len_hbm, p_hbm, slots_ref, picks_ref, clean_ref, cand_ref, len_ref, raw_ref, sems
):
    rows = cand_ref.shape[0]
    shards = slots_ref.shape[0]
    groups = p_hbm.shape[0] // GROUP

    def fetch(g):
        part = pl.ds(g * GROUP, GROUP)
        return pltpu.make_async_copy(p_hbm.at[part], raw_ref.at[part], sems.at[g])

    fetch_cand = pltpu.make_async_copy(cand_hbm, cand_ref, sems.at[groups])
    fetch_len = pltpu.make_async_copy(len_hbm, len_ref, sems.at[groups + 1])
    fetch_cand.start()
    fetch_len.start()
    for g in range(groups):
        fetch(g).start()

    fetch_cand.wait()
    cand = cand_ref[...]
    owner = cand // QBD
    block = cand - owner * QBD
    lane = lax.broadcasted_iota(jnp.int32, (rows, LANES), 1).astype(jnp.float32)
    sub = lax.broadcasted_iota(jnp.int32, (rows, LANES), 0)
    for o in range(shards):
        mine = owner == o
        named = jnp.max(jnp.where(mine, block, 0), axis=1, keepdims=True)
        picks_ref[o:o + 1, :] = jnp.broadcast_to(jnp.max(named, axis=0, keepdims=True), (1, LANES))
        named_here = jnp.sum(jnp.where(mine, 1.0, 0.0), axis=1, keepdims=True)
        upto = jnp.broadcast_to(named_here, (rows, LANES))
        step = 1
        while step < rows:
            upto = upto + jnp.where(sub >= step, pltpu.roll(upto, step, 0), 0.0)
            step *= 2
        slots_ref[o:o + 1, :] = jnp.sum(jnp.where(upto <= lane, 1.0, 0.0), axis=0, keepdims=True)

    fetch_len.wait()
    u = lax.broadcasted_iota(jnp.int32, (PT, LANES), 0)

    @pl.loop(0, groups)
    def _(g):
        fetch(g).wait()
        for i in range(GROUP):
            p = g * GROUP + i
            tokens = raw_ref[p].astype(jnp.float32)
            clean_ref[p] = jnp.where(u < len_ref[p], tokens, tokens[0:1]).astype(jnp.bfloat16)


def prepare(shards, candidates, lengths, passages):
    hbm = pl.BlockSpec(memory_space=pltpu.HBM)
    vmem = pl.BlockSpec(memory_space=pltpu.VMEM)
    operands = [pltpu.with_memory_space_constraint(x, pltpu.HBM) for x in (candidates, lengths, passages)]
    return pl.pallas_call(
        prepare_kernel,
        out_shape=[
            jax.ShapeDtypeStruct((shards, LANES), jnp.float32),
            jax.ShapeDtypeStruct((shards, LANES), jnp.int32),
            jax.ShapeDtypeStruct(passages.shape, passages.dtype),
        ],
        in_specs=[hbm] * 3,
        out_specs=[vmem] * 3,
        scratch_shapes=[
            pltpu.VMEM(candidates.shape, candidates.dtype),
            pltpu.SMEM(lengths.shape, lengths.dtype),
            pltpu.VMEM(passages.shape, passages.dtype),
            pltpu.SemaphoreType.DMA((passages.shape[0] // GROUP + 2,)),
        ],
        compiler_params=pltpu.CompilerParams(vmem_limit_bytes=24 * 1024 * 1024),
        cost_estimate=pl.CostEstimate(flops=passages.size, bytes_accessed=2 * passages.size, transcendentals=0),
    )(*operands)


def picked(picks_ref, owner, q_ref):
    pick = jnp.max(picks_ref[pl.ds(owner, 1), :])
    return q_ref[pl.ds(pick * QB * QT, QB * QT), :]


def pack_kernel(partners, cand_ref, *refs):
    q_refs, out_ref = refs[:-1], refs[-1]
    me = lax.axis_index("psg")
    cand = cand_ref[...]
    owner = cand // QBD
    block = cand - owner * QBD
    for n, k in enumerate(partners):
        pick = jnp.max(jnp.where(owner == me ^ k, block, 0))
        out_ref[n * QB * QT:(n + 1) * QB * QT, :] = q_refs[n][pl.ds(pick * QB * QT, QB * QT), :]


def pack(partners, candidates, blocks):
    vmem = pl.BlockSpec(memory_space=pltpu.VMEM)
    return pl.pallas_call(
        functools.partial(pack_kernel, partners),
        out_shape=jax.ShapeDtypeStruct((len(partners) * QB * QT, DIM), blocks[0].dtype),
        in_specs=[vmem] * (1 + len(blocks)),
        out_specs=vmem,
        compiler_params=pltpu.CompilerParams(vmem_limit_bytes=4 * 1024 * 1024),
    )(candidates, *blocks)


def score_picked(sel_ref, p_ref, max_ref):
    count = p_ref.shape[0]
    sel = sel_ref[...]
    tokens = sel.shape[0]
    for g in range(count // GROUP):
        left = p_ref[g * GROUP:(g + 1) * GROUP].reshape(GROUP * PT, DIM)
        dots = lax.dot_general(left, sel, (((1,), (1,)), ((), ())), preferred_element_type=jnp.float32)
        best = jnp.max(dots.reshape(GROUP, PT, tokens), axis=1)
        max_ref[g * GROUP:(g + 1) * GROUP, :] = best

    best = max_ref[...]
    high = best.astype(jnp.bfloat16)
    rest = best - high.astype(jnp.float32)
    mid = rest.astype(jnp.bfloat16)
    low = (rest - mid.astype(jnp.float32)).astype(jnp.bfloat16)
    query = lax.broadcasted_iota(jnp.int32, (tokens // QT, tokens), 0)
    token = lax.broadcasted_iota(jnp.int32, (tokens // QT, tokens), 1)
    ones = jnp.where(token // QT == query, 1.0, 0.0).astype(jnp.bfloat16)
    total = jnp.zeros((tokens // QT, count), jnp.float32)
    for part in (low, mid, high):
        total = total + lax.dot_general(ones, part, (((1,), (1,)), ((), ())), preferred_element_type=jnp.float32)
    return total * (1.0 / QT)


def score_kernel(partners, slots_ref, picks_ref, p_ref, *refs):
    q_refs, (out_ref, sel_ref, max_ref) = refs[:-3], refs[-3:]
    me = lax.axis_index("psg")
    for n, k in enumerate(partners):
        sel_ref[n * QB * QT:(n + 1) * QB * QT, :] = picked(picks_ref, me ^ k, q_refs[n])
    total = score_picked(sel_ref, p_ref, max_ref)
    for n, k in enumerate(partners):
        out_ref[n, 0:QB, :] = total[n * QB:(n + 1) * QB]
        out_ref[n, QB:QB + 1, :] = slots_ref[pl.ds(me ^ k, 1), :]


def join_kernel(partners, slots_ref, p_ref, sel_ref, earlier_ref, out_ref, max_ref):
    me = lax.axis_index("psg")
    total = score_picked(sel_ref, p_ref, max_ref)
    for n, k in enumerate(partners):
        out_ref[me ^ k, 0:QB, :] = total[n * QB:(n + 1) * QB]
        out_ref[me ^ k, QB:QB + 1, :] = slots_ref[pl.ds(me ^ k, 1), :]
        out_ref[me ^ k ^ 1] = earlier_ref[n]


def all_kernel(slots_ref, picks_ref, p_ref, q_ref, out_ref, sel_ref, max_ref):
    some = q_ref.shape[0]
    for n in range(some):
        sel_ref[n * QB * QT:(n + 1) * QB * QT, :] = picked(picks_ref, n, q_ref.at[n])
    total = score_picked(sel_ref, p_ref, max_ref)
    for n in range(some):
        out_ref[n, 0:QB, :] = total[n * QB:(n + 1) * QB]
        out_ref[n, QB:QB + 1, :] = slots_ref[n:n + 1, :]


def score(kernel, tiles, some, selects, passages, *more):
    count = passages.shape[0]
    vmem = pl.BlockSpec(memory_space=pltpu.VMEM)
    return pl.pallas_call(
        kernel,
        out_shape=jax.ShapeDtypeStruct((tiles, QB + 1, LANES), jnp.float32),
        in_specs=[vmem] * len(more),
        out_specs=vmem,
        scratch_shapes=[pltpu.VMEM((some * QB * QT, DIM), jnp.bfloat16)] * selects + [
            pltpu.VMEM((count, some * QB * QT), jnp.float32),
        ],
        compiler_params=pltpu.CompilerParams(vmem_limit_bytes=32 * 1024 * 1024),
        cost_estimate=pl.CostEstimate(
            flops=2 * passages.size * some * QB * QT, bytes_accessed=2 * passages.size, transcendentals=0
        ),
    )(*more)


def place_kernel(in_ref, out_ref):
    slots = out_ref.shape[-1]
    m = lax.broadcasted_iota(jnp.int32, (PBS, LANES), 0)
    for j in range(in_ref.shape[0]):
        row = in_ref[j, QB:QB + 1, :].astype(jnp.int32)
        where = jnp.minimum(row * PBS, LANES - PBS) + m
        for i in range(QB):
            tile = jnp.broadcast_to(in_ref[j, i:i + 1, :], (PBS, LANES))
            out_ref[j, i] = jnp.take_along_axis(tile, where, axis=1)[:, :slots]


def place(tiles, slots):
    vmem = pl.BlockSpec(memory_space=pltpu.VMEM)
    shards = tiles.shape[0]
    return pl.pallas_call(
        place_kernel,
        out_shape=jax.ShapeDtypeStruct((shards, QB, PBS, slots), jnp.float32),
        in_specs=[vmem],
        out_specs=vmem,
        compiler_params=pltpu.CompilerParams(vmem_limit_bytes=8 * 1024 * 1024),
    )(tiles)


def by_partners(own, shards, candidates, lengths, passages):
    def swap(x, k):
        return lax.ppermute(x, "psg", [(j, j ^ k) for j in range(shards)])

    near = list(range(0, shards, 2))
    theirs = swap(candidates, 1)
    queries = {0: own} | {k: swap(own, k) for k in reversed(near[1:])}
    slots, picks, clean = prepare(shards, candidates, lengths, passages)
    *arrived, clean = lax.optimization_barrier((*[queries[k] for k in near[1:]], clean))
    blocks = [own, *arrived]
    far = swap(pack(near, theirs, blocks), 1)
    tiles = score(
        functools.partial(score_kernel, near), len(near), len(near), 1, clean, slots, picks, clean, *blocks
    )
    far, tiles = lax.optimization_barrier((far, tiles))
    return score(
        functools.partial(join_kernel, [k + 1 for k in near]), shards, len(near), 0, clean, slots, clean, far, tiles
    )


def by_gather(own, shards, candidates, lengths, passages):
    slots, picks, clean = prepare(shards, candidates, lengths, passages)
    gathered = lax.all_gather(own, "psg", axis=0)
    some = min(shards, 8)

    def score_some(items):
        return score(all_kernel, some, some, 1, clean, items[0], items[1], clean, items[2])

    parts = [x.reshape(shards // some, some, *x.shape[1:]) for x in (slots, picks, gathered)]
    return lax.map(score_some, parts).reshape(shards, QB + 1, LANES)


def per_device(queries, passages, lengths, candidates):
    shards = lax.axis_size("psg")
    rows = passages.shape[0] // PBS
    form = by_partners if shards in (4, 8) else by_gather
    tiles = form(
        queries.reshape(QBD * QB * QT, DIM), shards, candidates.reshape(rows, KB), lengths, passages
    )
    tiles = lax.all_to_all(tiles, "psg", split_axis=0, concat_axis=0, tiled=True)
    return place(tiles, rows * KB // shards).transpose(0, 3, 1, 2)[None]


def solution(mesh):
    return jax.shard_map(
        per_device,
        mesh=mesh,
        in_specs=(
            P(("grp", "psg", "qry"), None, None),
            P(("grp", "psg"), None, None),
            P(("grp", "psg")),
            P("qry", ("grp", "psg"), None),
        ),
        out_specs=P(("grp", "psg", "qry"), None, None, None, None),
        check_vma=False,
    )
```

```python
import functools

import jax
import jax.numpy as jnp
from jax import lax
from jax.experimental import pallas as pl
from jax.experimental.pallas import tpu as pltpu
from jax.sharding import PartitionSpec as P

DIM = 128
QT = 32
PT = 64
QB = 2
QBD = 4
PBS = 16
KB = 32
LANES = 128
GROUP = 8


def prepare_kernel(
    cand_hbm, len_hbm, p_hbm, slots_ref, picks_ref, clean_ref, cand_ref, len_ref, raw_ref, sems
):
    rows = cand_ref.shape[0]
    shards = slots_ref.shape[0]
    groups = p_hbm.shape[0] // GROUP

    def fetch(g):
        part = pl.ds(g * GROUP, GROUP)
        return pltpu.make_async_copy(p_hbm.at[part], raw_ref.at[part], sems.at[g])

    fetch_cand = pltpu.make_async_copy(cand_hbm, cand_ref, sems.at[groups])
    fetch_len = pltpu.make_async_copy(len_hbm, len_ref, sems.at[groups + 1])
    fetch_cand.start()
    fetch_len.start()
    for g in range(groups):
        fetch(g).start()

    fetch_cand.wait()
    cand = cand_ref[...]
    owner = cand // QBD
    block = cand - owner * QBD
    lane = lax.broadcasted_iota(jnp.int32, (rows, LANES), 1).astype(jnp.float32)
    sub = lax.broadcasted_iota(jnp.int32, (rows, LANES), 0)
    for o in range(shards):
        mine = owner == o
        named = jnp.max(jnp.where(mine, block, 0), axis=1, keepdims=True)
        picks_ref[o:o + 1, :] = jnp.broadcast_to(jnp.max(named, axis=0, keepdims=True), (1, LANES))
        named_here = jnp.sum(jnp.where(mine, 1.0, 0.0), axis=1, keepdims=True)
        upto = jnp.broadcast_to(named_here, (rows, LANES))
        step = 1
        while step < rows:
            upto = upto + jnp.where(sub >= step, pltpu.roll(upto, step, 0), 0.0)
            step *= 2
        slots_ref[o:o + 1, :] = jnp.sum(jnp.where(upto <= lane, 1.0, 0.0), axis=0, keepdims=True)

    fetch_len.wait()
    u = lax.broadcasted_iota(jnp.int32, (PT, LANES), 0)

    @pl.loop(0, groups)
    def _(g):
        fetch(g).wait()
        for i in range(GROUP):
            p = g * GROUP + i
            tokens = raw_ref[p].astype(jnp.float32)
            clean_ref[p] = jnp.where(u < len_ref[p], tokens, tokens[0:1]).astype(jnp.bfloat16)


def prepare(shards, candidates, lengths, passages):
    hbm = pl.BlockSpec(memory_space=pltpu.HBM)
    vmem = pl.BlockSpec(memory_space=pltpu.VMEM)
    operands = [pltpu.with_memory_space_constraint(x, pltpu.HBM) for x in (candidates, lengths, passages)]
    return pl.pallas_call(
        prepare_kernel,
        out_shape=[
            jax.ShapeDtypeStruct((shards, LANES), jnp.float32),
            jax.ShapeDtypeStruct((shards, LANES), jnp.int32),
            jax.ShapeDtypeStruct(passages.shape, passages.dtype),
        ],
        in_specs=[hbm] * 3,
        out_specs=[vmem] * 3,
        scratch_shapes=[
            pltpu.VMEM(candidates.shape, candidates.dtype),
            pltpu.SMEM(lengths.shape, lengths.dtype),
            pltpu.VMEM(passages.shape, passages.dtype),
            pltpu.SemaphoreType.DMA((passages.shape[0] // GROUP + 2,)),
        ],
        compiler_params=pltpu.CompilerParams(vmem_limit_bytes=24 * 1024 * 1024),
        cost_estimate=pl.CostEstimate(flops=passages.size, bytes_accessed=2 * passages.size, transcendentals=0),
    )(*operands)


def picked(picks_ref, owner, q_ref):
    pick = jnp.max(picks_ref[pl.ds(owner, 1), :])
    return q_ref[pl.ds(pick * QB * QT, QB * QT), :]


def pack_kernel(partners, cand_ref, *refs):
    q_refs, out_ref = refs[:-1], refs[-1]
    me = lax.axis_index("psg")
    cand = cand_ref[...]
    owner = cand // QBD
    block = cand - owner * QBD
    for n, k in enumerate(partners):
        pick = jnp.max(jnp.where(owner == me ^ k, block, 0))
        out_ref[n * QB * QT:(n + 1) * QB * QT, :] = q_refs[n][pl.ds(pick * QB * QT, QB * QT), :]


def pack(partners, candidates, blocks):
    vmem = pl.BlockSpec(memory_space=pltpu.VMEM)
    return pl.pallas_call(
        functools.partial(pack_kernel, partners),
        out_shape=jax.ShapeDtypeStruct((len(partners) * QB * QT, DIM), blocks[0].dtype),
        in_specs=[vmem] * (1 + len(blocks)),
        out_specs=vmem,
        compiler_params=pltpu.CompilerParams(vmem_limit_bytes=4 * 1024 * 1024),
    )(candidates, *blocks)


def score_picked(sel_ref, p_ref, max_ref):
    count = p_ref.shape[0]
    sel = sel_ref[...]
    tokens = sel.shape[0]
    for g in range(count // GROUP):
        left = p_ref[g * GROUP:(g + 1) * GROUP].reshape(GROUP * PT, DIM)
        dots = lax.dot_general(left, sel, (((1,), (1,)), ((), ())), preferred_element_type=jnp.float32)
        best = jnp.max(dots.reshape(GROUP, PT, tokens), axis=1)
        max_ref[g * GROUP:(g + 1) * GROUP, :] = best

    best = max_ref[...]
    high = best.astype(jnp.bfloat16)
    rest = best - high.astype(jnp.float32)
    mid = rest.astype(jnp.bfloat16)
    low = (rest - mid.astype(jnp.float32)).astype(jnp.bfloat16)
    query = lax.broadcasted_iota(jnp.int32, (tokens // QT, tokens), 0)
    token = lax.broadcasted_iota(jnp.int32, (tokens // QT, tokens), 1)
    ones = jnp.where(token // QT == query, 1.0, 0.0).astype(jnp.bfloat16)
    total = jnp.zeros((tokens // QT, count), jnp.float32)
    for part in (low, mid, high):
        total = total + lax.dot_general(ones, part, (((1,), (1,)), ((), ())), preferred_element_type=jnp.float32)
    return total * (1.0 / QT)


def score_kernel(partners, slots_ref, picks_ref, p_ref, *refs):
    q_refs, (out_ref, sel_ref, max_ref) = refs[:-3], refs[-3:]
    me = lax.axis_index("psg")
    for n, k in enumerate(partners):
        sel_ref[n * QB * QT:(n + 1) * QB * QT, :] = picked(picks_ref, me ^ k, q_refs[n])
    total = score_picked(sel_ref, p_ref, max_ref)
    for n, k in enumerate(partners):
        out_ref[n, 0:QB, :] = total[n * QB:(n + 1) * QB]
        out_ref[n, QB:QB + 1, :] = slots_ref[pl.ds(me ^ k, 1), :]


def score_far_kernel(partners, slots_ref, p_ref, sel_ref, out_ref, max_ref):
    me = lax.axis_index("psg")
    total = score_picked(sel_ref, p_ref, max_ref)
    for n, k in enumerate(partners):
        out_ref[n, 0:QB, :] = total[n * QB:(n + 1) * QB]
        out_ref[n, QB:QB + 1, :] = slots_ref[pl.ds(me ^ k, 1), :]


def all_kernel(slots_ref, picks_ref, p_ref, q_ref, out_ref, sel_ref, max_ref):
    some = q_ref.shape[0]
    for n in range(some):
        sel_ref[n * QB * QT:(n + 1) * QB * QT, :] = picked(picks_ref, n, q_ref.at[n])
    total = score_picked(sel_ref, p_ref, max_ref)
    for n in range(some):
        out_ref[n, 0:QB, :] = total[n * QB:(n + 1) * QB]
        out_ref[n, QB:QB + 1, :] = slots_ref[n:n + 1, :]


def score(kernel, tiles, some, selects, passages, *more):
    count = passages.shape[0]
    vmem = pl.BlockSpec(memory_space=pltpu.VMEM)
    return pl.pallas_call(
        kernel,
        out_shape=jax.ShapeDtypeStruct((tiles, QB + 1, LANES), jnp.float32),
        in_specs=[vmem] * len(more),
        out_specs=vmem,
        scratch_shapes=[pltpu.VMEM((some * QB * QT, DIM), jnp.bfloat16)] * selects + [
            pltpu.VMEM((count, some * QB * QT), jnp.float32),
        ],
        compiler_params=pltpu.CompilerParams(vmem_limit_bytes=32 * 1024 * 1024),
        cost_estimate=pl.CostEstimate(
            flops=2 * passages.size * some * QB * QT, bytes_accessed=2 * passages.size, transcendentals=0
        ),
    )(*more)


def collect(tiles):
    arrays = {id(array): array for array, _, _ in tiles}
    places = {key: n for n, key in enumerate(arrays)}
    return list(arrays.values()), [(places[id(array)], n, source) for array, n, source in tiles]


def join_kernel(tiles, *refs):
    for n, (array, index, _) in enumerate(tiles):
        refs[-1][n] = refs[array][index]


def join(tiles):
    arrays, tiles = collect(tiles)
    vmem = pl.BlockSpec(memory_space=pltpu.VMEM)
    return pl.pallas_call(
        functools.partial(join_kernel, tiles),
        out_shape=jax.ShapeDtypeStruct((len(tiles), QB + 1, LANES), jnp.float32),
        in_specs=[vmem] * len(arrays),
        out_specs=vmem,
        compiler_params=pltpu.CompilerParams(vmem_limit_bytes=4 * 1024 * 1024),
    )(*arrays)


def place_kernel(tiles, paired, *refs):
    out_ref = refs[-1]
    slots = out_ref.shape[-1]
    me = lax.axis_index("psg") if paired else 0
    m = lax.broadcasted_iota(jnp.int32, (PBS, LANES), 0)
    for array, index, source in tiles:
        tile_ref = refs[array].at[index]
        row = tile_ref[QB:QB + 1, :].astype(jnp.int32)
        where = jnp.minimum(row * PBS, LANES - PBS) + m
        for i in range(QB):
            tile = jnp.broadcast_to(tile_ref[i:i + 1, :], (PBS, LANES))
            out_ref[me ^ source, i] = jnp.take_along_axis(tile, where, axis=1)[:, :slots]


def place(tiles, paired, slots):
    arrays, tiles = collect(tiles)
    vmem = pl.BlockSpec(memory_space=pltpu.VMEM)
    return pl.pallas_call(
        functools.partial(place_kernel, tiles, paired),
        out_shape=jax.ShapeDtypeStruct((len(tiles), QB, PBS, slots), jnp.float32),
        in_specs=[vmem] * len(arrays),
        out_specs=vmem,
        compiler_params=pltpu.CompilerParams(vmem_limit_bytes=8 * 1024 * 1024),
    )(*arrays)


def by_partners(own, shards, slot_count, candidates, lengths, passages):
    def swap(x, k):
        return lax.ppermute(x, "psg", [(j, j ^ k) for j in range(shards)])

    near = list(range(0, shards, 2))
    theirs = swap(candidates, 1)
    queries = {0: own} | {k: swap(own, k) for k in reversed(near[1:])}
    slots, picks, clean = prepare(shards, candidates, lengths, passages)
    *arrived, clean = lax.optimization_barrier((*[queries[k] for k in near[1:]], clean))
    blocks = [own, *arrived]
    far = swap(pack(near, theirs, blocks), 1)
    near_tiles = score(
        functools.partial(score_kernel, near), len(near), len(near), 1, clean, slots, picks, clean, *blocks
    )
    far, near_tiles = lax.optimization_barrier((far, near_tiles))
    far_tiles = score(
        functools.partial(score_far_kernel, [k + 1 for k in near]), len(near), len(near), 0, clean, slots, clean, far
    )
    joined = swap(far_tiles, 1)
    tiles = {k: [(near_tiles, n, 0), (joined, n, 1)] for n, k in enumerate(near)}
    step = 2
    while step < shards:
        across = [k for k in tiles if k & step]
        handed = [(k ^ step, source ^ step) for k in across for _, _, source in tiles[k]]
        joined = swap(join([tile for k in across for tile in tiles.pop(k)]), step)
        for n, (k, source) in enumerate(handed):
            tiles[k].append((joined, n, source))
        step *= 2
    return place(tiles[0], True, slot_count)


def by_gather(own, shards, slot_count, candidates, lengths, passages):
    slots, picks, clean = prepare(shards, candidates, lengths, passages)
    gathered = lax.all_gather(own, "psg", axis=0)
    some = min(shards, 8)

    def score_some(items):
        return score(all_kernel, some, some, 1, clean, items[0], items[1], clean, items[2])

    parts = [x.reshape(shards // some, some, *x.shape[1:]) for x in (slots, picks, gathered)]
    tiles = lax.map(score_some, parts).reshape(shards, QB + 1, LANES)
    tiles = lax.all_to_all(tiles, "psg", split_axis=0, concat_axis=0, tiled=True)
    return place([(tiles, n, n) for n in range(shards)], False, slot_count)


def per_device(queries, passages, lengths, candidates):
    shards = lax.axis_size("psg")
    rows = passages.shape[0] // PBS
    form = by_partners if shards in (4, 8) else by_gather
    placed = form(
        queries.reshape(QBD * QB * QT, DIM), shards, rows * KB // shards,
        candidates.reshape(rows, KB), lengths, passages,
    )
    return placed.transpose(0, 3, 1, 2)[None]


def solution(mesh):
    return jax.shard_map(
        per_device,
        mesh=mesh,
        in_specs=(
            P(("grp", "psg", "qry"), None, None),
            P(("grp", "psg"), None, None),
            P(("grp", "psg")),
            P("qry", ("grp", "psg"), None),
        ),
        out_specs=P(("grp", "psg", "qry"), None, None, None, None),
        check_vma=False,
    )
```

```python
import functools

import jax
import jax.numpy as jnp
from jax import lax
from jax.experimental import pallas as pl
from jax.experimental.pallas import tpu as pltpu
from jax.sharding import PartitionSpec as P

DIM = 128
QT = 32
PT = 64
QB = 2
QBD = 4
PBS = 16
KB = 32
LANES = 128
GROUP = 8


def prepare_kernel(
    cand_hbm, len_hbm, p_hbm, slots_ref, picks_ref, clean_ref, cand_ref, len_ref, raw_ref, sems
):
    rows = cand_ref.shape[0]
    shards = slots_ref.shape[0]
    groups = p_hbm.shape[0] // GROUP

    def fetch(g):
        part = pl.ds(g * GROUP, GROUP)
        return pltpu.make_async_copy(p_hbm.at[part], raw_ref.at[part], sems.at[g])

    fetch_cand = pltpu.make_async_copy(cand_hbm, cand_ref, sems.at[groups])
    fetch_len = pltpu.make_async_copy(len_hbm, len_ref, sems.at[groups + 1])
    fetch_cand.start()
    fetch_len.start()
    for g in range(groups):
        fetch(g).start()

    fetch_cand.wait()
    cand = cand_ref[...]
    owner = cand // QBD
    block = cand - owner * QBD
    lane = lax.broadcasted_iota(jnp.int32, (rows, LANES), 1).astype(jnp.float32)
    sub = lax.broadcasted_iota(jnp.int32, (rows, LANES), 0)
    for o in range(shards):
        mine = owner == o
        named = jnp.max(jnp.where(mine, block, 0), axis=1, keepdims=True)
        picks_ref[o:o + 1, :] = jnp.broadcast_to(jnp.max(named, axis=0, keepdims=True), (1, LANES))
        named_here = jnp.sum(jnp.where(mine, 1.0, 0.0), axis=1, keepdims=True)
        upto = jnp.broadcast_to(named_here, (rows, LANES))
        step = 1
        while step < rows:
            upto = upto + jnp.where(sub >= step, pltpu.roll(upto, step, 0), 0.0)
            step *= 2
        slots_ref[o:o + 1, :] = jnp.sum(jnp.where(upto <= lane, 1.0, 0.0), axis=0, keepdims=True)

    fetch_len.wait()
    u = lax.broadcasted_iota(jnp.int32, (PT, LANES), 0)

    @pl.loop(0, groups)
    def _(g):
        fetch(g).wait()
        for i in range(GROUP):
            p = g * GROUP + i
            tokens = raw_ref[p].astype(jnp.float32)
            clean_ref[p] = jnp.where(u < len_ref[p], tokens, tokens[0:1]).astype(jnp.bfloat16)


def prepare(shards, candidates, lengths, passages):
    hbm = pl.BlockSpec(memory_space=pltpu.HBM)
    vmem = pl.BlockSpec(memory_space=pltpu.VMEM)
    operands = [pltpu.with_memory_space_constraint(x, pltpu.HBM) for x in (candidates, lengths, passages)]
    return pl.pallas_call(
        prepare_kernel,
        out_shape=[
            jax.ShapeDtypeStruct((shards, LANES), jnp.float32),
            jax.ShapeDtypeStruct((shards, LANES), jnp.int32),
            jax.ShapeDtypeStruct(passages.shape, passages.dtype),
        ],
        in_specs=[hbm] * 3,
        out_specs=[vmem] * 3,
        scratch_shapes=[
            pltpu.VMEM(candidates.shape, candidates.dtype),
            pltpu.SMEM(lengths.shape, lengths.dtype),
            pltpu.VMEM(passages.shape, passages.dtype),
            pltpu.SemaphoreType.DMA((passages.shape[0] // GROUP + 2,)),
        ],
        compiler_params=pltpu.CompilerParams(vmem_limit_bytes=24 * 1024 * 1024),
        cost_estimate=pl.CostEstimate(flops=passages.size, bytes_accessed=2 * passages.size, transcendentals=0),
    )(*operands)


def picked(picks_ref, owner, q_ref):
    pick = jnp.max(picks_ref[pl.ds(owner, 1), :])
    return q_ref[pl.ds(pick * QB * QT, QB * QT), :]


def pack_kernel(partners, cand_ref, *refs):
    q_refs, out_ref = refs[:-1], refs[-1]
    me = lax.axis_index("psg")
    cand = cand_ref[...]
    owner = cand // QBD
    block = cand - owner * QBD
    for n, k in enumerate(partners):
        pick = jnp.max(jnp.where(owner == me ^ k, block, 0))
        out_ref[n * QB * QT:(n + 1) * QB * QT, :] = q_refs[n][pl.ds(pick * QB * QT, QB * QT), :]


def pack(partners, candidates, blocks):
    vmem = pl.BlockSpec(memory_space=pltpu.VMEM)
    return pl.pallas_call(
        functools.partial(pack_kernel, partners),
        out_shape=jax.ShapeDtypeStruct((len(partners) * QB * QT, DIM), blocks[0].dtype),
        in_specs=[vmem] * (1 + len(blocks)),
        out_specs=vmem,
        compiler_params=pltpu.CompilerParams(vmem_limit_bytes=4 * 1024 * 1024),
    )(candidates, *blocks)


def score_picked(sel_ref, p_ref, max_ref, piece):
    count = p_ref.shape[0]
    sel = sel_ref[...]
    tokens = sel.shape[0]
    for g in range(0, count, piece):
        left = p_ref[g:g + piece].reshape(piece * PT, DIM)
        dots = lax.dot_general(left, sel, (((1,), (1,)), ((), ())), preferred_element_type=jnp.float32)
        max_ref[g:g + piece, :] = jnp.max(dots.reshape(piece, PT, tokens), axis=1)

    best = max_ref[...]
    high = best.astype(jnp.bfloat16)
    rest = best - high.astype(jnp.float32)
    mid = rest.astype(jnp.bfloat16)
    low = (rest - mid.astype(jnp.float32)).astype(jnp.bfloat16)
    query = lax.broadcasted_iota(jnp.int32, (tokens // QT, tokens), 0)
    token = lax.broadcasted_iota(jnp.int32, (tokens // QT, tokens), 1)
    ones = jnp.where(token // QT == query, 1.0, 0.0).astype(jnp.bfloat16)
    total = jnp.zeros((tokens // QT, count), jnp.float32)
    for part in (low, mid, high):
        total = total + lax.dot_general(ones, part, (((1,), (1,)), ((), ())), preferred_element_type=jnp.float32)
    return total * (1.0 / QT)


def score_kernel(partners, slots_ref, picks_ref, p_ref, *refs):
    q_refs, (out_ref, sel_ref, max_ref) = refs[:-3], refs[-3:]
    me = lax.axis_index("psg")
    for n, k in enumerate(partners):
        sel_ref[n * QB * QT:(n + 1) * QB * QT, :] = picked(picks_ref, me ^ k, q_refs[n])
    total = score_picked(sel_ref, p_ref, max_ref, 16)
    for n, k in enumerate(partners):
        out_ref[n, 0:QB, :] = total[n * QB:(n + 1) * QB]
        out_ref[n, QB:QB + 1, :] = slots_ref[pl.ds(me ^ k, 1), :]


def join_kernel(partners, slots_ref, p_ref, sel_ref, earlier_ref, out_ref, max_ref):
    me = lax.axis_index("psg")
    total = score_picked(sel_ref, p_ref, max_ref, 32)
    for n, k in enumerate(partners):
        out_ref[me ^ k, 0:QB, :] = total[n * QB:(n + 1) * QB]
        out_ref[me ^ k, QB:QB + 1, :] = slots_ref[pl.ds(me ^ k, 1), :]
        out_ref[me ^ k ^ 1] = earlier_ref[n]


def all_kernel(slots_ref, picks_ref, p_ref, q_ref, out_ref, sel_ref, max_ref):
    some = q_ref.shape[0]
    for n in range(some):
        sel_ref[n * QB * QT:(n + 1) * QB * QT, :] = picked(picks_ref, n, q_ref.at[n])
    total = score_picked(sel_ref, p_ref, max_ref, GROUP)
    for n in range(some):
        out_ref[n, 0:QB, :] = total[n * QB:(n + 1) * QB]
        out_ref[n, QB:QB + 1, :] = slots_ref[n:n + 1, :]


def score(kernel, tiles, some, selects, passages, *more):
    count = passages.shape[0]
    vmem = pl.BlockSpec(memory_space=pltpu.VMEM)
    return pl.pallas_call(
        kernel,
        out_shape=jax.ShapeDtypeStruct((tiles, QB + 1, LANES), jnp.float32),
        in_specs=[vmem] * len(more),
        out_specs=vmem,
        scratch_shapes=[pltpu.VMEM((some * QB * QT, DIM), jnp.bfloat16)] * selects + [
            pltpu.VMEM((count, some * QB * QT), jnp.float32),
        ],
        compiler_params=pltpu.CompilerParams(vmem_limit_bytes=32 * 1024 * 1024),
        cost_estimate=pl.CostEstimate(
            flops=2 * passages.size * some * QB * QT, bytes_accessed=2 * passages.size, transcendentals=0
        ),
    )(*more)


def place_kernel(in_ref, out_ref):
    slots = out_ref.shape[-1]
    m = lax.broadcasted_iota(jnp.int32, (PBS, LANES), 0)
    for j in range(in_ref.shape[0]):
        row = in_ref[j, QB:QB + 1, :].astype(jnp.int32)
        where = jnp.minimum(row * PBS, LANES - PBS) + m
        for i in range(QB):
            tile = jnp.broadcast_to(in_ref[j, i:i + 1, :], (PBS, LANES))
            out_ref[j, i] = jnp.take_along_axis(tile, where, axis=1)[:, :slots]


def place(tiles, slots):
    vmem = pl.BlockSpec(memory_space=pltpu.VMEM)
    shards = tiles.shape[0]
    return pl.pallas_call(
        place_kernel,
        out_shape=jax.ShapeDtypeStruct((shards, QB, PBS, slots), jnp.float32),
        in_specs=[vmem],
        out_specs=vmem,
        compiler_params=pltpu.CompilerParams(vmem_limit_bytes=8 * 1024 * 1024),
    )(tiles)


def by_partners(own, shards, candidates, lengths, passages):
    def swap(x, k):
        return lax.ppermute(x, "psg", [(j, j ^ k) for j in range(shards)])

    near = list(range(0, shards, 2))
    theirs = swap(candidates, 1)
    queries = {0: own} | {k: swap(own, k) for k in near[1:]}
    slots, picks, clean = prepare(shards, candidates, lengths, passages)
    clean, *arrived = lax.optimization_barrier((clean, *[queries[k] for k in reversed(near[1:])]))
    blocks = [own, *reversed(arrived)]
    far = swap(pack(near, theirs, blocks), 1)
    tiles = score(
        functools.partial(score_kernel, near), len(near), len(near), 1, clean, slots, picks, clean, *blocks
    )
    far, tiles = lax.optimization_barrier((far, tiles))
    return score(
        functools.partial(join_kernel, [k + 1 for k in near]), shards, len(near), 0, clean, slots, clean, far, tiles
    )


def by_gather(own, shards, candidates, lengths, passages):
    slots, picks, clean = prepare(shards, candidates, lengths, passages)
    gathered = lax.all_gather(own, "psg", axis=0)
    some = min(shards, 8)

    def score_some(items):
        return score(all_kernel, some, some, 1, clean, items[0], items[1], clean, items[2])

    parts = [x.reshape(shards // some, some, *x.shape[1:]) for x in (slots, picks, gathered)]
    return lax.map(score_some, parts).reshape(shards, QB + 1, LANES)


def per_device(queries, passages, lengths, candidates):
    shards = lax.axis_size("psg")
    rows = passages.shape[0] // PBS
    form = by_partners if shards in (4, 8) else by_gather
    tiles = form(
        queries.reshape(QBD * QB * QT, DIM), shards, candidates.reshape(rows, KB), lengths, passages
    )
    tiles = lax.all_to_all(tiles, "psg", split_axis=0, concat_axis=0, tiled=True)
    return place(tiles, rows * KB // shards).transpose(0, 3, 1, 2)[None]


def solution(mesh):
    return jax.shard_map(
        per_device,
        mesh=mesh,
        in_specs=(
            P(("grp", "psg", "qry"), None, None),
            P(("grp", "psg"), None, None),
            P(("grp", "psg")),
            P("qry", ("grp", "psg"), None),
        ),
        out_specs=P(("grp", "psg", "qry"), None, None, None, None),
        check_vma=False,
    )
```

```python
import functools

import jax
import jax.numpy as jnp
from jax import lax
from jax.experimental import pallas as pl
from jax.experimental.pallas import tpu as pltpu
from jax.sharding import PartitionSpec as P

DIM = 128
QT = 32
PT = 64
QB = 2
QBD = 4
PBS = 16
KB = 32
LANES = 128
GROUP = 8


def clean_passages(len_hbm, p_hbm, clean_ref, len_ref, raw_ref, sems, meanwhile=lambda: None):
    groups = p_hbm.shape[0] // GROUP

    def fetch(g):
        part = pl.ds(g * GROUP, GROUP)
        return pltpu.make_async_copy(p_hbm.at[part], raw_ref.at[part], sems.at[g])

    fetch_len = pltpu.make_async_copy(len_hbm, len_ref, sems.at[groups])
    fetch_len.start()
    for g in range(groups):
        fetch(g).start()
    meanwhile()
    fetch_len.wait()
    u = lax.broadcasted_iota(jnp.int32, (PT, LANES), 0)

    @pl.loop(0, groups)
    def _(g):
        fetch(g).wait()
        for i in range(GROUP):
            p = g * GROUP + i
            tokens = raw_ref[p].astype(jnp.float32)
            clean_ref[p] = jnp.where(u < len_ref[p], tokens, tokens[0:1]).astype(jnp.bfloat16)


def read_candidates(cand_ref, slots_ref, picks_ref):
    rows = cand_ref.shape[0]
    cand = cand_ref[...]
    owner = cand // QBD
    block = cand - owner * QBD
    lane = lax.broadcasted_iota(jnp.int32, (rows, LANES), 1).astype(jnp.float32)
    sub = lax.broadcasted_iota(jnp.int32, (rows, LANES), 0)
    for o in range(slots_ref.shape[0]):
        mine = owner == o
        named = jnp.max(jnp.where(mine, block, 0), axis=1, keepdims=True)
        picks_ref[o:o + 1, :] = jnp.broadcast_to(jnp.max(named, axis=0, keepdims=True), (1, LANES))
        named_here = jnp.sum(jnp.where(mine, 1.0, 0.0), axis=1, keepdims=True)
        upto = jnp.broadcast_to(named_here, (rows, LANES))
        step = 1
        while step < rows:
            upto = upto + jnp.where(sub >= step, pltpu.roll(upto, step, 0), 0.0)
            step *= 2
        slots_ref[o:o + 1, :] = jnp.sum(jnp.where(upto <= lane, 1.0, 0.0), axis=0, keepdims=True)


def prepare_early_kernel(len_hbm, p_hbm, clean_ref, *scratch):
    @pl.when(lax.axis_index("qry") % 2 == 1)
    def _():
        clean_passages(len_hbm, p_hbm, clean_ref, *scratch)


def prepare_kernel(early, cand_hbm, len_hbm, p_hbm, *refs):
    early_refs, (slots_ref, picks_ref, clean_ref, len_ref, raw_ref, sems, cand_ref) = refs[:early], refs[early:]
    fetch_cand = pltpu.make_async_copy(cand_hbm, cand_ref, sems.at[sems.shape[0] - 1])
    fetch_cand.start()

    def candidates():
        fetch_cand.wait()
        read_candidates(cand_ref, slots_ref, picks_ref)

    def now():
        clean_passages(len_hbm, p_hbm, clean_ref, len_ref, raw_ref, sems, candidates)

    if not early:
        now()
        return
    odd = lax.axis_index("qry") % 2 == 1
    pl.when(jnp.logical_not(odd))(now)

    @pl.when(odd)
    def _():
        candidates()

        @pl.loop(0, clean_ref.shape[0] // GROUP)
        def _(g):
            part = pl.ds(g * GROUP, GROUP)
            clean_ref[part] = early_refs[0][part]


def prepare_scratch(lengths, passages):
    return [
        pltpu.SMEM(lengths.shape, lengths.dtype),
        pltpu.VMEM(passages.shape, passages.dtype),
        pltpu.SemaphoreType.DMA((passages.shape[0] // GROUP + 2,)),
    ]


def prepare_early(lengths, passages):
    hbm = pl.BlockSpec(memory_space=pltpu.HBM)
    return pl.pallas_call(
        prepare_early_kernel,
        out_shape=jax.ShapeDtypeStruct(passages.shape, passages.dtype),
        in_specs=[hbm] * 2,
        out_specs=pl.BlockSpec(memory_space=pltpu.VMEM),
        scratch_shapes=prepare_scratch(lengths, passages),
        compiler_params=pltpu.CompilerParams(vmem_limit_bytes=24 * 1024 * 1024),
    )(*[pltpu.with_memory_space_constraint(x, pltpu.HBM) for x in (lengths, passages)])


def prepare(shards, candidates, lengths, passages, *early):
    hbm = pl.BlockSpec(memory_space=pltpu.HBM)
    vmem = pl.BlockSpec(memory_space=pltpu.VMEM)
    operands = [pltpu.with_memory_space_constraint(x, pltpu.HBM) for x in (candidates, lengths, passages)]
    return pl.pallas_call(
        functools.partial(prepare_kernel, len(early)),
        out_shape=[
            jax.ShapeDtypeStruct((shards, LANES), jnp.float32),
            jax.ShapeDtypeStruct((shards, LANES), jnp.int32),
            jax.ShapeDtypeStruct(passages.shape, passages.dtype),
        ],
        in_specs=[hbm] * 3 + [vmem] * len(early),
        out_specs=[vmem] * 3,
        scratch_shapes=prepare_scratch(lengths, passages) + [pltpu.VMEM(candidates.shape, candidates.dtype)],
        compiler_params=pltpu.CompilerParams(vmem_limit_bytes=24 * 1024 * 1024),
        cost_estimate=pl.CostEstimate(flops=passages.size, bytes_accessed=2 * passages.size, transcendentals=0),
    )(*operands, *early)


def picked(picks_ref, owner, q_ref):
    pick = jnp.max(picks_ref[pl.ds(owner, 1), :])
    return q_ref[pl.ds(pick * QB * QT, QB * QT), :]


def pack_kernel(partners, cand_ref, *refs):
    q_refs, out_ref = refs[:-1], refs[-1]
    me = lax.axis_index("psg")
    cand = cand_ref[...]
    owner = cand // QBD
    block = cand - owner * QBD
    for n, k in enumerate(partners):
        pick = jnp.max(jnp.where(owner == me ^ k, block, 0))
        out_ref[n * QB * QT:(n + 1) * QB * QT, :] = q_refs[n][pl.ds(pick * QB * QT, QB * QT), :]


def pack(partners, candidates, blocks):
    vmem = pl.BlockSpec(memory_space=pltpu.VMEM)
    return pl.pallas_call(
        functools.partial(pack_kernel, partners),
        out_shape=jax.ShapeDtypeStruct((len(partners) * QB * QT, DIM), blocks[0].dtype),
        in_specs=[vmem] * (1 + len(blocks)),
        out_specs=vmem,
        compiler_params=pltpu.CompilerParams(vmem_limit_bytes=4 * 1024 * 1024),
    )(candidates, *blocks)


def score_picked(sel_ref, p_ref, max_ref):
    count = p_ref.shape[0]
    sel = sel_ref[...]
    tokens = sel.shape[0]
    for g in range(0, count, 2 * GROUP):
        left = p_ref[g:g + 2 * GROUP].reshape(2 * GROUP * PT, DIM)
        dots = lax.dot_general(left, sel, (((1,), (1,)), ((), ())), preferred_element_type=jnp.float32)
        max_ref[g:g + 2 * GROUP, :] = jnp.max(dots.reshape(2 * GROUP, PT, tokens), axis=1)

    best = max_ref[...]
    high = best.astype(jnp.bfloat16)
    rest = best - high.astype(jnp.float32)
    mid = rest.astype(jnp.bfloat16)
    low = (rest - mid.astype(jnp.float32)).astype(jnp.bfloat16)
    query = lax.broadcasted_iota(jnp.int32, (tokens // QT, tokens), 0)
    token = lax.broadcasted_iota(jnp.int32, (tokens // QT, tokens), 1)
    ones = jnp.where(token // QT == query, 1.0, 0.0).astype(jnp.bfloat16)
    total = jnp.zeros((tokens // QT, count), jnp.float32)
    for part in (low, mid, high):
        total = total + lax.dot_general(ones, part, (((1,), (1,)), ((), ())), preferred_element_type=jnp.float32)
    return total * (1.0 / QT)


def score_kernel(partners, slots_ref, picks_ref, p_ref, *refs):
    q_refs, (out_ref, sel_ref, max_ref) = refs[:-3], refs[-3:]
    me = lax.axis_index("psg")
    for n, k in enumerate(partners):
        sel_ref[n * QB * QT:(n + 1) * QB * QT, :] = picked(picks_ref, me ^ k, q_refs[n])
    total = score_picked(sel_ref, p_ref, max_ref)
    for n, k in enumerate(partners):
        out_ref[n, 0:QB, :] = total[n * QB:(n + 1) * QB]
        out_ref[n, QB:QB + 1, :] = slots_ref[pl.ds(me ^ k, 1), :]


def join_kernel(partners, slots_ref, p_ref, sel_ref, earlier_ref, out_ref, max_ref):
    me = lax.axis_index("psg")
    total = score_picked(sel_ref, p_ref, max_ref)
    for n, k in enumerate(partners):
        out_ref[me ^ k, 0:QB, :] = total[n * QB:(n + 1) * QB]
        out_ref[me ^ k, QB:QB + 1, :] = slots_ref[pl.ds(me ^ k, 1), :]
        out_ref[me ^ k ^ 1] = earlier_ref[n]


def all_kernel(slots_ref, picks_ref, p_ref, q_ref, out_ref, sel_ref, max_ref):
    some = q_ref.shape[0]
    for n in range(some):
        sel_ref[n * QB * QT:(n + 1) * QB * QT, :] = picked(picks_ref, n, q_ref.at[n])
    total = score_picked(sel_ref, p_ref, max_ref)
    for n in range(some):
        out_ref[n, 0:QB, :] = total[n * QB:(n + 1) * QB]
        out_ref[n, QB:QB + 1, :] = slots_ref[n:n + 1, :]


def score(kernel, tiles, some, selects, passages, *more):
    count = passages.shape[0]
    vmem = pl.BlockSpec(memory_space=pltpu.VMEM)
    return pl.pallas_call(
        kernel,
        out_shape=jax.ShapeDtypeStruct((tiles, QB + 1, LANES), jnp.float32),
        in_specs=[vmem] * len(more),
        out_specs=vmem,
        scratch_shapes=[pltpu.VMEM((some * QB * QT, DIM), jnp.bfloat16)] * selects + [
            pltpu.VMEM((count, some * QB * QT), jnp.float32),
        ],
        compiler_params=pltpu.CompilerParams(vmem_limit_bytes=32 * 1024 * 1024),
        cost_estimate=pl.CostEstimate(
            flops=2 * passages.size * some * QB * QT, bytes_accessed=2 * passages.size, transcendentals=0
        ),
    )(*more)


def place_kernel(in_ref, out_ref):
    slots = out_ref.shape[-1]
    m = lax.broadcasted_iota(jnp.int32, (PBS, LANES), 0)
    for j in range(in_ref.shape[0]):
        row = in_ref[j, QB:QB + 1, :].astype(jnp.int32)
        where = jnp.minimum(row * PBS, LANES - PBS) + m
        for i in range(QB):
            tile = jnp.broadcast_to(in_ref[j, i:i + 1, :], (PBS, LANES))
            out_ref[j, i] = jnp.take_along_axis(tile, where, axis=1)[:, :slots]


def place(tiles, slots):
    vmem = pl.BlockSpec(memory_space=pltpu.VMEM)
    shards = tiles.shape[0]
    return pl.pallas_call(
        place_kernel,
        out_shape=jax.ShapeDtypeStruct((shards, QB, PBS, slots), jnp.float32),
        in_specs=[vmem],
        out_specs=vmem,
        compiler_params=pltpu.CompilerParams(vmem_limit_bytes=8 * 1024 * 1024),
    )(tiles)


def by_partners(own, shards, candidates, lengths, passages):
    def swap(x, k):
        return lax.ppermute(x, "psg", [(j, j ^ k) for j in range(shards)])

    near = list(range(0, shards, 2))
    theirs = swap(candidates, 1)
    own, early = lax.optimization_barrier((own, prepare_early(lengths, passages)))
    queries = {0: own} | {k: swap(own, k) for k in near[1:]}
    slots, picks, clean = prepare(shards, candidates, lengths, passages, early)
    clean, *arrived = lax.optimization_barrier((clean, *[queries[k] for k in reversed(near[1:])]))
    blocks = [own, *reversed(arrived)]
    far = swap(pack(near, theirs, blocks), 1)
    tiles = score(
        functools.partial(score_kernel, near), len(near), len(near), 1, clean, slots, picks, clean, *blocks
    )
    far, tiles = lax.optimization_barrier((far, tiles))
    return score(
        functools.partial(join_kernel, [k + 1 for k in near]), shards, len(near), 0, clean, slots, clean, far, tiles
    )


def by_gather(own, shards, candidates, lengths, passages):
    slots, picks, clean = prepare(shards, candidates, lengths, passages)
    gathered = lax.all_gather(own, "psg", axis=0)
    some = min(shards, 8)

    def score_some(items):
        return score(all_kernel, some, some, 1, clean, items[0], items[1], clean, items[2])

    parts = [x.reshape(shards // some, some, *x.shape[1:]) for x in (slots, picks, gathered)]
    return lax.map(score_some, parts).reshape(shards, QB + 1, LANES)


def per_device(queries, passages, lengths, candidates):
    shards = lax.axis_size("psg")
    rows = passages.shape[0] // PBS
    form = by_partners if shards in (4, 8) else by_gather
    tiles = form(
        queries.reshape(QBD * QB * QT, DIM), shards, candidates.reshape(rows, KB), lengths, passages
    )
    tiles = lax.all_to_all(tiles, "psg", split_axis=0, concat_axis=0, tiled=True)
    return place(tiles, rows * KB // shards).transpose(0, 3, 1, 2)[None]


def solution(mesh):
    return jax.shard_map(
        per_device,
        mesh=mesh,
        in_specs=(
            P(("grp", "psg", "qry"), None, None),
            P(("grp", "psg"), None, None),
            P(("grp", "psg")),
            P("qry", ("grp", "psg"), None),
        ),
        out_specs=P(("grp", "psg", "qry"), None, None, None, None),
        check_vma=False,
    )
```

```python
import functools

import jax
import jax.numpy as jnp
from jax import lax
from jax.experimental import pallas as pl
from jax.experimental.pallas import tpu as pltpu
from jax.sharding import PartitionSpec as P

DIM = 128
QT = 32
PT = 64
QB = 2
QBD = 4
PBS = 16
KB = 32
LANES = 128
GROUP = 8


def prepare_kernel(
    cand_hbm, len_hbm, p_hbm, slots_ref, picks_ref, clean_ref, cand_ref, len_ref, raw_ref, sems
):
    rows = cand_ref.shape[0]
    shards = slots_ref.shape[0]
    groups = p_hbm.shape[0] // GROUP

    def fetch(g):
        part = pl.ds(g * GROUP, GROUP)
        return pltpu.make_async_copy(p_hbm.at[part], raw_ref.at[part], sems.at[g])

    fetch_cand = pltpu.make_async_copy(cand_hbm, cand_ref, sems.at[groups])
    fetch_len = pltpu.make_async_copy(len_hbm, len_ref, sems.at[groups + 1])
    fetch_cand.start()
    fetch_len.start()
    for g in range(groups):
        fetch(g).start()

    fetch_cand.wait()
    cand = cand_ref[...]
    owner = cand // QBD
    block = cand - owner * QBD
    lane = lax.broadcasted_iota(jnp.int32, (rows, LANES), 1).astype(jnp.float32)
    sub = lax.broadcasted_iota(jnp.int32, (rows, LANES), 0)
    for o in range(shards):
        mine = owner == o
        named = jnp.max(jnp.where(mine, block, 0), axis=1, keepdims=True)
        picks_ref[o:o + 1, :] = jnp.broadcast_to(jnp.max(named, axis=0, keepdims=True), (1, LANES))
        named_here = jnp.sum(jnp.where(mine, 1.0, 0.0), axis=1, keepdims=True)
        upto = jnp.broadcast_to(named_here, (rows, LANES))
        step = 1
        while step < rows:
            upto = upto + jnp.where(sub >= step, pltpu.roll(upto, step, 0), 0.0)
            step *= 2
        slots_ref[o:o + 1, :] = jnp.sum(jnp.where(upto <= lane, 1.0, 0.0), axis=0, keepdims=True)

    fetch_len.wait()
    u = lax.broadcasted_iota(jnp.int32, (PT, LANES), 0)

    @pl.loop(0, groups)
    def _(g):
        fetch(g).wait()
        for i in range(GROUP):
            p = g * GROUP + i
            tokens = raw_ref[p].astype(jnp.float32)
            clean_ref[p] = jnp.where(u < len_ref[p], tokens, tokens[0:1]).astype(jnp.bfloat16)


def prepare(shards, candidates, lengths, passages):
    hbm = pl.BlockSpec(memory_space=pltpu.HBM)
    vmem = pl.BlockSpec(memory_space=pltpu.VMEM)
    operands = [pltpu.with_memory_space_constraint(x, pltpu.HBM) for x in (candidates, lengths, passages)]
    return pl.pallas_call(
        prepare_kernel,
        out_shape=[
            jax.ShapeDtypeStruct((shards, LANES), jnp.float32),
            jax.ShapeDtypeStruct((shards, LANES), jnp.int32),
            jax.ShapeDtypeStruct(passages.shape, passages.dtype),
        ],
        in_specs=[hbm] * 3,
        out_specs=[vmem] * 3,
        scratch_shapes=[
            pltpu.VMEM(candidates.shape, candidates.dtype),
            pltpu.SMEM(lengths.shape, lengths.dtype),
            pltpu.VMEM(passages.shape, passages.dtype),
            pltpu.SemaphoreType.DMA((passages.shape[0] // GROUP + 2,)),
        ],
        compiler_params=pltpu.CompilerParams(vmem_limit_bytes=24 * 1024 * 1024),
        cost_estimate=pl.CostEstimate(flops=passages.size, bytes_accessed=2 * passages.size, transcendentals=0),
    )(*operands)


def picked(pick, takes_first, q_refs):
    parts = [ref[pl.ds(pick * QB * QT, QB * QT), :] for ref in q_refs]
    return jnp.where(takes_first, *parts) if len(parts) == 2 else parts[0]


def by_partner(partners, me, refs):
    refs = iter(refs)
    lowest = me >> 1 == 0
    return [(lowest | (me >> 1 == k >> 1), [next(refs) for _ in range(2 if k else 1)]) for k in partners]


def pack_kernel(partners, cand_ref, *refs):
    q_refs, out_ref = refs[:-1], refs[-1]
    me = lax.axis_index("psg")
    cand = cand_ref[...]
    owner = cand // QBD
    block = cand - owner * QBD
    for n, (k, (takes_first, some_refs)) in enumerate(zip(partners, by_partner(partners, me, q_refs))):
        pick = jnp.max(jnp.where(owner == me ^ k, block, 0))
        out_ref[n * QB * QT:(n + 1) * QB * QT, :] = picked(pick, takes_first, some_refs)


def pack(partners, candidates, blocks):
    vmem = pl.BlockSpec(memory_space=pltpu.VMEM)
    return pl.pallas_call(
        functools.partial(pack_kernel, partners),
        out_shape=jax.ShapeDtypeStruct((len(partners) * QB * QT, DIM), blocks[0].dtype),
        in_specs=[vmem] * (1 + len(blocks)),
        out_specs=vmem,
        compiler_params=pltpu.CompilerParams(vmem_limit_bytes=4 * 1024 * 1024),
    )(candidates, *blocks)


def score_picked(sel_ref, p_ref, max_ref):
    count = p_ref.shape[0]
    sel = sel_ref[...]
    tokens = sel.shape[0]
    piece = 2 * GROUP
    for g in range(0, count, piece):
        left = p_ref[g:g + piece].reshape(piece * PT, DIM)
        dots = lax.dot_general(left, sel, (((1,), (1,)), ((), ())), preferred_element_type=jnp.float32)
        max_ref[g:g + piece, :] = jnp.max(dots.reshape(piece, PT, tokens), axis=1)

    best = max_ref[...]
    high = best.astype(jnp.bfloat16)
    rest = best - high.astype(jnp.float32)
    mid = rest.astype(jnp.bfloat16)
    low = (rest - mid.astype(jnp.float32)).astype(jnp.bfloat16)
    query = lax.broadcasted_iota(jnp.int32, (tokens // QT, tokens), 0)
    token = lax.broadcasted_iota(jnp.int32, (tokens // QT, tokens), 1)
    ones = jnp.where(token // QT == query, 1.0, 0.0).astype(jnp.bfloat16)
    total = jnp.zeros((tokens // QT, count), jnp.float32)
    for part in (low, mid, high):
        total = total + lax.dot_general(ones, part, (((1,), (1,)), ((), ())), preferred_element_type=jnp.float32)
    return total * (1.0 / QT)


def score_kernel(partners, slots_ref, picks_ref, p_ref, *refs):
    q_refs, (out_ref, sel_ref, max_ref) = refs[:-3], refs[-3:]
    me = lax.axis_index("psg")
    for n, (k, (takes_first, some_refs)) in enumerate(zip(partners, by_partner(partners, me, q_refs))):
        pick = jnp.max(picks_ref[pl.ds(me ^ k, 1), :])
        sel_ref[n * QB * QT:(n + 1) * QB * QT, :] = picked(pick, takes_first, some_refs)
    total = score_picked(sel_ref, p_ref, max_ref)
    for n, k in enumerate(partners):
        out_ref[n, 0:QB, :] = total[n * QB:(n + 1) * QB]
        out_ref[n, QB:QB + 1, :] = slots_ref[pl.ds(me ^ k, 1), :]


def join_kernel(partners, slots_ref, p_ref, sel_ref, earlier_ref, out_ref, max_ref):
    me = lax.axis_index("psg")
    total = score_picked(sel_ref, p_ref, max_ref)
    for n, k in enumerate(partners):
        out_ref[me ^ k, 0:QB, :] = total[n * QB:(n + 1) * QB]
        out_ref[me ^ k, QB:QB + 1, :] = slots_ref[pl.ds(me ^ k, 1), :]
        out_ref[me ^ k ^ 1] = earlier_ref[n]


def all_kernel(slots_ref, picks_ref, p_ref, q_ref, out_ref, sel_ref, max_ref):
    some = q_ref.shape[0]
    for n in range(some):
        sel_ref[n * QB * QT:(n + 1) * QB * QT, :] = picked(jnp.max(picks_ref[n:n + 1, :]), True, [q_ref.at[n]])
    total = score_picked(sel_ref, p_ref, max_ref)
    for n in range(some):
        out_ref[n, 0:QB, :] = total[n * QB:(n + 1) * QB]
        out_ref[n, QB:QB + 1, :] = slots_ref[n:n + 1, :]


def score(kernel, tiles, some, selects, passages, *more):
    count = passages.shape[0]
    vmem = pl.BlockSpec(memory_space=pltpu.VMEM)
    return pl.pallas_call(
        kernel,
        out_shape=jax.ShapeDtypeStruct((tiles, QB + 1, LANES), jnp.float32),
        in_specs=[vmem] * len(more),
        out_specs=vmem,
        scratch_shapes=[pltpu.VMEM((some * QB * QT, DIM), jnp.bfloat16)] * selects + [
            pltpu.VMEM((count, some * QB * QT), jnp.float32),
        ],
        compiler_params=pltpu.CompilerParams(vmem_limit_bytes=32 * 1024 * 1024),
        cost_estimate=pl.CostEstimate(
            flops=2 * passages.size * some * QB * QT, bytes_accessed=2 * passages.size, transcendentals=0
        ),
    )(*more)


def place_kernel(in_ref, out_ref):
    slots = out_ref.shape[-1]
    m = lax.broadcasted_iota(jnp.int32, (PBS, LANES), 0)
    for j in range(in_ref.shape[0]):
        row = in_ref[j, QB:QB + 1, :].astype(jnp.int32)
        where = jnp.minimum(row * PBS, LANES - PBS) + m
        for i in range(QB):
            tile = jnp.broadcast_to(in_ref[j, i:i + 1, :], (PBS, LANES))
            out_ref[j, i] = jnp.take_along_axis(tile, where, axis=1)[:, :slots]


def place(tiles, slots):
    vmem = pl.BlockSpec(memory_space=pltpu.VMEM)
    shards = tiles.shape[0]
    return pl.pallas_call(
        place_kernel,
        out_shape=jax.ShapeDtypeStruct((shards, QB, PBS, slots), jnp.float32),
        in_specs=[vmem],
        out_specs=vmem,
        compiler_params=pltpu.CompilerParams(vmem_limit_bytes=8 * 1024 * 1024),
    )(tiles)


def by_partners(own, shards, candidates, lengths, passages):
    def swap(x, k):
        return lax.ppermute(x, "psg", [(j, j ^ k) for j in range(shards)])

    def swap_planes(x, low, high):
        ends = [(2 * low + j, 2 * high + j) for j in range(2)]
        return lax.ppermute(x, "psg", ends + [(high, low) for low, high in ends])

    near = list(range(0, shards, 2))
    theirs = swap(candidates, 1)
    pairs = [(low, high) for high in range(shards // 2) for low in range(high)]
    arrived = {pair: swap_planes(own, *pair) for pair in pairs}
    slots, picks, clean = prepare(shards, candidates, lengths, passages)
    clean, *swapped = lax.optimization_barrier((clean, *[arrived[pair] for pair in reversed(pairs)]))
    arrived = dict(zip(reversed(pairs), swapped))
    blocks = [own]
    for k in near[1:]:
        blocks += [arrived[pair] for pair in sorted(pairs) if pair[0] ^ pair[1] == k >> 1]
    far = swap(pack(near, theirs, blocks), 1)
    tiles = score(
        functools.partial(score_kernel, near), len(near), len(near), 1, clean, slots, picks, clean, *blocks
    )
    far, tiles = lax.optimization_barrier((far, tiles))
    return score(
        functools.partial(join_kernel, [k + 1 for k in near]), shards, len(near), 0, clean, slots, clean, far, tiles
    )


def by_gather(own, shards, candidates, lengths, passages):
    slots, picks, clean = prepare(shards, candidates, lengths, passages)
    gathered = lax.all_gather(own, "psg", axis=0)
    some = min(shards, 8)

    def score_some(items):
        return score(all_kernel, some, some, 1, clean, items[0], items[1], clean, items[2])

    parts = [x.reshape(shards // some, some, *x.shape[1:]) for x in (slots, picks, gathered)]
    return lax.map(score_some, parts).reshape(shards, QB + 1, LANES)


def per_device(queries, passages, lengths, candidates):
    shards = lax.axis_size("psg")
    rows = passages.shape[0] // PBS
    form = by_partners if shards == 8 else by_gather
    tiles = form(
        queries.reshape(QBD * QB * QT, DIM), shards, candidates.reshape(rows, KB), lengths, passages
    )
    tiles = lax.all_to_all(tiles, "psg", split_axis=0, concat_axis=0, tiled=True)
    return place(tiles, rows * KB // shards).transpose(0, 3, 1, 2)[None]


def solution(mesh):
    return jax.shard_map(
        per_device,
        mesh=mesh,
        in_specs=(
            P(("grp", "psg", "qry"), None, None),
            P(("grp", "psg"), None, None),
            P(("grp", "psg")),
            P("qry", ("grp", "psg"), None),
        ),
        out_specs=P(("grp", "psg", "qry"), None, None, None, None),
        check_vma=False,
    )
```

```python
import functools

import jax
import jax.numpy as jnp
from jax import lax
from jax.experimental import pallas as pl
from jax.experimental.pallas import tpu as pltpu
from jax.sharding import PartitionSpec as P

DIM = 128
QT = 32
PT = 64
QB = 2
QBD = 4
PBS = 16
KB = 32
LANES = 128
GROUP = 8


def prepare_kernel(
    cand_hbm, len_hbm, p_hbm, slots_ref, picks_ref, clean_ref, cand_ref, len_ref, raw_ref, sems
):
    rows = cand_ref.shape[0]
    shards = slots_ref.shape[0]
    groups = p_hbm.shape[0] // GROUP

    def fetch(g):
        part = pl.ds(g * GROUP, GROUP)
        return pltpu.make_async_copy(p_hbm.at[part], raw_ref.at[part], sems.at[g])

    fetch_cand = pltpu.make_async_copy(cand_hbm, cand_ref, sems.at[groups])
    fetch_len = pltpu.make_async_copy(len_hbm, len_ref, sems.at[groups + 1])
    fetch_cand.start()
    fetch_len.start()
    for g in range(groups):
        fetch(g).start()

    fetch_cand.wait()
    cand = cand_ref[...]
    owner = cand // QBD
    block = cand - owner * QBD
    lane = lax.broadcasted_iota(jnp.int32, (rows, LANES), 1).astype(jnp.float32)
    sub = lax.broadcasted_iota(jnp.int32, (rows, LANES), 0)
    for o in range(shards):
        mine = owner == o
        named = jnp.max(jnp.where(mine, block, 0), axis=1, keepdims=True)
        picks_ref[o:o + 1, :] = jnp.broadcast_to(jnp.max(named, axis=0, keepdims=True), (1, LANES))
        named_here = jnp.sum(jnp.where(mine, 1.0, 0.0), axis=1, keepdims=True)
        upto = jnp.broadcast_to(named_here, (rows, LANES))
        step = 1
        while step < rows:
            upto = upto + jnp.where(sub >= step, pltpu.roll(upto, step, 0), 0.0)
            step *= 2
        slots_ref[o:o + 1, :] = jnp.sum(jnp.where(upto <= lane, 1.0, 0.0), axis=0, keepdims=True)

    fetch_len.wait()
    u = lax.broadcasted_iota(jnp.int32, (PT, LANES), 0)

    @pl.loop(0, groups)
    def _(g):
        fetch(g).wait()
        for i in range(GROUP):
            p = g * GROUP + i
            tokens = raw_ref[p].astype(jnp.float32)
            clean_ref[p] = jnp.where(u < len_ref[p], tokens, tokens[0:1]).astype(jnp.bfloat16)


def prepare(shards, candidates, lengths, passages):
    hbm = pl.BlockSpec(memory_space=pltpu.HBM)
    vmem = pl.BlockSpec(memory_space=pltpu.VMEM)
    operands = [pltpu.with_memory_space_constraint(x, pltpu.HBM) for x in (candidates, lengths, passages)]
    return pl.pallas_call(
        prepare_kernel,
        out_shape=[
            jax.ShapeDtypeStruct((shards, LANES), jnp.float32),
            jax.ShapeDtypeStruct((shards, LANES), jnp.int32),
            jax.ShapeDtypeStruct(passages.shape, passages.dtype),
        ],
        in_specs=[hbm] * 3,
        out_specs=[vmem] * 3,
        scratch_shapes=[
            pltpu.VMEM(candidates.shape, candidates.dtype),
            pltpu.SMEM(lengths.shape, lengths.dtype),
            pltpu.VMEM(passages.shape, passages.dtype),
            pltpu.SemaphoreType.DMA((passages.shape[0] // GROUP + 2,)),
        ],
        compiler_params=pltpu.CompilerParams(vmem_limit_bytes=24 * 1024 * 1024),
        cost_estimate=pl.CostEstimate(flops=passages.size, bytes_accessed=2 * passages.size, transcendentals=0),
    )(*operands)


def picked(picks_ref, owner, q_ref):
    pick = jnp.max(picks_ref[pl.ds(owner, 1), :])
    return q_ref[pl.ds(pick * QB * QT, QB * QT), :]


def pack_kernel(partners, cand_ref, *refs):
    q_refs, out_ref = refs[:-1], refs[-1]
    me = lax.axis_index("psg")
    cand = cand_ref[...]
    owner = cand // QBD
    block = cand - owner * QBD
    for n, k in enumerate(partners):
        pick = jnp.max(jnp.where(owner == me ^ k, block, 0))
        out_ref[n * QB * QT:(n + 1) * QB * QT, :] = q_refs[n][pl.ds(pick * QB * QT, QB * QT), :]


def pack(partners, candidates, blocks):
    vmem = pl.BlockSpec(memory_space=pltpu.VMEM)
    return pl.pallas_call(
        functools.partial(pack_kernel, partners),
        out_shape=jax.ShapeDtypeStruct((len(partners) * QB * QT, DIM), blocks[0].dtype),
        in_specs=[vmem] * (1 + len(blocks)),
        out_specs=vmem,
        compiler_params=pltpu.CompilerParams(vmem_limit_bytes=4 * 1024 * 1024),
    )(candidates, *blocks)


def score_picked(sel_ref, p_ref, max_ref):
    count = p_ref.shape[0]
    sel = sel_ref[...]
    tokens = sel.shape[0]
    piece = 2 * GROUP
    for g in range(0, count, piece):
        left = p_ref[g:g + piece].reshape(piece * PT, DIM)
        dots = lax.dot_general(left, sel, (((1,), (1,)), ((), ())), preferred_element_type=jnp.float32)
        max_ref[g:g + piece, :] = jnp.max(dots.reshape(piece, PT, tokens), axis=1)

    best = max_ref[...]
    high = best.astype(jnp.bfloat16)
    rest = best - high.astype(jnp.float32)
    mid = rest.astype(jnp.bfloat16)
    low = (rest - mid.astype(jnp.float32)).astype(jnp.bfloat16)
    query = lax.broadcasted_iota(jnp.int32, (tokens // QT, tokens), 0)
    token = lax.broadcasted_iota(jnp.int32, (tokens // QT, tokens), 1)
    ones = jnp.where(token // QT == query, 1.0, 0.0).astype(jnp.bfloat16)
    total = jnp.zeros((tokens // QT, count), jnp.float32)
    for part in (low, mid, high):
        total = total + lax.dot_general(ones, part, (((1,), (1,)), ((), ())), preferred_element_type=jnp.float32)
    return total * (1.0 / QT)


def score_kernel(partners, slots_ref, picks_ref, p_ref, *refs):
    q_refs, (out_ref, sel_ref, max_ref) = refs[:-3], refs[-3:]
    me = lax.axis_index("psg")
    for n, k in enumerate(partners):
        sel_ref[n * QB * QT:(n + 1) * QB * QT, :] = picked(picks_ref, me ^ k, q_refs[n])
    total = score_picked(sel_ref, p_ref, max_ref)
    for n, k in enumerate(partners):
        out_ref[n, 0:QB, :] = total[n * QB:(n + 1) * QB]
        out_ref[n, QB:QB + 1, :] = slots_ref[pl.ds(me ^ k, 1), :]


def score_far_kernel(partners, slots_ref, p_ref, sel_ref, out_ref, max_ref):
    me = lax.axis_index("psg")
    total = score_picked(sel_ref, p_ref, max_ref)
    for n, k in enumerate(partners):
        out_ref[n, 0:QB, :] = total[n * QB:(n + 1) * QB]
        out_ref[n, QB:QB + 1, :] = slots_ref[pl.ds(me ^ k, 1), :]


def all_kernel(slots_ref, picks_ref, p_ref, q_ref, out_ref, sel_ref, max_ref):
    some = q_ref.shape[0]
    for n in range(some):
        sel_ref[n * QB * QT:(n + 1) * QB * QT, :] = picked(picks_ref, n, q_ref.at[n])
    total = score_picked(sel_ref, p_ref, max_ref)
    for n in range(some):
        out_ref[n, 0:QB, :] = total[n * QB:(n + 1) * QB]
        out_ref[n, QB:QB + 1, :] = slots_ref[n:n + 1, :]


def score(kernel, tiles, some, selects, passages, *more):
    count = passages.shape[0]
    vmem = pl.BlockSpec(memory_space=pltpu.VMEM)
    return pl.pallas_call(
        kernel,
        out_shape=jax.ShapeDtypeStruct((tiles, QB + 1, LANES), jnp.float32),
        in_specs=[vmem] * len(more),
        out_specs=vmem,
        scratch_shapes=[pltpu.VMEM((some * QB * QT, DIM), jnp.bfloat16)] * selects + [
            pltpu.VMEM((count, some * QB * QT), jnp.float32),
        ],
        compiler_params=pltpu.CompilerParams(vmem_limit_bytes=32 * 1024 * 1024),
        cost_estimate=pl.CostEstimate(
            flops=2 * passages.size * some * QB * QT, bytes_accessed=2 * passages.size, transcendentals=0
        ),
    )(*more)


def join_kernel(partners, near_ref, theirs_ref, out_ref):
    plane = lax.axis_index("psg") >> 1
    for n, k in enumerate(partners):
        out_ref[plane ^ k >> 1, 0:QB + 1, :] = near_ref[n]
        out_ref[plane ^ k >> 1, QB + 1:2 * QB + 2, :] = theirs_ref[n]


def join(partners, near_tiles, their_tiles):
    vmem = pl.BlockSpec(memory_space=pltpu.VMEM)
    return pl.pallas_call(
        functools.partial(join_kernel, partners),
        out_shape=jax.ShapeDtypeStruct((len(partners), 2 * QB + 2, LANES), jnp.float32),
        in_specs=[vmem] * 2,
        out_specs=vmem,
        compiler_params=pltpu.CompilerParams(vmem_limit_bytes=4 * 1024 * 1024),
    )(near_tiles, their_tiles)


def place_kernel(paired, in_ref, out_ref):
    slots = out_ref.shape[-1]
    side = lax.axis_index("psg") & 1 if paired else 0
    m = lax.broadcasted_iota(jnp.int32, (PBS, LANES), 0)
    for j in range(out_ref.shape[0]):
        tile_ref = in_ref.at[j // 2, pl.ds(j % 2 * (QB + 1), QB + 1)] if paired else in_ref.at[j]
        row = tile_ref[QB:QB + 1, :].astype(jnp.int32)
        where = jnp.minimum(row * PBS, LANES - PBS) + m
        for i in range(QB):
            tile = jnp.broadcast_to(tile_ref[i:i + 1, :], (PBS, LANES))
            out_ref[j ^ side, i] = jnp.take_along_axis(tile, where, axis=1)[:, :slots]


def place(paired, tiles, shards, slots):
    vmem = pl.BlockSpec(memory_space=pltpu.VMEM)
    return pl.pallas_call(
        functools.partial(place_kernel, paired),
        out_shape=jax.ShapeDtypeStruct((shards, QB, PBS, slots), jnp.float32),
        in_specs=[vmem],
        out_specs=vmem,
        compiler_params=pltpu.CompilerParams(vmem_limit_bytes=8 * 1024 * 1024),
    )(tiles)


def by_partners(own, shards, slot_count, candidates, lengths, passages):
    def swap(x, k):
        return lax.ppermute(x, "psg", [(j, j ^ k) for j in range(shards)])

    near = list(range(0, shards, 2))
    theirs = swap(candidates, 1)
    queries = {0: own} | {k: swap(own, k) for k in near[1:]}
    slots, picks, clean = prepare(shards, candidates, lengths, passages)
    clean, *arrived = lax.optimization_barrier((clean, *[queries[k] for k in reversed(near[1:])]))
    blocks = [own, *reversed(arrived)]
    far = swap(pack(near, theirs, blocks), 1)
    far_tiles = score(
        functools.partial(score_far_kernel, [k + 1 for k in near]), len(near), len(near), 0, clean, slots, clean, far
    )
    theirs = swap(far_tiles, 1)
    *blocks, far_tiles = lax.optimization_barrier((*blocks, far_tiles))
    near_tiles = score(
        functools.partial(score_kernel, near), len(near), len(near), 1, clean, slots, picks, clean, *blocks
    )
    planes = [[j + side for j in near] for side in range(2)]
    tiles = lax.all_to_all(
        join(near, near_tiles, theirs), "psg", split_axis=0, concat_axis=0, tiled=True, axis_index_groups=planes
    )
    return place(True, tiles, shards, slot_count)


def by_gather(own, shards, slot_count, candidates, lengths, passages):
    slots, picks, clean = prepare(shards, candidates, lengths, passages)
    gathered = lax.all_gather(own, "psg", axis=0)
    some = min(shards, 8)

    def score_some(items):
        return score(all_kernel, some, some, 1, clean, items[0], items[1], clean, items[2])

    parts = [x.reshape(shards // some, some, *x.shape[1:]) for x in (slots, picks, gathered)]
    tiles = lax.map(score_some, parts).reshape(shards, QB + 1, LANES)
    tiles = lax.all_to_all(tiles, "psg", split_axis=0, concat_axis=0, tiled=True)
    return place(False, tiles, shards, slot_count)


def per_device(queries, passages, lengths, candidates):
    shards = lax.axis_size("psg")
    rows = passages.shape[0] // PBS
    form = by_partners if shards == 8 else by_gather
    placed = form(
        queries.reshape(QBD * QB * QT, DIM), shards, rows * KB // shards,
        candidates.reshape(rows, KB), lengths, passages,
    )
    return placed.transpose(0, 3, 1, 2)[None]


def solution(mesh):
    return jax.shard_map(
        per_device,
        mesh=mesh,
        in_specs=(
            P(("grp", "psg", "qry"), None, None),
            P(("grp", "psg"), None, None),
            P(("grp", "psg")),
            P("qry", ("grp", "psg"), None),
        ),
        out_specs=P(("grp", "psg", "qry"), None, None, None, None),
        check_vma=False,
    )
```

```python
import functools

import jax
import jax.numpy as jnp
from jax import lax
from jax.experimental import pallas as pl
from jax.experimental.pallas import tpu as pltpu
from jax.sharding import PartitionSpec as P

DIM = 128
QT = 32
PT = 64
QB = 2
QBD = 4
PBS = 16
KB = 32
LANES = 128
GROUP = 8


def prepare_kernel(
    cand_hbm, len_hbm, p_hbm, slots_ref, picks_ref, clean_ref, cand_ref, len_ref, raw_ref, sems
):
    rows = cand_ref.shape[0]
    shards = slots_ref.shape[0]
    groups = p_hbm.shape[0] // GROUP

    def fetch(g):
        part = pl.ds(g * GROUP, GROUP)
        return pltpu.make_async_copy(p_hbm.at[part], raw_ref.at[part], sems.at[g])

    fetch_cand = pltpu.make_async_copy(cand_hbm, cand_ref, sems.at[groups])
    fetch_len = pltpu.make_async_copy(len_hbm, len_ref, sems.at[groups + 1])
    fetch_cand.start()
    fetch_len.start()
    for g in range(groups):
        fetch(g).start()

    fetch_cand.wait()
    cand = cand_ref[...]
    owner = cand // QBD
    block = cand - owner * QBD
    lane = lax.broadcasted_iota(jnp.int32, (rows, LANES), 1).astype(jnp.float32)
    sub = lax.broadcasted_iota(jnp.int32, (rows, LANES), 0)
    for o in range(shards):
        mine = owner == o
        named = jnp.max(jnp.where(mine, block, 0), axis=1, keepdims=True)
        picks_ref[o:o + 1, :] = jnp.broadcast_to(jnp.max(named, axis=0, keepdims=True), (1, LANES))
        named_here = jnp.sum(jnp.where(mine, 1.0, 0.0), axis=1, keepdims=True)
        upto = jnp.broadcast_to(named_here, (rows, LANES))
        step = 1
        while step < rows:
            upto = upto + jnp.where(sub >= step, pltpu.roll(upto, step, 0), 0.0)
            step *= 2
        slots_ref[o:o + 1, :] = jnp.sum(jnp.where(upto <= lane, 1.0, 0.0), axis=0, keepdims=True)

    fetch_len.wait()
    u = lax.broadcasted_iota(jnp.int32, (PT, LANES), 0)

    @pl.loop(0, groups)
    def _(g):
        fetch(g).wait()
        for i in range(GROUP):
            p = g * GROUP + i
            tokens = raw_ref[p].astype(jnp.float32)
            clean_ref[p] = jnp.where(u < len_ref[p], tokens, tokens[0:1]).astype(jnp.bfloat16)


def prepare(shards, candidates, lengths, passages):
    hbm = pl.BlockSpec(memory_space=pltpu.HBM)
    vmem = pl.BlockSpec(memory_space=pltpu.VMEM)
    operands = [pltpu.with_memory_space_constraint(x, pltpu.HBM) for x in (candidates, lengths, passages)]
    return pl.pallas_call(
        prepare_kernel,
        out_shape=[
            jax.ShapeDtypeStruct((shards, LANES), jnp.float32),
            jax.ShapeDtypeStruct((shards, LANES), jnp.int32),
            jax.ShapeDtypeStruct(passages.shape, passages.dtype),
        ],
        in_specs=[hbm] * 3,
        out_specs=[vmem] * 3,
        scratch_shapes=[
            pltpu.VMEM(candidates.shape, candidates.dtype),
            pltpu.SMEM(lengths.shape, lengths.dtype),
            pltpu.VMEM(passages.shape, passages.dtype),
            pltpu.SemaphoreType.DMA((passages.shape[0] // GROUP + 2,)),
        ],
        compiler_params=pltpu.CompilerParams(vmem_limit_bytes=24 * 1024 * 1024),
        cost_estimate=pl.CostEstimate(flops=passages.size, bytes_accessed=2 * passages.size, transcendentals=0),
    )(*operands)


def near_owner(me, step, planes):
    return lax.rem((me >> 1) + planes - step, planes) << 1 | me & 1


def picked(picks_ref, owner, q_ref):
    pick = jnp.max(picks_ref[pl.ds(owner, 1), :])
    return q_ref[pl.ds(pick * QB * QT, QB * QT), :]


def pack_kernel(cand_ref, *refs):
    q_refs, out_ref = refs[:-1], refs[-1]
    me = lax.axis_index("psg")
    planes = len(q_refs)
    cand = cand_ref[...]
    owner = cand // QBD
    block = cand - owner * QBD
    for n in range(planes):
        pick = jnp.max(jnp.where(owner == near_owner(me, n, planes), block, 0))
        out_ref[n * QB * QT:(n + 1) * QB * QT, :] = q_refs[n][pl.ds(pick * QB * QT, QB * QT), :]


def pack(candidates, blocks):
    vmem = pl.BlockSpec(memory_space=pltpu.VMEM)
    return pl.pallas_call(
        pack_kernel,
        out_shape=jax.ShapeDtypeStruct((len(blocks) * QB * QT, DIM), blocks[0].dtype),
        in_specs=[vmem] * (1 + len(blocks)),
        out_specs=vmem,
        compiler_params=pltpu.CompilerParams(vmem_limit_bytes=4 * 1024 * 1024),
    )(candidates, *blocks)


def score_picked(sel_ref, p_ref, max_ref):
    count = p_ref.shape[0]
    sel = sel_ref[...]
    tokens = sel.shape[0]
    piece = 2 * GROUP
    for g in range(0, count, piece):
        left = p_ref[g:g + piece].reshape(piece * PT, DIM)
        dots = lax.dot_general(left, sel, (((1,), (1,)), ((), ())), preferred_element_type=jnp.float32)
        max_ref[g:g + piece, :] = jnp.max(dots.reshape(piece, PT, tokens), axis=1)

    best = max_ref[...]
    high = best.astype(jnp.bfloat16)
    rest = best - high.astype(jnp.float32)
    mid = rest.astype(jnp.bfloat16)
    low = (rest - mid.astype(jnp.float32)).astype(jnp.bfloat16)
    parts = jnp.concatenate([low, mid, high], axis=1)
    query = lax.broadcasted_iota(jnp.int32, (tokens // QT, tokens), 0)
    token = lax.broadcasted_iota(jnp.int32, (tokens // QT, tokens), 1)
    ones = jnp.where(token // QT == query, 1.0, 0.0).astype(jnp.bfloat16)
    total = lax.dot_general(
        jnp.concatenate([ones] * 3, axis=1), parts, (((1,), (1,)), ((), ())), preferred_element_type=jnp.float32
    )
    return total * (1.0 / QT)


def near_kernel(slots_ref, picks_ref, p_ref, *refs):
    q_refs, (out_ref, sel_ref, max_ref) = refs[:-3], refs[-3:]
    me = lax.axis_index("psg")
    owners = [near_owner(me, n, len(q_refs)) for n in range(len(q_refs))]
    for n, owner in enumerate(owners):
        sel_ref[n * QB * QT:(n + 1) * QB * QT, :] = picked(picks_ref, owner, q_refs[n])
    total = score_picked(sel_ref, p_ref, max_ref)
    for n, owner in enumerate(owners):
        out_ref[n, 0:QB, :] = total[n * QB:(n + 1) * QB]
        out_ref[n, QB:QB + 1, :] = slots_ref[pl.ds(owner, 1), :]


def far_kernel(slots_ref, p_ref, sel_ref, earlier_ref, out_ref, max_ref):
    me = lax.axis_index("psg")
    planes = earlier_ref.shape[0]
    total = score_picked(sel_ref, p_ref, max_ref)
    for n in range(planes):
        owner = near_owner(me, n, planes)
        out_ref[owner] = earlier_ref[n]
        out_ref[owner ^ 1, 0:QB, :] = total[n * QB:(n + 1) * QB]
        out_ref[owner ^ 1, QB:QB + 1, :] = slots_ref[pl.ds(owner ^ 1, 1), :]


def all_kernel(slots_ref, picks_ref, p_ref, q_ref, out_ref, sel_ref, max_ref):
    some = q_ref.shape[0]
    for n in range(some):
        sel_ref[n * QB * QT:(n + 1) * QB * QT, :] = picked(picks_ref, n, q_ref.at[n])
    total = score_picked(sel_ref, p_ref, max_ref)
    for n in range(some):
        out_ref[n, 0:QB, :] = total[n * QB:(n + 1) * QB]
        out_ref[n, QB:QB + 1, :] = slots_ref[n:n + 1, :]


def score(kernel, tiles, some, selects, passages, *more):
    count = passages.shape[0]
    vmem = pl.BlockSpec(memory_space=pltpu.VMEM)
    return pl.pallas_call(
        kernel,
        out_shape=jax.ShapeDtypeStruct((tiles, QB + 1, LANES), jnp.float32),
        in_specs=[vmem] * len(more),
        out_specs=vmem,
        scratch_shapes=[pltpu.VMEM((some * QB * QT, DIM), jnp.bfloat16)] * selects + [
            pltpu.VMEM((count, some * QB * QT), jnp.float32),
        ],
        compiler_params=pltpu.CompilerParams(vmem_limit_bytes=32 * 1024 * 1024),
        cost_estimate=pl.CostEstimate(
            flops=2 * passages.size * some * QB * QT, bytes_accessed=2 * passages.size, transcendentals=0
        ),
    )(*more)


def place_kernel(in_ref, out_hbm, placed_ref, sems):
    shards, _, _, slots = placed_ref.shape
    m = lax.broadcasted_iota(jnp.int32, (PBS, LANES), 0)

    def send(j):
        return pltpu.make_async_copy(placed_ref.at[j], out_hbm.at[j], sems.at[j])

    for j in range(shards):
        row = in_ref[j, QB:QB + 1, :].astype(jnp.int32)
        where = jnp.minimum(row * PBS, LANES - PBS) + m
        for i in range(QB):
            tile = jnp.broadcast_to(in_ref[j, i:i + 1, :], (PBS, LANES))
            placed_ref[j, i] = jnp.take_along_axis(tile, where, axis=1)[:, :slots]
        send(j).start()
    for j in range(shards):
        send(j).wait()


def place(tiles, slots):
    shape = (tiles.shape[0], QB, PBS, slots)
    return pl.pallas_call(
        place_kernel,
        out_shape=jax.ShapeDtypeStruct(shape, jnp.float32),
        in_specs=[pl.BlockSpec(memory_space=pltpu.VMEM)],
        out_specs=pl.BlockSpec(memory_space=pltpu.HBM),
        scratch_shapes=[pltpu.VMEM(shape, jnp.float32), pltpu.SemaphoreType.DMA((shape[0],))],
        compiler_params=pltpu.CompilerParams(vmem_limit_bytes=16 * 1024 * 1024),
    )(tiles)


def by_planes(own, shards, candidates, lengths, passages):
    planes = shards // 2

    def swap_sides(x):
        return lax.ppermute(x, "psg", [(j, j ^ 1) for j in range(shards)])

    def shift(x, step):
        return lax.ppermute(x, "psg", [(j, (j + 2 * step) % shards) for j in range(shards)])

    theirs = swap_sides(candidates)
    shifted = [shift(own, step) for step in range(1, planes)]
    slots, picks, clean = prepare(shards, candidates, lengths, passages)
    clean, *shifted = lax.optimization_barrier((clean, *reversed(shifted)))
    blocks = [own, *reversed(shifted)]
    far = swap_sides(pack(theirs, blocks))
    tiles = score(near_kernel, planes, planes, 1, clean, slots, picks, clean, *blocks)
    far, tiles = lax.optimization_barrier((far, tiles))
    return score(far_kernel, shards, planes, 0, clean, slots, clean, far, tiles)


def by_gather(own, shards, candidates, lengths, passages):
    slots, picks, clean = prepare(shards, candidates, lengths, passages)
    gathered = lax.all_gather(own, "psg", axis=0)
    some = min(shards, 8)

    def score_some(items):
        return score(all_kernel, some, some, 1, clean, items[0], items[1], clean, items[2])

    parts = [x.reshape(shards // some, some, *x.shape[1:]) for x in (slots, picks, gathered)]
    return lax.map(score_some, parts).reshape(shards, QB + 1, LANES)


def per_device(queries, passages, lengths, candidates):
    shards = lax.axis_size("psg")
    rows = passages.shape[0] // PBS
    form = by_planes if shards in (4, 8) else by_gather
    tiles = form(
        queries.reshape(QBD * QB * QT, DIM), shards, candidates.reshape(rows, KB), lengths, passages
    )
    tiles = lax.all_to_all(tiles, "psg", split_axis=0, concat_axis=0, tiled=True)
    return place(tiles, rows * KB // shards).transpose(0, 3, 1, 2)[None]


def solution(mesh):
    return jax.shard_map(
        per_device,
        mesh=mesh,
        in_specs=(
            P(("grp", "psg", "qry"), None, None),
            P(("grp", "psg"), None, None),
            P(("grp", "psg")),
            P("qry", ("grp", "psg"), None),
        ),
        out_specs=P(("grp", "psg", "qry"), None, None, None, None),
        check_vma=False,
    )
```

```python
import functools

import jax
import jax.numpy as jnp
from jax import lax
from jax.experimental import pallas as pl
from jax.experimental.pallas import tpu as pltpu
from jax.sharding import PartitionSpec as P

DIM = 128
QT = 32
PT = 64
QB = 2
QBD = 4
PBS = 16
KB = 32
LANES = 128
GROUP = 8


def prepare_kernel(
    cand_hbm, len_hbm, p_hbm, slots_ref, picks_ref, clean_ref, cand_ref, len_ref, raw_ref, sems
):
    rows = cand_ref.shape[0]
    shards = slots_ref.shape[0]
    groups = p_hbm.shape[0] // GROUP

    def fetch(g):
        part = pl.ds(g * GROUP, GROUP)
        return pltpu.make_async_copy(p_hbm.at[part], raw_ref.at[part], sems.at[g])

    fetch_cand = pltpu.make_async_copy(cand_hbm, cand_ref, sems.at[groups])
    fetch_len = pltpu.make_async_copy(len_hbm, len_ref, sems.at[groups + 1])
    fetch_cand.start()
    fetch_len.start()
    for g in range(groups):
        fetch(g).start()

    fetch_cand.wait()
    cand = cand_ref[...]
    owner = cand // QBD
    block = cand - owner * QBD
    lane = lax.broadcasted_iota(jnp.int32, (rows, LANES), 1).astype(jnp.float32)
    sub = lax.broadcasted_iota(jnp.int32, (rows, LANES), 0)
    for o in range(shards):
        mine = owner == o
        named = jnp.max(jnp.where(mine, block, 0), axis=1, keepdims=True)
        picks_ref[o:o + 1, :] = jnp.broadcast_to(jnp.max(named, axis=0, keepdims=True), (1, LANES))
        named_here = jnp.sum(jnp.where(mine, 1.0, 0.0), axis=1, keepdims=True)
        upto = jnp.broadcast_to(named_here, (rows, LANES))
        step = 1
        while step < rows:
            upto = upto + jnp.where(sub >= step, pltpu.roll(upto, step, 0), 0.0)
            step *= 2
        slots_ref[o:o + 1, :] = jnp.sum(jnp.where(upto <= lane, 1.0, 0.0), axis=0, keepdims=True)

    fetch_len.wait()
    u = lax.broadcasted_iota(jnp.int32, (PT, LANES), 0)

    @pl.loop(0, groups)
    def _(g):
        fetch(g).wait()
        for i in range(GROUP):
            p = g * GROUP + i
            tokens = raw_ref[p].astype(jnp.float32)
            clean_ref[p] = jnp.where(u < len_ref[p], tokens, tokens[0:1]).astype(jnp.bfloat16)


def prepare(shards, candidates, lengths, passages):
    hbm = pl.BlockSpec(memory_space=pltpu.HBM)
    vmem = pl.BlockSpec(memory_space=pltpu.VMEM)
    operands = [pltpu.with_memory_space_constraint(x, pltpu.HBM) for x in (candidates, lengths, passages)]
    return pl.pallas_call(
        prepare_kernel,
        out_shape=[
            jax.ShapeDtypeStruct((shards, LANES), jnp.float32),
            jax.ShapeDtypeStruct((shards, LANES), jnp.int32),
            jax.ShapeDtypeStruct(passages.shape, passages.dtype),
        ],
        in_specs=[hbm] * 3,
        out_specs=[vmem] * 3,
        scratch_shapes=[
            pltpu.VMEM(candidates.shape, candidates.dtype),
            pltpu.SMEM(lengths.shape, lengths.dtype),
            pltpu.VMEM(passages.shape, passages.dtype),
            pltpu.SemaphoreType.DMA((passages.shape[0] // GROUP + 2,)),
        ],
        compiler_params=pltpu.CompilerParams(vmem_limit_bytes=24 * 1024 * 1024),
        cost_estimate=pl.CostEstimate(flops=passages.size, bytes_accessed=2 * passages.size, transcendentals=0),
    )(*operands)


def near_owner(me, step, planes):
    return lax.rem((me >> 1) + planes - step, planes) << 1 | me & 1


def picked(picks_ref, owner, q_ref):
    pick = jnp.max(picks_ref[pl.ds(owner, 1), :])
    return q_ref[pl.ds(pick * QB * QT, QB * QT), :]


def pack_kernel(cand_ref, *refs):
    q_refs, out_ref = refs[:-1], refs[-1]
    me = lax.axis_index("psg")
    planes = len(q_refs)
    cand = cand_ref[...]
    owner = cand // QBD
    block = cand - owner * QBD
    for n in range(planes):
        pick = jnp.max(jnp.where(owner == near_owner(me, n, planes), block, 0))
        out_ref[n * QB * QT:(n + 1) * QB * QT, :] = q_refs[n][pl.ds(pick * QB * QT, QB * QT), :]


def pack(candidates, blocks):
    vmem = pl.BlockSpec(memory_space=pltpu.VMEM)
    return pl.pallas_call(
        pack_kernel,
        out_shape=jax.ShapeDtypeStruct((len(blocks) * QB * QT, DIM), blocks[0].dtype),
        in_specs=[vmem] * (1 + len(blocks)),
        out_specs=vmem,
        compiler_params=pltpu.CompilerParams(vmem_limit_bytes=4 * 1024 * 1024),
    )(candidates, *blocks)


def score_picked(sel_ref, p_ref, max_ref):
    count = p_ref.shape[0]
    sel = sel_ref[...]
    tokens = sel.shape[0]
    piece = 2 * GROUP
    for g in range(0, count, piece):
        left = p_ref[g:g + piece].reshape(piece * PT, DIM)
        dots = lax.dot_general(left, sel, (((1,), (1,)), ((), ())), preferred_element_type=jnp.float32)
        max_ref[g:g + piece, :] = jnp.max(dots.reshape(piece, PT, tokens), axis=1)

    best = max_ref[...]
    high = best.astype(jnp.bfloat16)
    rest = best - high.astype(jnp.float32)
    mid = rest.astype(jnp.bfloat16)
    low = (rest - mid.astype(jnp.float32)).astype(jnp.bfloat16)
    parts = jnp.concatenate([low, mid, high], axis=1)
    query = lax.broadcasted_iota(jnp.int32, (tokens // QT, tokens), 0)
    token = lax.broadcasted_iota(jnp.int32, (tokens // QT, tokens), 1)
    ones = jnp.where(token // QT == query, 1.0, 0.0).astype(jnp.bfloat16)
    total = lax.dot_general(
        jnp.concatenate([ones] * 3, axis=1), parts, (((1,), (1,)), ((), ())), preferred_element_type=jnp.float32
    )
    return total * (1.0 / QT)


def near_kernel(slots_ref, picks_ref, p_ref, *refs):
    q_refs, (out_ref, sel_ref, max_ref) = refs[:-3], refs[-3:]
    me = lax.axis_index("psg")
    owners = [near_owner(me, n, len(q_refs)) for n in range(len(q_refs))]
    for n, owner in enumerate(owners):
        sel_ref[n * QB * QT:(n + 1) * QB * QT, :] = picked(picks_ref, owner, q_refs[n])
    total = score_picked(sel_ref, p_ref, max_ref)
    for n, owner in enumerate(owners):
        out_ref[n, 0:QB, :] = total[n * QB:(n + 1) * QB]
        out_ref[n, QB:QB + 1, :] = slots_ref[pl.ds(owner, 1), :]


def far_kernel(slots_ref, p_ref, sel_ref, earlier_ref, out_ref, max_ref):
    me = lax.axis_index("psg")
    planes = earlier_ref.shape[0]
    total = score_picked(sel_ref, p_ref, max_ref)
    for n in range(planes):
        owner = near_owner(me, n, planes)
        out_ref[owner] = earlier_ref[n]
        out_ref[owner ^ 1, 0:QB, :] = total[n * QB:(n + 1) * QB]
        out_ref[owner ^ 1, QB:QB + 1, :] = slots_ref[pl.ds(owner ^ 1, 1), :]


def all_kernel(slots_ref, picks_ref, p_ref, q_ref, out_ref, sel_ref, max_ref):
    some = q_ref.shape[0]
    for n in range(some):
        sel_ref[n * QB * QT:(n + 1) * QB * QT, :] = picked(picks_ref, n, q_ref.at[n])
    total = score_picked(sel_ref, p_ref, max_ref)
    for n in range(some):
        out_ref[n, 0:QB, :] = total[n * QB:(n + 1) * QB]
        out_ref[n, QB:QB + 1, :] = slots_ref[n:n + 1, :]


def score(kernel, tiles, some, selects, passages, *more):
    count = passages.shape[0]
    vmem = pl.BlockSpec(memory_space=pltpu.VMEM)
    return pl.pallas_call(
        kernel,
        out_shape=jax.ShapeDtypeStruct((tiles, QB + 1, LANES), jnp.float32),
        in_specs=[vmem] * len(more),
        out_specs=vmem,
        scratch_shapes=[pltpu.VMEM((some * QB * QT, DIM), jnp.bfloat16)] * selects + [
            pltpu.VMEM((count, some * QB * QT), jnp.float32),
        ],
        compiler_params=pltpu.CompilerParams(vmem_limit_bytes=32 * 1024 * 1024),
        cost_estimate=pl.CostEstimate(
            flops=2 * passages.size * some * QB * QT, bytes_accessed=2 * passages.size, transcendentals=0
        ),
    )(*more)


def place_kernel(in_ref, out_ref):
    slots = out_ref.shape[-1]
    m = lax.broadcasted_iota(jnp.int32, (PBS, LANES), 0)
    for j in range(in_ref.shape[0]):
        row = in_ref[j, QB:QB + 1, :].astype(jnp.int32)
        where = jnp.minimum(row * PBS, LANES - PBS) + m
        for i in range(QB):
            tile = jnp.broadcast_to(in_ref[j, i:i + 1, :], (PBS, LANES))
            out_ref[j, i] = jnp.take_along_axis(tile, where, axis=1)[:, :slots]


def place(tiles, slots):
    vmem = pl.BlockSpec(memory_space=pltpu.VMEM)
    shards = tiles.shape[0]
    return pl.pallas_call(
        place_kernel,
        out_shape=jax.ShapeDtypeStruct((shards, QB, PBS, slots), jnp.float32),
        in_specs=[vmem],
        out_specs=vmem,
        compiler_params=pltpu.CompilerParams(vmem_limit_bytes=8 * 1024 * 1024),
    )(tiles)


def by_planes(own, shards, candidates, lengths, passages):
    planes = shards // 2

    def swap_sides(x):
        return lax.ppermute(x, "psg", [(j, j ^ 1) for j in range(shards)])

    def shift(x, step):
        return lax.ppermute(x, "psg", [(j, (j + 2 * step) % shards) for j in range(shards)])

    theirs = swap_sides(candidates)
    shifted = [shift(own, step) for step in range(1, planes)]
    slots, picks, clean = prepare(shards, candidates, lengths, passages)
    clean, *shifted = lax.optimization_barrier((clean, *shifted))
    blocks = [own, *shifted]
    far = swap_sides(pack(theirs, blocks))
    tiles = score(near_kernel, planes, planes, 1, clean, slots, picks, clean, *blocks)
    far, tiles = lax.optimization_barrier((far, tiles))
    return score(far_kernel, shards, planes, 0, clean, slots, clean, far, tiles)


def by_gather(own, shards, candidates, lengths, passages):
    slots, picks, clean = prepare(shards, candidates, lengths, passages)
    gathered = lax.all_gather(own, "psg", axis=0)
    some = min(shards, 8)

    def score_some(items):
        return score(all_kernel, some, some, 1, clean, items[0], items[1], clean, items[2])

    parts = [x.reshape(shards // some, some, *x.shape[1:]) for x in (slots, picks, gathered)]
    return lax.map(score_some, parts).reshape(shards, QB + 1, LANES)


def per_device(queries, passages, lengths, candidates):
    shards = lax.axis_size("psg")
    rows = passages.shape[0] // PBS
    form = by_planes if shards in (4, 8) else by_gather
    tiles = form(
        queries.reshape(QBD * QB * QT, DIM), shards, candidates.reshape(rows, KB), lengths, passages
    )
    tiles = lax.all_to_all(tiles, "psg", split_axis=0, concat_axis=0, tiled=True)
    return place(tiles, rows * KB // shards).transpose(0, 3, 1, 2)[None]


def solution(mesh):
    return jax.shard_map(
        per_device,
        mesh=mesh,
        in_specs=(
            P(("grp", "psg", "qry"), None, None),
            P(("grp", "psg"), None, None),
            P(("grp", "psg")),
            P("qry", ("grp", "psg"), None),
        ),
        out_specs=P(("grp", "psg", "qry"), None, None, None, None),
        check_vma=False,
    )
```

```python
import functools

import jax
import jax.numpy as jnp
from jax import lax
from jax.experimental import pallas as pl
from jax.experimental.pallas import tpu as pltpu
from jax.sharding import PartitionSpec as P

DIM = 128
QT = 32
PT = 64
QB = 2
QBD = 4
PBS = 16
KB = 32
LANES = 128
GROUP = 8


def prepare_kernel(
    cand_hbm, len_hbm, p_hbm, slots_ref, picks_ref, clean_ref, cand_ref, len_ref, raw_ref, sems
):
    rows = cand_ref.shape[0]
    shards = slots_ref.shape[0]
    groups = p_hbm.shape[0] // GROUP

    def fetch(g):
        part = pl.ds(g * GROUP, GROUP)
        return pltpu.make_async_copy(p_hbm.at[part], raw_ref.at[part], sems.at[g])

    fetch_cand = pltpu.make_async_copy(cand_hbm, cand_ref, sems.at[groups])
    fetch_len = pltpu.make_async_copy(len_hbm, len_ref, sems.at[groups + 1])
    fetch_cand.start()
    fetch_len.start()
    for g in range(groups):
        fetch(g).start()

    fetch_cand.wait()
    cand = cand_ref[...]
    owner = cand // QBD
    block = cand - owner * QBD
    lane = lax.broadcasted_iota(jnp.int32, (rows, LANES), 1).astype(jnp.float32)
    sub = lax.broadcasted_iota(jnp.int32, (rows, LANES), 0)
    for o in range(shards):
        mine = owner == o
        named = jnp.max(jnp.where(mine, block, 0), axis=1, keepdims=True)
        picks_ref[o:o + 1, :] = jnp.broadcast_to(jnp.max(named, axis=0, keepdims=True), (1, LANES))
        named_here = jnp.sum(jnp.where(mine, 1.0, 0.0), axis=1, keepdims=True)
        upto = jnp.broadcast_to(named_here, (rows, LANES))
        step = 1
        while step < rows:
            upto = upto + jnp.where(sub >= step, pltpu.roll(upto, step, 0), 0.0)
            step *= 2
        slots_ref[o:o + 1, :] = jnp.sum(jnp.where(upto <= lane, 1.0, 0.0), axis=0, keepdims=True)

    fetch_len.wait()
    u = lax.broadcasted_iota(jnp.int32, (PT, LANES), 0)

    @pl.loop(0, groups)
    def _(g):
        fetch(g).wait()
        for i in range(GROUP):
            p = g * GROUP + i
            tokens = raw_ref[p].astype(jnp.float32)
            clean_ref[p] = jnp.where(u < len_ref[p], tokens, tokens[0:1]).astype(jnp.bfloat16)


def prepare(shards, candidates, lengths, passages):
    hbm = pl.BlockSpec(memory_space=pltpu.HBM)
    vmem = pl.BlockSpec(memory_space=pltpu.VMEM)
    operands = [pltpu.with_memory_space_constraint(x, pltpu.HBM) for x in (candidates, lengths, passages)]
    return pl.pallas_call(
        prepare_kernel,
        out_shape=[
            jax.ShapeDtypeStruct((shards, LANES), jnp.float32),
            jax.ShapeDtypeStruct((shards, LANES), jnp.int32),
            jax.ShapeDtypeStruct(passages.shape, passages.dtype),
        ],
        in_specs=[hbm] * 3,
        out_specs=[vmem] * 3,
        scratch_shapes=[
            pltpu.VMEM(candidates.shape, candidates.dtype),
            pltpu.SMEM(lengths.shape, lengths.dtype),
            pltpu.VMEM(passages.shape, passages.dtype),
            pltpu.SemaphoreType.DMA((passages.shape[0] // GROUP + 2,)),
        ],
        compiler_params=pltpu.CompilerParams(vmem_limit_bytes=24 * 1024 * 1024),
        cost_estimate=pl.CostEstimate(flops=passages.size, bytes_accessed=2 * passages.size, transcendentals=0),
    )(*operands)


def near_owner(me, step, planes):
    return lax.rem((me >> 1) + planes - step, planes) << 1 | me & 1


def picked(picks_ref, owner, q_ref):
    pick = jnp.max(picks_ref[pl.ds(owner, 1), :])
    return q_ref[pl.ds(pick * QB * QT, QB * QT), :]


def pack_kernel(steps, planes, cand_ref, *refs):
    q_refs, out_ref = refs[:-1], refs[-1]
    me = lax.axis_index("psg")
    cand = cand_ref[...]
    owner = cand // QBD
    block = cand - owner * QBD
    for n, step in enumerate(steps):
        pick = jnp.max(jnp.where(owner == near_owner(me, step, planes), block, 0))
        out_ref[n * QB * QT:(n + 1) * QB * QT, :] = q_refs[n][pl.ds(pick * QB * QT, QB * QT), :]


def pack(steps, planes, candidates, blocks):
    vmem = pl.BlockSpec(memory_space=pltpu.VMEM)
    return pl.pallas_call(
        functools.partial(pack_kernel, steps, planes),
        out_shape=jax.ShapeDtypeStruct((len(blocks) * QB * QT, DIM), blocks[0].dtype),
        in_specs=[vmem] * (1 + len(blocks)),
        out_specs=vmem,
        compiler_params=pltpu.CompilerParams(vmem_limit_bytes=4 * 1024 * 1024),
    )(candidates, *blocks)


def sum_tokens(best):
    tokens = best.shape[1]
    high = best.astype(jnp.bfloat16)
    rest = best - high.astype(jnp.float32)
    mid = rest.astype(jnp.bfloat16)
    low = (rest - mid.astype(jnp.float32)).astype(jnp.bfloat16)
    parts = jnp.concatenate([low, mid, high], axis=1)
    query = lax.broadcasted_iota(jnp.int32, (tokens // QT, tokens), 0)
    token = lax.broadcasted_iota(jnp.int32, (tokens // QT, tokens), 1)
    ones = jnp.where(token // QT == query, 1.0, 0.0).astype(jnp.bfloat16)
    total = lax.dot_general(
        jnp.concatenate([ones] * 3, axis=1), parts, (((1,), (1,)), ((), ())), preferred_element_type=jnp.float32
    )
    return total * (1.0 / QT)


def best_tokens(left_of, sel, max_ref):
    count, tokens = max_ref.shape
    piece = 2 * GROUP
    for g in range(0, count, piece):
        dots = lax.dot_general(left_of(g, piece), sel, (((1,), (1,)), ((), ())), preferred_element_type=jnp.float32)
        max_ref[g:g + piece, :] = jnp.max(dots.reshape(piece, PT, tokens), axis=1)
    return max_ref[...]


def score_picked(sel, p_ref, max_ref):
    def left_of(g, piece):
        return p_ref[g:g + piece].reshape(piece * PT, DIM)

    return sum_tokens(best_tokens(left_of, sel, max_ref))


def score_picked_few(sel, p_ref, wide_ref, max_ref):
    tokens, half = sel.shape[0], p_ref.shape[0] // 2
    wide_ref[...] = jnp.zeros_like(wide_ref)
    wide_ref[0:tokens, 0:DIM] = sel
    wide_ref[tokens:, DIM:] = sel

    def left_of(g, piece):
        return jnp.concatenate(
            [p_ref[h + g:h + g + piece].reshape(piece * PT, DIM) for h in (0, half)], axis=1
        )

    best = best_tokens(left_of, wide_ref[...], max_ref)
    return jnp.concatenate([sum_tokens(best[:, :tokens]), sum_tokens(best[:, tokens:])], axis=1)


def put(out_ref, place, total, n, slots_ref, owner):
    out_ref[place, 0:QB, :] = total[n * QB:(n + 1) * QB]
    out_ref[place, QB:QB + 1, :] = slots_ref[pl.ds(owner, 1), :]


def near_kernel(slots_ref, picks_ref, p_ref, *refs):
    q_refs, (out_ref, sel_ref, max_ref) = refs[:-3], refs[-3:]
    me = lax.axis_index("psg")
    owners = [near_owner(me, n, len(q_refs)) for n in range(len(q_refs))]
    for n, owner in enumerate(owners):
        sel_ref[n * QB * QT:(n + 1) * QB * QT, :] = picked(picks_ref, owner, q_refs[n])
    total = score_picked(sel_ref[...], p_ref, max_ref)
    for n, owner in enumerate(owners):
        put(out_ref, n, total, n, slots_ref, owner)


def some_far_kernel(steps, planes, slots_ref, p_ref, sel_ref, out_ref, wide_ref, max_ref):
    me = lax.axis_index("psg")
    total = score_picked_few(sel_ref[...], p_ref, wide_ref, max_ref)
    for n, step in enumerate(steps):
        put(out_ref, n, total, n, slots_ref, near_owner(me, step, planes) ^ 1)


def last_far_kernel(steps, planes, slots_ref, p_ref, sel_ref, near_ref, far_ref, out_ref, wide_ref, max_ref):
    me = lax.axis_index("psg")
    total = score_picked_few(sel_ref[...], p_ref, wide_ref, max_ref)
    for n, step in enumerate(steps):
        owner = near_owner(me, step, planes) ^ 1
        put(out_ref, owner, total, n, slots_ref, owner)
    others = [step for step in range(planes) if step not in steps]
    for step in range(planes):
        out_ref[near_owner(me, step, planes)] = near_ref[step]
    for n, step in enumerate(others):
        out_ref[near_owner(me, step, planes) ^ 1] = far_ref[n]


def all_kernel(slots_ref, picks_ref, p_ref, q_ref, out_ref, sel_ref, max_ref):
    some = q_ref.shape[0]
    for n in range(some):
        sel_ref[n * QB * QT:(n + 1) * QB * QT, :] = picked(picks_ref, n, q_ref.at[n])
    total = score_picked(sel_ref[...], p_ref, max_ref)
    for n in range(some):
        put(out_ref, n, total, n, slots_ref, n)


def score(kernel, tiles, some, few, passages, *more):
    count, tokens = passages.shape[0], some * QB * QT
    vmem = pl.BlockSpec(memory_space=pltpu.VMEM)
    if few:
        scratch = [pltpu.VMEM((2 * tokens, 2 * DIM), jnp.bfloat16), pltpu.VMEM((count // 2, 2 * tokens), jnp.float32)]
    else:
        scratch = [pltpu.VMEM((tokens, DIM), jnp.bfloat16), pltpu.VMEM((count, tokens), jnp.float32)]
    return pl.pallas_call(
        kernel,
        out_shape=jax.ShapeDtypeStruct((tiles, QB + 1, LANES), jnp.float32),
        in_specs=[vmem] * len(more),
        out_specs=vmem,
        scratch_shapes=scratch,
        compiler_params=pltpu.CompilerParams(vmem_limit_bytes=32 * 1024 * 1024),
        cost_estimate=pl.CostEstimate(
            flops=2 * passages.size * tokens, bytes_accessed=2 * passages.size, transcendentals=0
        ),
    )(*more)


def place_kernel(in_ref, out_ref):
    slots = out_ref.shape[-1]
    m = lax.broadcasted_iota(jnp.int32, (PBS, LANES), 0)
    for j in range(in_ref.shape[0]):
        row = in_ref[j, QB:QB + 1, :].astype(jnp.int32)
        where = jnp.minimum(row * PBS, LANES - PBS) + m
        for i in range(QB):
            tile = jnp.broadcast_to(in_ref[j, i:i + 1, :], (PBS, LANES))
            out_ref[j, i] = jnp.take_along_axis(tile, where, axis=1)[:, :slots]


def place(tiles, slots):
    vmem = pl.BlockSpec(memory_space=pltpu.VMEM)
    shards = tiles.shape[0]
    return pl.pallas_call(
        place_kernel,
        out_shape=jax.ShapeDtypeStruct((shards, QB, PBS, slots), jnp.float32),
        in_specs=[vmem],
        out_specs=vmem,
        compiler_params=pltpu.CompilerParams(vmem_limit_bytes=8 * 1024 * 1024),
    )(tiles)


def by_planes(own, shards, candidates, lengths, passages):
    planes = shards // 2

    def swap_sides(x):
        return lax.ppermute(x, "psg", [(j, j ^ 1) for j in range(shards)])

    def shift(x, step):
        return lax.ppermute(x, "psg", [(j, (j + 2 * step) % shards) for j in range(shards)])

    theirs = swap_sides(candidates)
    shifted = [shift(own, step) for step in range(1, planes)]
    slots, picks, clean = prepare(shards, candidates, lengths, passages)
    clean, *early = lax.optimization_barrier((clean, *reversed(shifted[:planes // 2 - 1])))
    early, late = [own, *reversed(early)], shifted[planes // 2 - 1:]
    steps = list(range(planes))
    first, last = steps[:planes // 2], steps[planes // 2:]
    packed = pack(first, planes, theirs, early)
    first_far = swap_sides(packed)
    *late, _ = lax.optimization_barrier((*reversed(late), packed))
    late = late[::-1]
    last_far = swap_sides(pack(last, planes, theirs, late))
    near_tiles = score(near_kernel, planes, planes, False, clean, slots, picks, clean, *early, *late)
    first_far, near_tiles = lax.optimization_barrier((first_far, near_tiles))
    far_tiles = score(
        functools.partial(some_far_kernel, first, planes), len(first), len(first), True, clean, slots, clean, first_far
    )
    last_far, far_tiles = lax.optimization_barrier((last_far, far_tiles))
    return score(
        functools.partial(last_far_kernel, last, planes), shards, len(last), True, clean,
        slots, clean, last_far, near_tiles, far_tiles,
    )


def by_gather(own, shards, candidates, lengths, passages):
    slots, picks, clean = prepare(shards, candidates, lengths, passages)
    gathered = lax.all_gather(own, "psg", axis=0)
    some = min(shards, 8)

    def score_some(items):
        return score(all_kernel, some, some, False, clean, items[0], items[1], clean, items[2])

    parts = [x.reshape(shards // some, some, *x.shape[1:]) for x in (slots, picks, gathered)]
    return lax.map(score_some, parts).reshape(shards, QB + 1, LANES)


def per_device(queries, passages, lengths, candidates):
    shards = lax.axis_size("psg")
    rows = passages.shape[0] // PBS
    form = by_planes if shards == 8 else by_gather
    tiles = form(
        queries.reshape(QBD * QB * QT, DIM), shards, candidates.reshape(rows, KB), lengths, passages
    )
    tiles = lax.all_to_all(tiles, "psg", split_axis=0, concat_axis=0, tiled=True)
    return place(tiles, rows * KB // shards).transpose(0, 3, 1, 2)[None]


def solution(mesh):
    return jax.shard_map(
        per_device,
        mesh=mesh,
        in_specs=(
            P(("grp", "psg", "qry"), None, None),
            P(("grp", "psg"), None, None),
            P(("grp", "psg")),
            P("qry", ("grp", "psg"), None),
        ),
        out_specs=P(("grp", "psg", "qry"), None, None, None, None),
        check_vma=False,
    )
```

```python
import functools

import jax
import jax.numpy as jnp
from jax import lax
from jax.experimental import pallas as pl
from jax.experimental.pallas import tpu as pltpu
from jax.sharding import PartitionSpec as P

DIM = 128
QT = 32
PT = 64
QB = 2
QBD = 4
PBS = 16
KB = 32
LANES = 128
GROUP = 8


def prepare_kernel(
    cand_hbm, len_hbm, p_hbm, slots_ref, picks_ref, clean_ref, cand_ref, len_ref, raw_ref, sems
):
    rows = cand_ref.shape[0]
    shards = slots_ref.shape[0]
    groups = p_hbm.shape[0] // GROUP

    def fetch(g):
        part = pl.ds(g * GROUP, GROUP)
        return pltpu.make_async_copy(p_hbm.at[part], raw_ref.at[part], sems.at[g])

    fetch_cand = pltpu.make_async_copy(cand_hbm, cand_ref, sems.at[groups])
    fetch_len = pltpu.make_async_copy(len_hbm, len_ref, sems.at[groups + 1])
    fetch_cand.start()
    fetch_len.start()
    for g in range(groups):
        fetch(g).start()

    fetch_cand.wait()
    cand = cand_ref[...]
    owner = cand // QBD
    block = cand - owner * QBD
    lane = lax.broadcasted_iota(jnp.int32, (rows, LANES), 1).astype(jnp.float32)
    sub = lax.broadcasted_iota(jnp.int32, (rows, LANES), 0)
    for o in range(shards):
        mine = owner == o
        named = jnp.max(jnp.where(mine, block, 0), axis=1, keepdims=True)
        picks_ref[o:o + 1, :] = jnp.broadcast_to(jnp.max(named, axis=0, keepdims=True), (1, LANES))
        named_here = jnp.sum(jnp.where(mine, 1.0, 0.0), axis=1, keepdims=True)
        upto = jnp.broadcast_to(named_here, (rows, LANES))
        step = 1
        while step < rows:
            upto = upto + jnp.where(sub >= step, pltpu.roll(upto, step, 0), 0.0)
            step *= 2
        slots_ref[o:o + 1, :] = jnp.sum(jnp.where(upto <= lane, 1.0, 0.0), axis=0, keepdims=True)

    fetch_len.wait()
    u = lax.broadcasted_iota(jnp.int32, (PT, LANES), 0)

    @pl.loop(0, groups)
    def _(g):
        fetch(g).wait()
        for i in range(GROUP):
            p = g * GROUP + i
            tokens = raw_ref[p].astype(jnp.float32)
            clean_ref[p] = jnp.where(u < len_ref[p], tokens, tokens[0:1]).astype(jnp.bfloat16)


def prepare(shards, candidates, lengths, passages):
    hbm = pl.BlockSpec(memory_space=pltpu.HBM)
    vmem = pl.BlockSpec(memory_space=pltpu.VMEM)
    operands = [pltpu.with_memory_space_constraint(x, pltpu.HBM) for x in (candidates, lengths, passages)]
    return pl.pallas_call(
        prepare_kernel,
        out_shape=[
            jax.ShapeDtypeStruct((shards, LANES), jnp.float32),
            jax.ShapeDtypeStruct((shards, LANES), jnp.int32),
            jax.ShapeDtypeStruct(passages.shape, passages.dtype),
        ],
        in_specs=[hbm] * 3,
        out_specs=[vmem] * 3,
        scratch_shapes=[
            pltpu.VMEM(candidates.shape, candidates.dtype),
            pltpu.SMEM(lengths.shape, lengths.dtype),
            pltpu.VMEM(passages.shape, passages.dtype),
            pltpu.SemaphoreType.DMA((passages.shape[0] // GROUP + 2,)),
        ],
        compiler_params=pltpu.CompilerParams(vmem_limit_bytes=24 * 1024 * 1024),
        cost_estimate=pl.CostEstimate(flops=passages.size, bytes_accessed=2 * passages.size, transcendentals=0),
    )(*operands)


def near_owner(me, step, planes):
    return lax.rem((me >> 1) + planes - step, planes) << 1 | me & 1


def picked(picks_ref, owner, q_ref):
    pick = jnp.max(picks_ref[pl.ds(owner, 1), :])
    return q_ref[pl.ds(pick * QB * QT, QB * QT), :]


def pack_kernel(steps, planes, cand_ref, *refs):
    q_refs, out_ref = refs[:-1], refs[-1]
    me = lax.axis_index("psg")
    cand = cand_ref[...]
    owner = cand // QBD
    block = cand - owner * QBD
    for n, step in enumerate(steps):
        pick = jnp.max(jnp.where(owner == near_owner(me, step, planes), block, 0))
        out_ref[n * QB * QT:(n + 1) * QB * QT, :] = q_refs[n][pl.ds(pick * QB * QT, QB * QT), :]


def pack(steps, planes, candidates, blocks):
    vmem = pl.BlockSpec(memory_space=pltpu.VMEM)
    return pl.pallas_call(
        functools.partial(pack_kernel, steps, planes),
        out_shape=jax.ShapeDtypeStruct((len(blocks) * QB * QT, DIM), blocks[0].dtype),
        in_specs=[vmem] * (1 + len(blocks)),
        out_specs=vmem,
        compiler_params=pltpu.CompilerParams(vmem_limit_bytes=4 * 1024 * 1024),
    )(candidates, *blocks)


def sum_tokens(best):
    tokens = best.shape[1]
    high = best.astype(jnp.bfloat16)
    rest = best - high.astype(jnp.float32)
    mid = rest.astype(jnp.bfloat16)
    low = (rest - mid.astype(jnp.float32)).astype(jnp.bfloat16)
    parts = jnp.concatenate([low, mid, high], axis=1)
    query = lax.broadcasted_iota(jnp.int32, (tokens // QT, tokens), 0)
    token = lax.broadcasted_iota(jnp.int32, (tokens // QT, tokens), 1)
    ones = jnp.where(token // QT == query, 1.0, 0.0).astype(jnp.bfloat16)
    total = lax.dot_general(
        jnp.concatenate([ones] * 3, axis=1), parts, (((1,), (1,)), ((), ())), preferred_element_type=jnp.float32
    )
    return total * (1.0 / QT)


def best_tokens(left_of, sel, max_ref):
    count, tokens = max_ref.shape
    piece = 2 * GROUP
    for g in range(0, count, piece):
        dots = lax.dot_general(left_of(g, piece), sel, (((1,), (1,)), ((), ())), preferred_element_type=jnp.float32)
        max_ref[g:g + piece, :] = jnp.max(dots.reshape(piece, PT, tokens), axis=1)
    return max_ref[...]


def score_picked(sel, p_ref, max_ref):
    def left_of(g, piece):
        return p_ref[g:g + piece].reshape(piece * PT, DIM)

    return sum_tokens(best_tokens(left_of, sel, max_ref))


def score_picked_few(sel, p_ref, wide_ref, max_ref):
    tokens, half = sel.shape[0], p_ref.shape[0] // 2
    wide_ref[...] = jnp.zeros_like(wide_ref)
    wide_ref[0:tokens, 0:DIM] = sel
    wide_ref[tokens:, DIM:] = sel

    def left_of(g, piece):
        return jnp.concatenate(
            [p_ref[h + g:h + g + piece].reshape(piece * PT, DIM) for h in (0, half)], axis=1
        )

    total = sum_tokens(best_tokens(left_of, wide_ref[...], max_ref))
    queries = tokens // QT
    return jnp.concatenate([total[:queries], total[queries:]], axis=1)


def put(out_ref, place, total, n, slots_ref, owner):
    out_ref[place, 0:QB, :] = total[n * QB:(n + 1) * QB]
    out_ref[place, QB:QB + 1, :] = slots_ref[pl.ds(owner, 1), :]


def most_kernel(steps, planes, slots_ref, picks_ref, p_ref, far_ref, *refs):
    q_refs, (out_ref, sel_ref, max_ref, wide_ref, few_max_ref) = refs[:-5], refs[-5:]
    me = lax.axis_index("psg")
    owners = [near_owner(me, n, planes) for n in range(planes)]
    for n, owner in enumerate(owners):
        sel_ref[n * QB * QT:(n + 1) * QB * QT, :] = picked(picks_ref, owner, q_refs[n])
    total = score_picked(sel_ref[...], p_ref, max_ref)
    for n, owner in enumerate(owners):
        put(out_ref, n, total, n, slots_ref, owner)
    total = score_picked_few(far_ref[...], p_ref, wide_ref, few_max_ref)
    for n, step in enumerate(steps):
        put(out_ref, planes + n, total, n, slots_ref, owners[step] ^ 1)


def last_kernel(steps, planes, slots_ref, p_ref, far_ref, earlier_ref, out_ref, wide_ref, few_max_ref):
    me = lax.axis_index("psg")
    owners = [near_owner(me, n, planes) for n in range(planes)]
    total = score_picked_few(far_ref[...], p_ref, wide_ref, few_max_ref)
    for n, step in enumerate(steps):
        put(out_ref, owners[step] ^ 1, total, n, slots_ref, owners[step] ^ 1)
    others = [step for step in range(planes) if step not in steps]
    for n, owner in enumerate(owners + [owners[step] ^ 1 for step in others]):
        out_ref[owner] = earlier_ref[n]


def all_kernel(slots_ref, picks_ref, p_ref, q_ref, out_ref, sel_ref, max_ref):
    some = q_ref.shape[0]
    for n in range(some):
        sel_ref[n * QB * QT:(n + 1) * QB * QT, :] = picked(picks_ref, n, q_ref.at[n])
    total = score_picked(sel_ref[...], p_ref, max_ref)
    for n in range(some):
        put(out_ref, n, total, n, slots_ref, n)


def score(kernel, tiles, some, few, passages, *more):
    count, tokens = passages.shape[0], some * QB * QT
    vmem = pl.BlockSpec(memory_space=pltpu.VMEM)
    scratch = []
    if some:
        scratch += [pltpu.VMEM((tokens, DIM), jnp.bfloat16), pltpu.VMEM((count, tokens), jnp.float32)]
    if few:
        wide = 2 * few * QB * QT
        scratch += [pltpu.VMEM((wide, 2 * DIM), jnp.bfloat16), pltpu.VMEM((count // 2, wide), jnp.float32)]
    return pl.pallas_call(
        kernel,
        out_shape=jax.ShapeDtypeStruct((tiles, QB + 1, LANES), jnp.float32),
        in_specs=[vmem] * len(more),
        out_specs=vmem,
        scratch_shapes=scratch,
        compiler_params=pltpu.CompilerParams(vmem_limit_bytes=32 * 1024 * 1024),
        cost_estimate=pl.CostEstimate(
            flops=2 * passages.size * (some + few) * QB * QT, bytes_accessed=2 * passages.size, transcendentals=0
        ),
    )(*more)


def place_kernel(in_ref, out_ref):
    slots = out_ref.shape[-1]
    m = lax.broadcasted_iota(jnp.int32, (PBS, LANES), 0)
    for j in range(in_ref.shape[0]):
        row = in_ref[j, QB:QB + 1, :].astype(jnp.int32)
        where = jnp.minimum(row * PBS, LANES - PBS) + m
        for i in range(QB):
            tile = jnp.broadcast_to(in_ref[j, i:i + 1, :], (PBS, LANES))
            out_ref[j, i] = jnp.take_along_axis(tile, where, axis=1)[:, :slots]


def place(tiles, slots):
    vmem = pl.BlockSpec(memory_space=pltpu.VMEM)
    shards = tiles.shape[0]
    return pl.pallas_call(
        place_kernel,
        out_shape=jax.ShapeDtypeStruct((shards, QB, PBS, slots), jnp.float32),
        in_specs=[vmem],
        out_specs=vmem,
        compiler_params=pltpu.CompilerParams(vmem_limit_bytes=8 * 1024 * 1024),
    )(tiles)


def by_planes(own, shards, candidates, lengths, passages):
    planes = shards // 2

    def swap_sides(x):
        return lax.ppermute(x, "psg", [(j, j ^ 1) for j in range(shards)])

    def shift(x, step):
        return lax.ppermute(x, "psg", [(j, (j + 2 * step) % shards) for j in range(shards)])

    theirs = swap_sides(candidates)
    shifted = [shift(own, step) for step in range(1, planes)]
    slots, picks, clean = prepare(shards, candidates, lengths, passages)
    half = planes // 2
    clean, *early = lax.optimization_barrier((clean, *reversed(shifted[:half - 1])))
    early, late = [own, *reversed(early)], shifted[half - 1:]
    first, last = list(range(half)), list(range(half, planes))
    packed = pack(first, planes, theirs, early)
    first_far = swap_sides(packed)
    *late, _ = lax.optimization_barrier((*late, packed))
    last_far = swap_sides(pack(last, planes, theirs, late))
    tiles = score(
        functools.partial(most_kernel, first, planes), planes + half, planes, half, clean,
        slots, picks, clean, first_far, *early, *late,
    )
    last_far, tiles = lax.optimization_barrier((last_far, tiles))
    return score(functools.partial(last_kernel, last, planes), shards, 0, half, clean, slots, clean, last_far, tiles)


def by_gather(own, shards, candidates, lengths, passages):
    slots, picks, clean = prepare(shards, candidates, lengths, passages)
    gathered = lax.all_gather(own, "psg", axis=0)
    some = min(shards, 8)

    def score_some(items):
        return score(all_kernel, some, some, 0, clean, items[0], items[1], clean, items[2])

    parts = [x.reshape(shards // some, some, *x.shape[1:]) for x in (slots, picks, gathered)]
    return lax.map(score_some, parts).reshape(shards, QB + 1, LANES)


def per_device(queries, passages, lengths, candidates):
    shards = lax.axis_size("psg")
    rows = passages.shape[0] // PBS
    form = by_planes if shards == 8 else by_gather
    tiles = form(
        queries.reshape(QBD * QB * QT, DIM), shards, candidates.reshape(rows, KB), lengths, passages
    )
    tiles = lax.all_to_all(tiles, "psg", split_axis=0, concat_axis=0, tiled=True)
    return place(tiles, rows * KB // shards).transpose(0, 3, 1, 2)[None]


def solution(mesh):
    return jax.shard_map(
        per_device,
        mesh=mesh,
        in_specs=(
            P(("grp", "psg", "qry"), None, None),
            P(("grp", "psg"), None, None),
            P(("grp", "psg")),
            P("qry", ("grp", "psg"), None),
        ),
        out_specs=P(("grp", "psg", "qry"), None, None, None, None),
        check_vma=False,
    )
```

```python
import functools

import jax
import jax.numpy as jnp
from jax import lax
from jax.experimental import pallas as pl
from jax.experimental.pallas import tpu as pltpu
from jax.sharding import PartitionSpec as P

DIM = 128
QT = 32
PT = 64
QB = 2
QBD = 4
PBS = 16
KB = 32
LANES = 128
GROUP = 8
PACK = 16


def prepare_kernel(
    cand_hbm, len_hbm, p_hbm, slots_ref, picks_ref, clean_ref, cand_ref, len_ref, raw_ref, sems
):
    rows = cand_ref.shape[0]
    shards = slots_ref.shape[0]
    groups = p_hbm.shape[0] // GROUP

    def fetch(g):
        part = pl.ds(g * GROUP, GROUP)
        return pltpu.make_async_copy(p_hbm.at[part], raw_ref.at[part], sems.at[g])

    fetch_cand = pltpu.make_async_copy(cand_hbm, cand_ref, sems.at[groups])
    fetch_len = pltpu.make_async_copy(len_hbm, len_ref, sems.at[groups + 1])
    fetch_cand.start()
    fetch_len.start()
    for g in range(groups):
        fetch(g).start()

    fetch_cand.wait()
    cand = cand_ref[...]
    owner = cand // QBD
    block = cand - owner * QBD
    lane = lax.broadcasted_iota(jnp.int32, (rows, LANES), 1).astype(jnp.float32)
    sub = lax.broadcasted_iota(jnp.int32, (rows, LANES), 0)
    for o in range(shards):
        mine = owner == o
        named = jnp.max(jnp.where(mine, block, 0), axis=1, keepdims=True)
        picks_ref[o:o + 1, :] = jnp.broadcast_to(jnp.max(named, axis=0, keepdims=True), (1, LANES))
        named_here = jnp.sum(jnp.where(mine, 1.0, 0.0), axis=1, keepdims=True)
        upto = jnp.broadcast_to(named_here, (rows, LANES))
        step = 1
        while step < rows:
            upto = upto + jnp.where(sub >= step, pltpu.roll(upto, step, 0), 0.0)
            step *= 2
        slots_ref[o:o + 1, :] = jnp.sum(jnp.where(upto <= lane, 1.0, 0.0), axis=0, keepdims=True)

    fetch_len.wait()
    u = lax.broadcasted_iota(jnp.int32, (PT, LANES), 0).astype(jnp.int16)

    @pl.loop(0, groups)
    def _(g):
        fetch(g).wait()
        for i in range(GROUP):
            p = g * GROUP + i
            tokens = raw_ref[p]
            first = jnp.broadcast_to(tokens[0:PACK].astype(jnp.float32)[0:1], (PACK, LANES)).astype(jnp.bfloat16)
            limit = jnp.full((PACK, LANES), len_ref[p], jnp.int32).astype(jnp.int16)
            live = u < jnp.concatenate([limit] * (PT // PACK))
            clean_ref[p] = jnp.where(live, tokens, jnp.concatenate([first] * (PT // PACK)))


def prepare(shards, candidates, lengths, passages):
    hbm = pl.BlockSpec(memory_space=pltpu.HBM)
    vmem = pl.BlockSpec(memory_space=pltpu.VMEM)
    operands = [pltpu.with_memory_space_constraint(x, pltpu.HBM) for x in (candidates, lengths, passages)]
    return pl.pallas_call(
        prepare_kernel,
        out_shape=[
            jax.ShapeDtypeStruct((shards, LANES), jnp.float32),
            jax.ShapeDtypeStruct((shards, LANES), jnp.int32),
            jax.ShapeDtypeStruct(passages.shape, passages.dtype),
        ],
        in_specs=[hbm] * 3,
        out_specs=[vmem] * 3,
        scratch_shapes=[
            pltpu.VMEM(candidates.shape, candidates.dtype),
            pltpu.SMEM(lengths.shape, lengths.dtype),
            pltpu.VMEM(passages.shape, passages.dtype),
            pltpu.SemaphoreType.DMA((passages.shape[0] // GROUP + 2,)),
        ],
        compiler_params=pltpu.CompilerParams(vmem_limit_bytes=24 * 1024 * 1024),
        cost_estimate=pl.CostEstimate(flops=passages.size, bytes_accessed=2 * passages.size, transcendentals=0),
    )(*operands)


def near_owner(me, step, planes):
    return lax.rem((me >> 1) + planes - step, planes) << 1 | me & 1


def picked(picks_ref, owner, q_ref):
    pick = jnp.max(picks_ref[pl.ds(owner, 1), :])
    return q_ref[pl.ds(pick * QB * QT, QB * QT), :]


def pack_kernel(steps, planes, cand_ref, *refs):
    q_refs, out_ref = refs[:-1], refs[-1]
    me = lax.axis_index("psg")
    cand = cand_ref[...]
    owner = cand // QBD
    block = cand - owner * QBD
    for n, step in enumerate(steps):
        pick = jnp.max(jnp.where(owner == near_owner(me, step, planes), block, 0))
        out_ref[n * QB * QT:(n + 1) * QB * QT, :] = q_refs[n][pl.ds(pick * QB * QT, QB * QT), :]


def pack(steps, planes, candidates, blocks):
    vmem = pl.BlockSpec(memory_space=pltpu.VMEM)
    return pl.pallas_call(
        functools.partial(pack_kernel, steps, planes),
        out_shape=jax.ShapeDtypeStruct((len(blocks) * QB * QT, DIM), blocks[0].dtype),
        in_specs=[vmem] * (1 + len(blocks)),
        out_specs=vmem,
        compiler_params=pltpu.CompilerParams(vmem_limit_bytes=4 * 1024 * 1024),
    )(candidates, *blocks)


def sum_tokens(best):
    tokens = best.shape[1]
    high = best.astype(jnp.bfloat16)
    rest = best - high.astype(jnp.float32)
    mid = rest.astype(jnp.bfloat16)
    low = (rest - mid.astype(jnp.float32)).astype(jnp.bfloat16)
    parts = jnp.concatenate([low, mid, high], axis=1)
    query = lax.broadcasted_iota(jnp.int32, (tokens // QT, tokens), 0)
    token = lax.broadcasted_iota(jnp.int32, (tokens // QT, tokens), 1)
    ones = jnp.where(token // QT == query, 1.0, 0.0).astype(jnp.bfloat16)
    total = lax.dot_general(
        jnp.concatenate([ones] * 3, axis=1), parts, (((1,), (1,)), ((), ())), preferred_element_type=jnp.float32
    )
    return total * (1.0 / QT)


def best_tokens(left_of, sel, max_ref):
    count, tokens = max_ref.shape
    piece = 2 * GROUP
    for g in range(0, count, piece):
        dots = lax.dot_general(left_of(g, piece), sel, (((1,), (1,)), ((), ())), preferred_element_type=jnp.float32)
        max_ref[g:g + piece, :] = jnp.max(dots.reshape(piece, PT, tokens), axis=1)
    return max_ref[...]


def score_picked(sel, p_ref, max_ref):
    def left_of(g, piece):
        return p_ref[g:g + piece].reshape(piece * PT, DIM)

    return sum_tokens(best_tokens(left_of, sel, max_ref))


def score_picked_few(sel, p_ref, wide_ref, max_ref):
    tokens, half = sel.shape[0], p_ref.shape[0] // 2
    wide_ref[...] = jnp.zeros_like(wide_ref)
    wide_ref[0:tokens, 0:DIM] = sel
    wide_ref[tokens:, DIM:] = sel

    def left_of(g, piece):
        return jnp.concatenate(
            [p_ref[h + g:h + g + piece].reshape(piece * PT, DIM) for h in (0, half)], axis=1
        )

    total = sum_tokens(best_tokens(left_of, wide_ref[...], max_ref))
    queries = tokens // QT
    return jnp.concatenate([total[:queries], total[queries:]], axis=1)


def put(out_ref, place, total, n, slots_ref, owner):
    out_ref[place, 0:QB, :] = total[n * QB:(n + 1) * QB]
    out_ref[place, QB:QB + 1, :] = slots_ref[pl.ds(owner, 1), :]


def near_kernel(slots_ref, picks_ref, p_ref, *refs):
    q_refs, (out_ref, sel_ref, max_ref) = refs[:-3], refs[-3:]
    me = lax.axis_index("psg")
    owners = [near_owner(me, n, len(q_refs)) for n in range(len(q_refs))]
    for n, owner in enumerate(owners):
        sel_ref[n * QB * QT:(n + 1) * QB * QT, :] = picked(picks_ref, owner, q_refs[n])
    total = score_picked(sel_ref[...], p_ref, max_ref)
    for n, owner in enumerate(owners):
        put(out_ref, n, total, n, slots_ref, owner)


def some_far_kernel(steps, planes, slots_ref, p_ref, sel_ref, out_ref, wide_ref, max_ref):
    me = lax.axis_index("psg")
    total = score_picked_few(sel_ref[...], p_ref, wide_ref, max_ref)
    for n, step in enumerate(steps):
        put(out_ref, n, total, n, slots_ref, near_owner(me, step, planes) ^ 1)


def last_far_kernel(steps, planes, slots_ref, p_ref, sel_ref, near_ref, far_ref, out_ref, wide_ref, max_ref):
    me = lax.axis_index("psg")
    total = score_picked_few(sel_ref[...], p_ref, wide_ref, max_ref)
    for n, step in enumerate(steps):
        owner = near_owner(me, step, planes) ^ 1
        put(out_ref, owner, total, n, slots_ref, owner)
    others = [step for step in range(planes) if step not in steps]
    for step in range(planes):
        out_ref[near_owner(me, step, planes)] = near_ref[step]
    for n, step in enumerate(others):
        out_ref[near_owner(me, step, planes) ^ 1] = far_ref[n]


def all_kernel(slots_ref, picks_ref, p_ref, q_ref, out_ref, sel_ref, max_ref):
    some = q_ref.shape[0]
    for n in range(some):
        sel_ref[n * QB * QT:(n + 1) * QB * QT, :] = picked(picks_ref, n, q_ref.at[n])
    total = score_picked(sel_ref[...], p_ref, max_ref)
    for n in range(some):
        put(out_ref, n, total, n, slots_ref, n)


def score(kernel, tiles, some, few, passages, *more):
    count, tokens = passages.shape[0], some * QB * QT
    vmem = pl.BlockSpec(memory_space=pltpu.VMEM)
    if few:
        scratch = [pltpu.VMEM((2 * tokens, 2 * DIM), jnp.bfloat16), pltpu.VMEM((count // 2, 2 * tokens), jnp.float32)]
    else:
        scratch = [pltpu.VMEM((tokens, DIM), jnp.bfloat16), pltpu.VMEM((count, tokens), jnp.float32)]
    return pl.pallas_call(
        kernel,
        out_shape=jax.ShapeDtypeStruct((tiles, QB + 1, LANES), jnp.float32),
        in_specs=[vmem] * len(more),
        out_specs=vmem,
        scratch_shapes=scratch,
        compiler_params=pltpu.CompilerParams(vmem_limit_bytes=32 * 1024 * 1024),
        cost_estimate=pl.CostEstimate(
            flops=2 * passages.size * tokens, bytes_accessed=2 * passages.size, transcendentals=0
        ),
    )(*more)


def place_kernel(in_ref, out_ref):
    slots = out_ref.shape[-1]
    m = lax.broadcasted_iota(jnp.int32, (PBS, LANES), 0)
    for j in range(in_ref.shape[0]):
        row = in_ref[j, QB:QB + 1, :].astype(jnp.int32)
        where = jnp.minimum(row * PBS, LANES - PBS) + m
        for i in range(QB):
            tile = jnp.broadcast_to(in_ref[j, i:i + 1, :], (PBS, LANES))
            out_ref[j, i] = jnp.take_along_axis(tile, where, axis=1)[:, :slots]


def place(tiles, slots):
    vmem = pl.BlockSpec(memory_space=pltpu.VMEM)
    shards = tiles.shape[0]
    return pl.pallas_call(
        place_kernel,
        out_shape=jax.ShapeDtypeStruct((shards, QB, PBS, slots), jnp.float32),
        in_specs=[vmem],
        out_specs=vmem,
        compiler_params=pltpu.CompilerParams(vmem_limit_bytes=8 * 1024 * 1024),
    )(tiles)


def by_planes(own, shards, candidates, lengths, passages):
    planes = shards // 2

    def swap_sides(x):
        return lax.ppermute(x, "psg", [(j, j ^ 1) for j in range(shards)])

    def shift(x, step):
        return lax.ppermute(x, "psg", [(j, (j + 2 * step) % shards) for j in range(shards)])

    theirs = swap_sides(candidates)
    shifted = [shift(own, step) for step in range(1, planes)]
    slots, picks, clean = prepare(shards, candidates, lengths, passages)
    clean, *early = lax.optimization_barrier((clean, *reversed(shifted[:planes // 2 - 1])))
    early, late = [own, *reversed(early)], shifted[planes // 2 - 1:]
    steps = list(range(planes))
    first, last = steps[:planes // 2], steps[planes // 2:]
    packed = pack(first, planes, theirs, early)
    first_far = swap_sides(packed)
    *late, _ = lax.optimization_barrier((*reversed(late), packed))
    late = late[::-1]
    last_far = swap_sides(pack(last, planes, theirs, late))
    near_tiles = score(near_kernel, planes, planes, False, clean, slots, picks, clean, *early, *late)
    first_far, near_tiles = lax.optimization_barrier((first_far, near_tiles))
    far_tiles = score(
        functools.partial(some_far_kernel, first, planes), len(first), len(first), True, clean, slots, clean, first_far
    )
    last_far, far_tiles = lax.optimization_barrier((last_far, far_tiles))
    return score(
        functools.partial(last_far_kernel, last, planes), shards, len(last), True, clean,
        slots, clean, last_far, near_tiles, far_tiles,
    )


def by_gather(own, shards, candidates, lengths, passages):
    slots, picks, clean = prepare(shards, candidates, lengths, passages)
    gathered = lax.all_gather(own, "psg", axis=0)
    some = min(shards, 8)

    def score_some(items):
        return score(all_kernel, some, some, False, clean, items[0], items[1], clean, items[2])

    parts = [x.reshape(shards // some, some, *x.shape[1:]) for x in (slots, picks, gathered)]
    return lax.map(score_some, parts).reshape(shards, QB + 1, LANES)


def per_device(queries, passages, lengths, candidates):
    shards = lax.axis_size("psg")
    rows = passages.shape[0] // PBS
    form = by_planes if shards == 8 else by_gather
    tiles = form(
        queries.reshape(QBD * QB * QT, DIM), shards, candidates.reshape(rows, KB), lengths, passages
    )
    tiles = lax.all_to_all(tiles, "psg", split_axis=0, concat_axis=0, tiled=True)
    return place(tiles, rows * KB // shards).transpose(0, 3, 1, 2)[None]


def solution(mesh):
    return jax.shard_map(
        per_device,
        mesh=mesh,
        in_specs=(
            P(("grp", "psg", "qry"), None, None),
            P(("grp", "psg"), None, None),
            P(("grp", "psg")),
            P("qry", ("grp", "psg"), None),
        ),
        out_specs=P(("grp", "psg", "qry"), None, None, None, None),
        check_vma=False,
    )
```

```python
import functools

import jax
import jax.numpy as jnp
from jax import lax
from jax.experimental import pallas as pl
from jax.experimental.pallas import tpu as pltpu
from jax.sharding import PartitionSpec as P

DIM = 128
QT = 32
PT = 64
QB = 2
QBD = 4
PBS = 16
KB = 32
LANES = 128
GROUP = 8


def prepare_kernel(
    cand_hbm, len_hbm, p_hbm, slots_ref, picks_ref, clean_ref, cand_ref, len_ref, raw_ref, sems
):
    rows = cand_ref.shape[0]
    shards = slots_ref.shape[0]
    groups = p_hbm.shape[0] // GROUP

    def fetch(g):
        part = pl.ds(g * GROUP, GROUP)
        return pltpu.make_async_copy(p_hbm.at[part], raw_ref.at[part], sems.at[g])

    fetch_cand = pltpu.make_async_copy(cand_hbm, cand_ref, sems.at[groups])
    fetch_len = pltpu.make_async_copy(len_hbm, len_ref, sems.at[groups + 1])
    fetch_cand.start()
    fetch_len.start()
    for g in range(groups):
        fetch(g).start()

    fetch_cand.wait()
    cand = cand_ref[...]
    owner = cand // QBD
    block = cand - owner * QBD
    lane = lax.broadcasted_iota(jnp.int32, (rows, LANES), 1).astype(jnp.float32)
    sub = lax.broadcasted_iota(jnp.int32, (rows, LANES), 0)
    for o in range(shards):
        mine = owner == o
        named = jnp.max(jnp.where(mine, block, 0), axis=1, keepdims=True)
        picks_ref[o:o + 1, :] = jnp.broadcast_to(jnp.max(named, axis=0, keepdims=True), (1, LANES))
        named_here = jnp.sum(jnp.where(mine, 1.0, 0.0), axis=1, keepdims=True)
        upto = jnp.broadcast_to(named_here, (rows, LANES))
        step = 1
        while step < rows:
            upto = upto + jnp.where(sub >= step, pltpu.roll(upto, step, 0), 0.0)
            step *= 2
        slots_ref[o:o + 1, :] = jnp.sum(jnp.where(upto <= lane, 1.0, 0.0), axis=0, keepdims=True)

    fetch_len.wait()
    u = lax.broadcasted_iota(jnp.int32, (PT, LANES), 0)

    @pl.loop(0, groups)
    def _(g):
        fetch(g).wait()
        for i in range(GROUP):
            p = g * GROUP + i
            tokens = raw_ref[p].astype(jnp.float32)
            clean_ref[p] = jnp.where(u < len_ref[p], tokens, tokens[0:1]).astype(jnp.bfloat16)


def prepare(shards, candidates, lengths, passages):
    hbm = pl.BlockSpec(memory_space=pltpu.HBM)
    vmem = pl.BlockSpec(memory_space=pltpu.VMEM)
    operands = [pltpu.with_memory_space_constraint(x, pltpu.HBM) for x in (candidates, lengths, passages)]
    return pl.pallas_call(
        prepare_kernel,
        out_shape=[
            jax.ShapeDtypeStruct((shards, LANES), jnp.float32),
            jax.ShapeDtypeStruct((shards, LANES), jnp.int32),
            jax.ShapeDtypeStruct(passages.shape, passages.dtype),
        ],
        in_specs=[hbm] * 3,
        out_specs=[vmem] * 3,
        scratch_shapes=[
            pltpu.VMEM(candidates.shape, candidates.dtype),
            pltpu.SMEM(lengths.shape, lengths.dtype),
            pltpu.VMEM(passages.shape, passages.dtype),
            pltpu.SemaphoreType.DMA((passages.shape[0] // GROUP + 2,)),
        ],
        compiler_params=pltpu.CompilerParams(vmem_limit_bytes=24 * 1024 * 1024),
        cost_estimate=pl.CostEstimate(flops=passages.size, bytes_accessed=2 * passages.size, transcendentals=0),
    )(*operands)


def near_owner(me, step, planes):
    return lax.rem((me >> 1) + planes - step, planes) << 1 | me & 1


def picked(picks_ref, owner, q_ref):
    pick = jnp.max(picks_ref[pl.ds(owner, 1), :])
    return q_ref[pl.ds(pick * QB * QT, QB * QT), :]


def pack_kernel(steps, planes, cand_ref, *refs):
    q_refs, out_ref = refs[:-1], refs[-1]
    me = lax.axis_index("psg")
    cand = cand_ref[...]
    owner = cand // QBD
    block = cand - owner * QBD
    for n, step in enumerate(steps):
        pick = jnp.max(jnp.where(owner == near_owner(me, step, planes), block, 0))
        out_ref[n * QB * QT:(n + 1) * QB * QT, :] = q_refs[n][pl.ds(pick * QB * QT, QB * QT), :]


def pack(steps, planes, candidates, blocks):
    vmem = pl.BlockSpec(memory_space=pltpu.VMEM)
    return pl.pallas_call(
        functools.partial(pack_kernel, steps, planes),
        out_shape=jax.ShapeDtypeStruct((len(blocks) * QB * QT, DIM), blocks[0].dtype),
        in_specs=[vmem] * (1 + len(blocks)),
        out_specs=vmem,
        compiler_params=pltpu.CompilerParams(vmem_limit_bytes=4 * 1024 * 1024),
    )(candidates, *blocks)


def sum_tokens(best):
    tokens = best.shape[1]
    high = best.astype(jnp.bfloat16)
    rest = best - high.astype(jnp.float32)
    mid = rest.astype(jnp.bfloat16)
    low = (rest - mid.astype(jnp.float32)).astype(jnp.bfloat16)
    parts = jnp.concatenate([low, mid, high], axis=1)
    query = lax.broadcasted_iota(jnp.int32, (tokens // QT, tokens), 0)
    token = lax.broadcasted_iota(jnp.int32, (tokens // QT, tokens), 1)
    ones = jnp.where(token // QT == query, 1.0, 0.0).astype(jnp.bfloat16)
    total = lax.dot_general(
        jnp.concatenate([ones] * 3, axis=1), parts, (((1,), (1,)), ((), ())), preferred_element_type=jnp.float32
    )
    return total * (1.0 / QT)


def best_tokens(left_of, sel, max_ref):
    count, tokens = max_ref.shape
    piece = 2 * GROUP
    for g in range(0, count, piece):
        dots = lax.dot_general(left_of(g, piece), sel, (((1,), (1,)), ((), ())), preferred_element_type=jnp.float32)
        max_ref[g:g + piece, :] = jnp.max(dots.reshape(piece, PT, tokens), axis=1)
    return max_ref[...]


def score_picked(sel, p_ref, max_ref):
    def left_of(g, piece):
        return p_ref[g:g + piece].reshape(piece * PT, DIM)

    return sum_tokens(best_tokens(left_of, sel, max_ref))


def score_picked_few(sel, p_ref, wide_ref, max_ref):
    tokens, half = sel.shape[0], p_ref.shape[0] // 2
    wide_ref[...] = jnp.zeros_like(wide_ref)
    wide_ref[0:tokens, 0:DIM] = sel
    wide_ref[tokens:, DIM:] = sel

    def left_of(g, piece):
        return jnp.concatenate(
            [p_ref[h + g:h + g + piece].reshape(piece * PT, DIM) for h in (0, half)], axis=1
        )

    total = sum_tokens(best_tokens(left_of, wide_ref[...], max_ref))
    queries = tokens // QT
    return jnp.concatenate([total[:queries], total[queries:]], axis=1)


def put(out_ref, place, total, n, slots_ref, owner):
    out_ref[place, 0:QB, :] = total[n * QB:(n + 1) * QB]
    out_ref[place, QB:QB + 1, :] = slots_ref[pl.ds(owner, 1), :]


def near_kernel(slots_ref, picks_ref, p_ref, *refs):
    q_refs, (out_ref, sel_ref, max_ref) = refs[:-3], refs[-3:]
    me = lax.axis_index("psg")
    owners = [near_owner(me, n, len(q_refs)) for n in range(len(q_refs))]
    for n, owner in enumerate(owners):
        sel_ref[n * QB * QT:(n + 1) * QB * QT, :] = picked(picks_ref, owner, q_refs[n])
    total = score_picked(sel_ref[...], p_ref, max_ref)
    for n, owner in enumerate(owners):
        put(out_ref, n, total, n, slots_ref, owner)


def some_far_kernel(steps, planes, slots_ref, p_ref, sel_ref, out_ref, wide_ref, max_ref):
    me = lax.axis_index("psg")
    total = score_picked_few(sel_ref[...], p_ref, wide_ref, max_ref)
    for n, step in enumerate(steps):
        put(out_ref, n, total, n, slots_ref, near_owner(me, step, planes) ^ 1)


def last_far_kernel(steps, planes, slots_ref, p_ref, sel_ref, near_ref, far_ref, out_ref, wide_ref, max_ref):
    me = lax.axis_index("psg")
    total = score_picked_few(sel_ref[...], p_ref, wide_ref, max_ref)
    for n, step in enumerate(steps):
        owner = near_owner(me, step, planes) ^ 1
        put(out_ref, owner, total, n, slots_ref, owner)
    others = [step for step in range(planes) if step not in steps]
    for step in range(planes):
        out_ref[near_owner(me, step, planes)] = near_ref[step]
    for n, step in enumerate(others):
        out_ref[near_owner(me, step, planes) ^ 1] = far_ref[n]


def all_kernel(slots_ref, picks_ref, p_ref, q_ref, out_ref, sel_ref, max_ref):
    some = q_ref.shape[0]
    for n in range(some):
        sel_ref[n * QB * QT:(n + 1) * QB * QT, :] = picked(picks_ref, n, q_ref.at[n])
    total = score_picked(sel_ref[...], p_ref, max_ref)
    for n in range(some):
        put(out_ref, n, total, n, slots_ref, n)


def score(kernel, tiles, some, few, passages, *more):
    count, tokens = passages.shape[0], some * QB * QT
    vmem = pl.BlockSpec(memory_space=pltpu.VMEM)
    if few:
        scratch = [pltpu.VMEM((2 * tokens, 2 * DIM), jnp.bfloat16), pltpu.VMEM((count // 2, 2 * tokens), jnp.float32)]
    else:
        scratch = [pltpu.VMEM((tokens, DIM), jnp.bfloat16), pltpu.VMEM((count, tokens), jnp.float32)]
    return pl.pallas_call(
        kernel,
        out_shape=jax.ShapeDtypeStruct((tiles, QB + 1, LANES), jnp.float32),
        in_specs=[vmem] * len(more),
        out_specs=vmem,
        scratch_shapes=scratch,
        compiler_params=pltpu.CompilerParams(vmem_limit_bytes=32 * 1024 * 1024),
        cost_estimate=pl.CostEstimate(
            flops=2 * passages.size * tokens, bytes_accessed=2 * passages.size, transcendentals=0
        ),
    )(*more)


def place_kernel(in_ref, out_ref):
    slots = out_ref.shape[-1]
    m = lax.broadcasted_iota(jnp.int32, (PBS, LANES), 0)
    for j in range(in_ref.shape[0]):
        row = in_ref[j, QB:QB + 1, :].astype(jnp.int32)
        where = jnp.minimum(row * PBS, LANES - PBS) + m
        for i in range(QB):
            tile = jnp.broadcast_to(in_ref[j, i:i + 1, :], (PBS, LANES))
            out_ref[j, i] = jnp.take_along_axis(tile, where, axis=1)[:, :slots]


def place(tiles, slots):
    vmem = pl.BlockSpec(memory_space=pltpu.VMEM)
    shards = tiles.shape[0]
    return pl.pallas_call(
        place_kernel,
        out_shape=jax.ShapeDtypeStruct((shards, QB, PBS, slots), jnp.float32),
        in_specs=[vmem],
        out_specs=vmem,
        compiler_params=pltpu.CompilerParams(vmem_limit_bytes=8 * 1024 * 1024),
    )(tiles)


def by_planes(own, shards, candidates, lengths, passages):
    planes = shards // 2

    def swap_sides(x):
        return lax.ppermute(x, "psg", [(j, j ^ 1) for j in range(shards)])

    def shift(x, step):
        return lax.ppermute(x, "psg", [(j, (j + 2 * step) % shards) for j in range(shards)])

    theirs = swap_sides(candidates)
    shifted = [shift(own, step) for step in range(1, planes)]
    slots, picks, clean = prepare(shards, candidates, lengths, passages)
    clean, *early = lax.optimization_barrier((clean, *reversed(shifted[:planes // 2 - 1])))
    early, late = [own, *reversed(early)], shifted[planes // 2 - 1:]
    steps = list(range(planes))
    first, last = steps[:planes // 2], steps[planes // 2:]
    packed = pack(first, planes, theirs, early)
    first_far = swap_sides(packed)
    *late, _ = lax.optimization_barrier((*late, packed))
    last_far = swap_sides(pack(last, planes, theirs, late))
    near_tiles = score(near_kernel, planes, planes, False, clean, slots, picks, clean, *early, *late)
    first_far, near_tiles = lax.optimization_barrier((first_far, near_tiles))
    far_tiles = score(
        functools.partial(some_far_kernel, first, planes), len(first), len(first), True, clean, slots, clean, first_far
    )
    last_far, far_tiles = lax.optimization_barrier((last_far, far_tiles))
    return score(
        functools.partial(last_far_kernel, last, planes), shards, len(last), True, clean,
        slots, clean, last_far, near_tiles, far_tiles,
    )


def by_gather(own, shards, candidates, lengths, passages):
    slots, picks, clean = prepare(shards, candidates, lengths, passages)
    gathered = lax.all_gather(own, "psg", axis=0)
    some = min(shards, 8)

    def score_some(items):
        return score(all_kernel, some, some, False, clean, items[0], items[1], clean, items[2])

    parts = [x.reshape(shards // some, some, *x.shape[1:]) for x in (slots, picks, gathered)]
    return lax.map(score_some, parts).reshape(shards, QB + 1, LANES)


def per_device(queries, passages, lengths, candidates):
    shards = lax.axis_size("psg")
    rows = passages.shape[0] // PBS
    form = by_planes if shards == 8 else by_gather
    tiles = form(
        queries.reshape(QBD * QB * QT, DIM), shards, candidates.reshape(rows, KB), lengths, passages
    )
    tiles = lax.all_to_all(tiles, "psg", split_axis=0, concat_axis=0, tiled=True)
    return place(tiles, rows * KB // shards).transpose(0, 3, 1, 2)[None]


def solution(mesh):
    return jax.shard_map(
        per_device,
        mesh=mesh,
        in_specs=(
            P(("grp", "psg", "qry"), None, None),
            P(("grp", "psg"), None, None),
            P(("grp", "psg")),
            P("qry", ("grp", "psg"), None),
        ),
        out_specs=P(("grp", "psg", "qry"), None, None, None, None),
        check_vma=False,
    )
```

```python
import functools

import jax
import jax.numpy as jnp
from jax import lax
from jax.experimental import pallas as pl
from jax.experimental.pallas import tpu as pltpu
from jax.sharding import PartitionSpec as P

DIM = 128
QT = 32
PT = 64
QB = 2
QBD = 4
PBS = 16
KB = 32
LANES = 128
GROUP = 8


def prepare_kernel(
    cand_hbm, len_hbm, p_hbm, slots_ref, picks_ref, clean_ref, cand_ref, len_ref, raw_ref, sems
):
    rows = cand_ref.shape[0]
    shards = slots_ref.shape[0]
    groups = p_hbm.shape[0] // GROUP

    def fetch(g):
        part = pl.ds(g * GROUP, GROUP)
        return pltpu.make_async_copy(p_hbm.at[part], raw_ref.at[part], sems.at[g])

    fetch_cand = pltpu.make_async_copy(cand_hbm, cand_ref, sems.at[groups])
    fetch_len = pltpu.make_async_copy(len_hbm, len_ref, sems.at[groups + 1])
    fetch_cand.start()
    fetch_len.start()
    for g in range(groups):
        fetch(g).start()

    fetch_cand.wait()
    cand = cand_ref[...]
    owner = cand // QBD
    block = cand - owner * QBD
    lane = lax.broadcasted_iota(jnp.int32, (rows, LANES), 1).astype(jnp.float32)
    sub = lax.broadcasted_iota(jnp.int32, (rows, LANES), 0)
    for o in range(shards):
        mine = owner == o
        named = jnp.max(jnp.where(mine, block, 0), axis=1, keepdims=True)
        picks_ref[o:o + 1, :] = jnp.broadcast_to(jnp.max(named, axis=0, keepdims=True), (1, LANES))
        named_here = jnp.sum(jnp.where(mine, 1.0, 0.0), axis=1, keepdims=True)
        upto = jnp.broadcast_to(named_here, (rows, LANES))
        step = 1
        while step < rows:
            upto = upto + jnp.where(sub >= step, pltpu.roll(upto, step, 0), 0.0)
            step *= 2
        slots_ref[o:o + 1, :] = jnp.sum(jnp.where(upto <= lane, 1.0, 0.0), axis=0, keepdims=True)

    fetch_len.wait()
    u = lax.broadcasted_iota(jnp.int32, (PT, LANES), 0)

    @pl.loop(0, groups)
    def _(g):
        fetch(g).wait()
        for i in range(GROUP):
            p = g * GROUP + i
            tokens = raw_ref[p].astype(jnp.float32)
            clean_ref[p] = jnp.where(u < len_ref[p], tokens, tokens[0:1]).astype(jnp.bfloat16)


def prepare(shards, candidates, lengths, passages):
    hbm = pl.BlockSpec(memory_space=pltpu.HBM)
    vmem = pl.BlockSpec(memory_space=pltpu.VMEM)
    operands = [pltpu.with_memory_space_constraint(x, pltpu.HBM) for x in (candidates, lengths, passages)]
    return pl.pallas_call(
        prepare_kernel,
        out_shape=[
            jax.ShapeDtypeStruct((shards, LANES), jnp.float32),
            jax.ShapeDtypeStruct((shards, LANES), jnp.int32),
            jax.ShapeDtypeStruct(passages.shape, passages.dtype),
        ],
        in_specs=[hbm] * 3,
        out_specs=[vmem] * 3,
        scratch_shapes=[
            pltpu.VMEM(candidates.shape, candidates.dtype),
            pltpu.SMEM(lengths.shape, lengths.dtype),
            pltpu.VMEM(passages.shape, passages.dtype),
            pltpu.SemaphoreType.DMA((passages.shape[0] // GROUP + 2,)),
        ],
        compiler_params=pltpu.CompilerParams(vmem_limit_bytes=24 * 1024 * 1024),
        cost_estimate=pl.CostEstimate(flops=passages.size, bytes_accessed=2 * passages.size, transcendentals=0),
    )(*operands)


def near_owner(me, step, planes):
    return lax.rem((me >> 1) + planes - step, planes) << 1 | me & 1


def picked(picks_ref, owner, q_ref):
    pick = jnp.max(picks_ref[pl.ds(owner, 1), :])
    return q_ref[pl.ds(pick * QB * QT, QB * QT), :]


def pack_kernel(steps, planes, cand_ref, *refs):
    q_refs, out_ref = refs[:-1], refs[-1]
    me = lax.axis_index("psg")
    cand = cand_ref[...]
    owner = cand // QBD
    block = cand - owner * QBD
    for n, step in enumerate(steps):
        pick = jnp.max(jnp.where(owner == near_owner(me, step, planes), block, 0))
        out_ref[n * QB * QT:(n + 1) * QB * QT, :] = q_refs[n][pl.ds(pick * QB * QT, QB * QT), :]


def pack(steps, planes, candidates, blocks):
    vmem = pl.BlockSpec(memory_space=pltpu.VMEM)
    return pl.pallas_call(
        functools.partial(pack_kernel, steps, planes),
        out_shape=jax.ShapeDtypeStruct((len(blocks) * QB * QT, DIM), blocks[0].dtype),
        in_specs=[vmem] * (1 + len(blocks)),
        out_specs=vmem,
        compiler_params=pltpu.CompilerParams(vmem_limit_bytes=4 * 1024 * 1024),
    )(candidates, *blocks)


def sum_tokens(best):
    tokens = best.shape[1]
    high = best.astype(jnp.bfloat16)
    rest = best - high.astype(jnp.float32)
    mid = rest.astype(jnp.bfloat16)
    low = (rest - mid.astype(jnp.float32)).astype(jnp.bfloat16)
    parts = jnp.concatenate([low, mid, high], axis=1)
    query = lax.broadcasted_iota(jnp.int32, (tokens // QT, tokens), 0)
    token = lax.broadcasted_iota(jnp.int32, (tokens // QT, tokens), 1)
    ones = jnp.where(token // QT == query, 1.0, 0.0).astype(jnp.bfloat16)
    total = lax.dot_general(
        jnp.concatenate([ones] * 3, axis=1), parts, (((1,), (1,)), ((), ())), preferred_element_type=jnp.float32
    )
    return total * (1.0 / QT)


def best_tokens(left_of, sel, max_ref):
    count, tokens = max_ref.shape
    piece = 2 * GROUP
    for g in range(0, count, piece):
        dots = lax.dot_general(left_of(g, piece), sel, (((1,), (1,)), ((), ())), preferred_element_type=jnp.float32)
        max_ref[g:g + piece, :] = jnp.max(dots.reshape(piece, PT, tokens), axis=1)
    return max_ref[...]


def score_picked(sel, p_ref, max_ref):
    def left_of(g, piece):
        return p_ref[g:g + piece].reshape(piece * PT, DIM)

    return sum_tokens(best_tokens(left_of, sel, max_ref))


def score_picked_few(sel, p_ref, wide_ref, max_ref):
    tokens, half = sel.shape[0], p_ref.shape[0] // 2
    wide_ref[...] = jnp.zeros_like(wide_ref)
    wide_ref[0:tokens, 0:DIM] = sel
    wide_ref[tokens:, DIM:] = sel

    def left_of(g, piece):
        return jnp.concatenate(
            [p_ref[h + g:h + g + piece].reshape(piece * PT, DIM) for h in (0, half)], axis=1
        )

    total = sum_tokens(best_tokens(left_of, wide_ref[...], max_ref))
    queries = tokens // QT
    return jnp.concatenate([total[:queries], total[queries:]], axis=1)


def put(out_ref, place, total, n, slots_ref, owner):
    out_ref[place, 0:QB, :] = total[n * QB:(n + 1) * QB]
    out_ref[place, QB:QB + 1, :] = slots_ref[pl.ds(owner, 1), :]


def near_kernel(slots_ref, picks_ref, p_ref, *refs):
    q_refs, (out_ref, sel_ref, max_ref) = refs[:-3], refs[-3:]
    me = lax.axis_index("psg")
    owners = [near_owner(me, n, len(q_refs)) for n in range(len(q_refs))]
    for n, owner in enumerate(owners):
        sel_ref[n * QB * QT:(n + 1) * QB * QT, :] = picked(picks_ref, owner, q_refs[n])
    total = score_picked(sel_ref[...], p_ref, max_ref)
    for n, owner in enumerate(owners):
        put(out_ref, n, total, n, slots_ref, owner)


def some_far_kernel(steps, planes, slots_ref, p_ref, sel_ref, out_ref, wide_ref, max_ref):
    me = lax.axis_index("psg")
    total = score_picked_few(sel_ref[...], p_ref, wide_ref, max_ref)
    for n, step in enumerate(steps):
        put(out_ref, n, total, n, slots_ref, near_owner(me, step, planes) ^ 1)


def last_far_kernel(steps, planes, slots_ref, p_ref, sel_ref, near_ref, far_ref, out_ref, wide_ref, max_ref):
    me = lax.axis_index("psg")
    total = score_picked_few(sel_ref[...], p_ref, wide_ref, max_ref)
    for n, step in enumerate(steps):
        owner = near_owner(me, step, planes) ^ 1
        put(out_ref, owner, total, n, slots_ref, owner)
    others = [step for step in range(planes) if step not in steps]
    for step in range(planes):
        out_ref[near_owner(me, step, planes)] = near_ref[step]
    for n, step in enumerate(others):
        out_ref[near_owner(me, step, planes) ^ 1] = far_ref[n]


def all_kernel(slots_ref, picks_ref, p_ref, q_ref, out_ref, sel_ref, max_ref):
    some = q_ref.shape[0]
    for n in range(some):
        sel_ref[n * QB * QT:(n + 1) * QB * QT, :] = picked(picks_ref, n, q_ref.at[n])
    total = score_picked(sel_ref[...], p_ref, max_ref)
    for n in range(some):
        put(out_ref, n, total, n, slots_ref, n)


def score(kernel, tiles, some, few, passages, *more):
    count, tokens = passages.shape[0], some * QB * QT
    vmem = pl.BlockSpec(memory_space=pltpu.VMEM)
    if few:
        scratch = [pltpu.VMEM((2 * tokens, 2 * DIM), jnp.bfloat16), pltpu.VMEM((count // 2, 2 * tokens), jnp.float32)]
    else:
        scratch = [pltpu.VMEM((tokens, DIM), jnp.bfloat16), pltpu.VMEM((count, tokens), jnp.float32)]
    return pl.pallas_call(
        kernel,
        out_shape=jax.ShapeDtypeStruct((tiles, QB + 1, LANES), jnp.float32),
        in_specs=[vmem] * len(more),
        out_specs=vmem,
        scratch_shapes=scratch,
        compiler_params=pltpu.CompilerParams(vmem_limit_bytes=32 * 1024 * 1024),
        cost_estimate=pl.CostEstimate(
            flops=2 * passages.size * tokens, bytes_accessed=2 * passages.size, transcendentals=0
        ),
    )(*more)


def place_kernel(in_ref, out_ref):
    slots = out_ref.shape[-1]
    m = lax.broadcasted_iota(jnp.int32, (PBS, LANES), 0)
    for j in range(in_ref.shape[0]):
        row = in_ref[j, QB:QB + 1, :].astype(jnp.int32)
        where = jnp.minimum(row * PBS, LANES - PBS) + m
        for i in range(QB):
            tile = jnp.broadcast_to(in_ref[j, i:i + 1, :], (PBS, LANES))
            out_ref[j, i] = jnp.take_along_axis(tile, where, axis=1)[:, :slots]


def place(tiles, slots):
    vmem = pl.BlockSpec(memory_space=pltpu.VMEM)
    shards = tiles.shape[0]
    return pl.pallas_call(
        place_kernel,
        out_shape=jax.ShapeDtypeStruct((shards, QB, PBS, slots), jnp.float32),
        in_specs=[vmem],
        out_specs=vmem,
        compiler_params=pltpu.CompilerParams(vmem_limit_bytes=8 * 1024 * 1024),
    )(tiles)


def by_planes(own, shards, candidates, lengths, passages):
    planes = shards // 2

    def swap_sides(x):
        return lax.ppermute(x, "psg", [(j, j ^ 1) for j in range(shards)])

    def shift(x, step):
        return lax.ppermute(x, "psg", [(j, (j + 2 * step) % shards) for j in range(shards)])

    theirs = swap_sides(candidates)
    shifted = [shift(own, step) for step in range(1, planes)]
    slots, picks, clean = prepare(shards, candidates, lengths, passages)
    first = [0, planes // 2]
    last = [step for step in range(planes) if step not in first]
    clean, shifted[first[1] - 1] = lax.optimization_barrier((clean, shifted[first[1] - 1]))
    blocks = [own, *shifted]
    packed = pack(first, planes, theirs, [blocks[step] for step in first])
    first_far = swap_sides(packed)
    *late, _ = lax.optimization_barrier((*[blocks[step] for step in reversed(last)], packed))
    for step, block in zip(reversed(last), late):
        blocks[step] = block
    last_far = swap_sides(pack(last, planes, theirs, [blocks[step] for step in last]))
    near_tiles = score(near_kernel, planes, planes, False, clean, slots, picks, clean, *blocks)
    first_far, near_tiles = lax.optimization_barrier((first_far, near_tiles))
    far_tiles = score(
        functools.partial(some_far_kernel, first, planes), len(first), len(first), True, clean, slots, clean, first_far
    )
    last_far, far_tiles = lax.optimization_barrier((last_far, far_tiles))
    return score(
        functools.partial(last_far_kernel, last, planes), shards, len(last), True, clean,
        slots, clean, last_far, near_tiles, far_tiles,
    )


def by_gather(own, shards, candidates, lengths, passages):
    slots, picks, clean = prepare(shards, candidates, lengths, passages)
    gathered = lax.all_gather(own, "psg", axis=0)
    some = min(shards, 8)

    def score_some(items):
        return score(all_kernel, some, some, False, clean, items[0], items[1], clean, items[2])

    parts = [x.reshape(shards // some, some, *x.shape[1:]) for x in (slots, picks, gathered)]
    return lax.map(score_some, parts).reshape(shards, QB + 1, LANES)


def per_device(queries, passages, lengths, candidates):
    shards = lax.axis_size("psg")
    rows = passages.shape[0] // PBS
    form = by_planes if shards == 8 else by_gather
    tiles = form(
        queries.reshape(QBD * QB * QT, DIM), shards, candidates.reshape(rows, KB), lengths, passages
    )
    tiles = lax.all_to_all(tiles, "psg", split_axis=0, concat_axis=0, tiled=True)
    return place(tiles, rows * KB // shards).transpose(0, 3, 1, 2)[None]


def solution(mesh):
    return jax.shard_map(
        per_device,
        mesh=mesh,
        in_specs=(
            P(("grp", "psg", "qry"), None, None),
            P(("grp", "psg"), None, None),
            P(("grp", "psg")),
            P("qry", ("grp", "psg"), None),
        ),
        out_specs=P(("grp", "psg", "qry"), None, None, None, None),
        check_vma=False,
    )
```

```python
import functools

import jax
import jax.numpy as jnp
from jax import lax
from jax.experimental import pallas as pl
from jax.experimental.pallas import tpu as pltpu
from jax.sharding import PartitionSpec as P

DIM = 128
QT = 32
PT = 64
QB = 2
QBD = 4
PBS = 16
KB = 32
LANES = 128
GROUP = 8


def prepare_kernel(
    cand_hbm, len_hbm, p_hbm, slots_ref, picks_ref, clean_ref, cand_ref, len_ref, raw_ref, sems
):
    rows = cand_ref.shape[0]
    shards = slots_ref.shape[0]
    groups = p_hbm.shape[0] // GROUP

    def fetch(g):
        part = pl.ds(g * GROUP, GROUP)
        return pltpu.make_async_copy(p_hbm.at[part], raw_ref.at[part], sems.at[g])

    fetch_cand = pltpu.make_async_copy(cand_hbm, cand_ref, sems.at[groups])
    fetch_len = pltpu.make_async_copy(len_hbm, len_ref, sems.at[groups + 1])
    fetch_cand.start()
    fetch_len.start()
    for g in range(groups):
        fetch(g).start()

    fetch_cand.wait()
    cand = cand_ref[...]
    owner = cand // QBD
    block = cand - owner * QBD
    lane = lax.broadcasted_iota(jnp.int32, (rows, LANES), 1).astype(jnp.float32)
    sub = lax.broadcasted_iota(jnp.int32, (rows, LANES), 0)
    for o in range(shards):
        mine = owner == o
        named = jnp.max(jnp.where(mine, block, 0), axis=1, keepdims=True)
        picks_ref[o:o + 1, :] = jnp.broadcast_to(jnp.max(named, axis=0, keepdims=True), (1, LANES))
        named_here = jnp.sum(jnp.where(mine, 1.0, 0.0), axis=1, keepdims=True)
        upto = jnp.broadcast_to(named_here, (rows, LANES))
        step = 1
        while step < rows:
            upto = upto + jnp.where(sub >= step, pltpu.roll(upto, step, 0), 0.0)
            step *= 2
        slots_ref[o:o + 1, :] = jnp.sum(jnp.where(upto <= lane, 1.0, 0.0), axis=0, keepdims=True)

    fetch_len.wait()
    u = lax.broadcasted_iota(jnp.int32, (PT, LANES), 0)

    @pl.loop(0, groups)
    def _(g):
        fetch(g).wait()
        for i in range(GROUP):
            p = g * GROUP + i
            tokens = raw_ref[p].astype(jnp.float32)
            clean_ref[p] = jnp.where(u < len_ref[p], tokens, tokens[0:1]).astype(jnp.bfloat16)


def prepare(shards, candidates, lengths, passages):
    hbm = pl.BlockSpec(memory_space=pltpu.HBM)
    vmem = pl.BlockSpec(memory_space=pltpu.VMEM)
    operands = [pltpu.with_memory_space_constraint(x, pltpu.HBM) for x in (candidates, lengths, passages)]
    return pl.pallas_call(
        prepare_kernel,
        out_shape=[
            jax.ShapeDtypeStruct((shards, LANES), jnp.float32),
            jax.ShapeDtypeStruct((shards, LANES), jnp.int32),
            jax.ShapeDtypeStruct(passages.shape, passages.dtype),
        ],
        in_specs=[hbm] * 3,
        out_specs=[vmem] * 3,
        scratch_shapes=[
            pltpu.VMEM(candidates.shape, candidates.dtype),
            pltpu.SMEM(lengths.shape, lengths.dtype),
            pltpu.VMEM(passages.shape, passages.dtype),
            pltpu.SemaphoreType.DMA((passages.shape[0] // GROUP + 2,)),
        ],
        compiler_params=pltpu.CompilerParams(vmem_limit_bytes=24 * 1024 * 1024),
        cost_estimate=pl.CostEstimate(flops=passages.size, bytes_accessed=2 * passages.size, transcendentals=0),
    )(*operands)


def near_owner(me, step, planes):
    return lax.rem((me >> 1) + planes - step, planes) << 1 | me & 1


def picked(picks_ref, owner, q_ref):
    pick = jnp.max(picks_ref[pl.ds(owner, 1), :])
    return q_ref[pl.ds(pick * QB * QT, QB * QT), :]


def pack_kernel(steps, planes, cand_ref, *refs):
    q_refs, out_ref = refs[:-1], refs[-1]
    me = lax.axis_index("psg")
    cand = cand_ref[...]
    owner = cand // QBD
    block = cand - owner * QBD
    for n, step in enumerate(steps):
        pick = jnp.max(jnp.where(owner == near_owner(me, step, planes), block, 0))
        out_ref[n * QB * QT:(n + 1) * QB * QT, :] = q_refs[n][pl.ds(pick * QB * QT, QB * QT), :]


def pack(steps, planes, candidates, blocks):
    vmem = pl.BlockSpec(memory_space=pltpu.VMEM)
    return pl.pallas_call(
        functools.partial(pack_kernel, steps, planes),
        out_shape=jax.ShapeDtypeStruct((len(blocks) * QB * QT, DIM), blocks[0].dtype),
        in_specs=[vmem] * (1 + len(blocks)),
        out_specs=vmem,
        compiler_params=pltpu.CompilerParams(vmem_limit_bytes=4 * 1024 * 1024),
    )(candidates, *blocks)


def sum_tokens(best):
    tokens = best.shape[1]
    high = best.astype(jnp.bfloat16)
    low = (best - high.astype(jnp.float32)).astype(jnp.bfloat16)
    parts = jnp.concatenate([low, high], axis=1)
    query = lax.broadcasted_iota(jnp.int32, (tokens // QT, tokens), 0)
    token = lax.broadcasted_iota(jnp.int32, (tokens // QT, tokens), 1)
    ones = jnp.where(token // QT == query, 1.0, 0.0).astype(jnp.bfloat16)
    total = lax.dot_general(
        jnp.concatenate([ones] * 2, axis=1), parts, (((1,), (1,)), ((), ())), preferred_element_type=jnp.float32
    )
    return total * (1.0 / QT)


def best_tokens(left_of, sel, max_ref, piece):
    count, tokens = max_ref.shape
    for g in range(0, count, piece):
        dots = lax.dot_general(left_of(g, piece), sel, (((1,), (1,)), ((), ())), preferred_element_type=jnp.float32)
        max_ref[g:g + piece, :] = jnp.max(dots.reshape(piece, PT, tokens), axis=1)
    return max_ref[...]


def score_picked(sel, p_ref, max_ref):
    def left_of(g, piece):
        return p_ref[g:g + piece].reshape(piece * PT, DIM)

    return sum_tokens(best_tokens(left_of, sel, max_ref, 2 * GROUP))


def score_picked_few(sel, p_ref, wide_ref, max_ref):
    tokens, half = sel.shape[0], p_ref.shape[0] // 2
    wide_ref[...] = jnp.zeros_like(wide_ref)
    wide_ref[0:tokens, 0:DIM] = sel
    wide_ref[tokens:, DIM:] = sel

    def left_of(g, piece):
        return jnp.concatenate(
            [p_ref[h + g:h + g + piece].reshape(piece * PT, DIM) for h in (0, half)], axis=1
        )

    total = sum_tokens(best_tokens(left_of, wide_ref[...], max_ref, GROUP))
    queries = tokens // QT
    return jnp.concatenate([total[:queries], total[queries:]], axis=1)


def put(out_ref, place, total, n, slots_ref, owner):
    out_ref[place, 0:QB, :] = total[n * QB:(n + 1) * QB]
    out_ref[place, QB:QB + 1, :] = slots_ref[pl.ds(owner, 1), :]


def near_kernel(slots_ref, picks_ref, p_ref, *refs):
    q_refs, (out_ref, sel_ref, max_ref) = refs[:-3], refs[-3:]
    me = lax.axis_index("psg")
    owners = [near_owner(me, n, len(q_refs)) for n in range(len(q_refs))]
    for n, owner in enumerate(owners):
        sel_ref[n * QB * QT:(n + 1) * QB * QT, :] = picked(picks_ref, owner, q_refs[n])
    total = score_picked(sel_ref[...], p_ref, max_ref)
    for n, owner in enumerate(owners):
        put(out_ref, n, total, n, slots_ref, owner)


def some_far_kernel(steps, planes, slots_ref, p_ref, sel_ref, out_ref, wide_ref, max_ref):
    me = lax.axis_index("psg")
    total = score_picked_few(sel_ref[...], p_ref, wide_ref, max_ref)
    for n, step in enumerate(steps):
        put(out_ref, n, total, n, slots_ref, near_owner(me, step, planes) ^ 1)


def last_far_kernel(steps, planes, slots_ref, p_ref, sel_ref, near_ref, far_ref, out_ref, wide_ref, max_ref):
    me = lax.axis_index("psg")
    total = score_picked_few(sel_ref[...], p_ref, wide_ref, max_ref)
    for n, step in enumerate(steps):
        owner = near_owner(me, step, planes) ^ 1
        put(out_ref, owner, total, n, slots_ref, owner)
    others = [step for step in range(planes) if step not in steps]
    for step in range(planes):
        out_ref[near_owner(me, step, planes)] = near_ref[step]
    for n, step in enumerate(others):
        out_ref[near_owner(me, step, planes) ^ 1] = far_ref[n]


def all_kernel(slots_ref, picks_ref, p_ref, q_ref, out_ref, sel_ref, max_ref):
    some = q_ref.shape[0]
    for n in range(some):
        sel_ref[n * QB * QT:(n + 1) * QB * QT, :] = picked(picks_ref, n, q_ref.at[n])
    total = score_picked(sel_ref[...], p_ref, max_ref)
    for n in range(some):
        put(out_ref, n, total, n, slots_ref, n)


def score(kernel, tiles, some, few, passages, *more):
    count, tokens = passages.shape[0], some * QB * QT
    vmem = pl.BlockSpec(memory_space=pltpu.VMEM)
    if few:
        scratch = [pltpu.VMEM((2 * tokens, 2 * DIM), jnp.bfloat16), pltpu.VMEM((count // 2, 2 * tokens), jnp.float32)]
    else:
        scratch = [pltpu.VMEM((tokens, DIM), jnp.bfloat16), pltpu.VMEM((count, tokens), jnp.float32)]
    return pl.pallas_call(
        kernel,
        out_shape=jax.ShapeDtypeStruct((tiles, QB + 1, LANES), jnp.float32),
        in_specs=[vmem] * len(more),
        out_specs=vmem,
        scratch_shapes=scratch,
        compiler_params=pltpu.CompilerParams(vmem_limit_bytes=32 * 1024 * 1024),
        cost_estimate=pl.CostEstimate(
            flops=2 * passages.size * tokens, bytes_accessed=2 * passages.size, transcendentals=0
        ),
    )(*more)


def place_kernel(in_ref, out_ref):
    slots = out_ref.shape[-1]
    m = lax.broadcasted_iota(jnp.int32, (PBS, LANES), 0)
    for j in range(in_ref.shape[0]):
        row = in_ref[j, QB:QB + 1, :].astype(jnp.int32)
        where = jnp.minimum(row * PBS, LANES - PBS) + m
        for i in range(QB):
            tile = jnp.broadcast_to(in_ref[j, i:i + 1, :], (PBS, LANES))
            out_ref[j, i] = jnp.take_along_axis(tile, where, axis=1)[:, :slots]


def place(tiles, slots):
    vmem = pl.BlockSpec(memory_space=pltpu.VMEM)
    shards = tiles.shape[0]
    return pl.pallas_call(
        place_kernel,
        out_shape=jax.ShapeDtypeStruct((shards, QB, PBS, slots), jnp.float32),
        in_specs=[vmem],
        out_specs=vmem,
        compiler_params=pltpu.CompilerParams(vmem_limit_bytes=8 * 1024 * 1024),
    )(tiles)


def by_planes(own, shards, candidates, lengths, passages):
    planes = shards // 2

    def swap_sides(x):
        return lax.ppermute(x, "psg", [(j, j ^ 1) for j in range(shards)])

    def shift(x, step):
        return lax.ppermute(x, "psg", [(j, (j + 2 * step) % shards) for j in range(shards)])

    theirs = swap_sides(candidates)
    shifted = [shift(own, step) for step in range(1, planes)]
    slots, picks, clean = prepare(shards, candidates, lengths, passages)
    clean, *early = lax.optimization_barrier((clean, *reversed(shifted[:planes // 2 - 1])))
    early, late = [own, *reversed(early)], shifted[planes // 2 - 1:]
    steps = list(range(planes))
    first, last = steps[:planes // 2], steps[planes // 2:]
    packed = pack(first, planes, theirs, early)
    first_far = swap_sides(packed)
    *late, _ = lax.optimization_barrier((*reversed(late), packed))
    late = late[::-1]
    last_far = swap_sides(pack(last, planes, theirs, late))
    near_tiles = score(near_kernel, planes, planes, False, clean, slots, picks, clean, *early, *late)
    first_far, near_tiles = lax.optimization_barrier((first_far, near_tiles))
    far_tiles = score(
        functools.partial(some_far_kernel, first, planes), len(first), len(first), True, clean, slots, clean, first_far
    )
    last_far, far_tiles = lax.optimization_barrier((last_far, far_tiles))
    return score(
        functools.partial(last_far_kernel, last, planes), shards, len(last), True, clean,
        slots, clean, last_far, near_tiles, far_tiles,
    )


def by_gather(own, shards, candidates, lengths, passages):
    slots, picks, clean = prepare(shards, candidates, lengths, passages)
    gathered = lax.all_gather(own, "psg", axis=0)
    some = min(shards, 8)

    def score_some(items):
        return score(all_kernel, some, some, False, clean, items[0], items[1], clean, items[2])

    parts = [x.reshape(shards // some, some, *x.shape[1:]) for x in (slots, picks, gathered)]
    return lax.map(score_some, parts).reshape(shards, QB + 1, LANES)


def per_device(queries, passages, lengths, candidates):
    shards = lax.axis_size("psg")
    rows = passages.shape[0] // PBS
    form = by_planes if shards == 8 else by_gather
    tiles = form(
        queries.reshape(QBD * QB * QT, DIM), shards, candidates.reshape(rows, KB), lengths, passages
    )
    tiles = lax.all_to_all(tiles, "psg", split_axis=0, concat_axis=0, tiled=True)
    return place(tiles, rows * KB // shards).transpose(0, 3, 1, 2)[None]


def solution(mesh):
    return jax.shard_map(
        per_device,
        mesh=mesh,
        in_specs=(
            P(("grp", "psg", "qry"), None, None),
            P(("grp", "psg"), None, None),
            P(("grp", "psg")),
            P("qry", ("grp", "psg"), None),
        ),
        out_specs=P(("grp", "psg", "qry"), None, None, None, None),
        check_vma=False,
    )
```

```python
import functools

import jax
import jax.numpy as jnp
from jax import lax
from jax.experimental import pallas as pl
from jax.experimental.pallas import tpu as pltpu
from jax.sharding import PartitionSpec as P

DIM = 128
QT = 32
PT = 64
QB = 2
QBD = 4
PBS = 16
KB = 32
LANES = 128
GROUP = 8


def prepare_kernel(
    cand_hbm, len_hbm, p_hbm, slots_ref, picks_ref, clean_ref, cand_ref, len_ref, raw_ref, sems
):
    rows = cand_ref.shape[0]
    shards = slots_ref.shape[0]
    groups = p_hbm.shape[0] // GROUP

    def fetch(g):
        part = pl.ds(g * GROUP, GROUP)
        return pltpu.make_async_copy(p_hbm.at[part], raw_ref.at[part], sems.at[g])

    fetch_cand = pltpu.make_async_copy(cand_hbm, cand_ref, sems.at[groups])
    fetch_len = pltpu.make_async_copy(len_hbm, len_ref, sems.at[groups + 1])
    fetch_cand.start()
    fetch_len.start()
    for g in range(groups):
        fetch(g).start()

    fetch_cand.wait()
    cand = cand_ref[...]
    owner = cand // QBD
    block = cand - owner * QBD
    lane = lax.broadcasted_iota(jnp.int32, (rows, LANES), 1).astype(jnp.float32)
    sub = lax.broadcasted_iota(jnp.int32, (rows, LANES), 0)
    for o in range(shards):
        mine = owner == o
        named = jnp.max(jnp.where(mine, block, 0), axis=1, keepdims=True)
        picks_ref[o:o + 1, :] = jnp.broadcast_to(jnp.max(named, axis=0, keepdims=True), (1, LANES))
        named_here = jnp.sum(jnp.where(mine, 1.0, 0.0), axis=1, keepdims=True)
        upto = jnp.broadcast_to(named_here, (rows, LANES))
        step = 1
        while step < rows:
            upto = upto + jnp.where(sub >= step, pltpu.roll(upto, step, 0), 0.0)
            step *= 2
        slots_ref[o:o + 1, :] = jnp.sum(jnp.where(upto <= lane, 1.0, 0.0), axis=0, keepdims=True)

    fetch_len.wait()
    u = lax.broadcasted_iota(jnp.int32, (PT, LANES), 0)

    @pl.loop(0, groups)
    def _(g):
        fetch(g).wait()
        for i in range(GROUP):
            p = g * GROUP + i
            tokens = raw_ref[p].astype(jnp.float32)
            clean_ref[p] = jnp.where(u < len_ref[p], tokens, tokens[0:1]).astype(jnp.bfloat16)


def prepare(shards, candidates, lengths, passages):
    hbm = pl.BlockSpec(memory_space=pltpu.HBM)
    vmem = pl.BlockSpec(memory_space=pltpu.VMEM)
    operands = [pltpu.with_memory_space_constraint(x, pltpu.HBM) for x in (candidates, lengths, passages)]
    return pl.pallas_call(
        prepare_kernel,
        out_shape=[
            jax.ShapeDtypeStruct((shards, LANES), jnp.float32),
            jax.ShapeDtypeStruct((shards, LANES), jnp.int32),
            jax.ShapeDtypeStruct(passages.shape, passages.dtype),
        ],
        in_specs=[hbm] * 3,
        out_specs=[vmem] * 3,
        scratch_shapes=[
            pltpu.VMEM(candidates.shape, candidates.dtype),
            pltpu.SMEM(lengths.shape, lengths.dtype),
            pltpu.VMEM(passages.shape, passages.dtype),
            pltpu.SemaphoreType.DMA((passages.shape[0] // GROUP + 2,)),
        ],
        compiler_params=pltpu.CompilerParams(vmem_limit_bytes=24 * 1024 * 1024),
        cost_estimate=pl.CostEstimate(flops=passages.size, bytes_accessed=2 * passages.size, transcendentals=0),
    )(*operands)


def near_owner(me, step, planes):
    return lax.rem((me >> 1) + planes - step, planes) << 1 | me & 1


def picked(picks_ref, owner, q_ref):
    pick = jnp.max(picks_ref[pl.ds(owner, 1), :])
    return q_ref[pl.ds(pick * QB * QT, QB * QT), :]


def pack_kernel(steps, planes, cand_ref, *refs):
    q_refs, out_ref = refs[:-1], refs[-1]
    me = lax.axis_index("psg")
    cand = cand_ref[...]
    owner = cand // QBD
    block = cand - owner * QBD
    for n, step in enumerate(steps):
        pick = jnp.max(jnp.where(owner == near_owner(me, step, planes), block, 0))
        out_ref[n * QB * QT:(n + 1) * QB * QT, :] = q_refs[n][pl.ds(pick * QB * QT, QB * QT), :]


def pack(steps, planes, candidates, blocks):
    vmem = pl.BlockSpec(memory_space=pltpu.VMEM)
    return pl.pallas_call(
        functools.partial(pack_kernel, steps, planes),
        out_shape=jax.ShapeDtypeStruct((len(blocks) * QB * QT, DIM), blocks[0].dtype),
        in_specs=[vmem] * (1 + len(blocks)),
        out_specs=vmem,
        compiler_params=pltpu.CompilerParams(vmem_limit_bytes=4 * 1024 * 1024),
    )(candidates, *blocks)


def sum_tokens(best):
    tokens = best.shape[1]
    high = best.astype(jnp.bfloat16)
    rest = best - high.astype(jnp.float32)
    mid = rest.astype(jnp.bfloat16)
    low = (rest - mid.astype(jnp.float32)).astype(jnp.bfloat16)
    parts = jnp.concatenate([low, mid, high], axis=1)
    query = lax.broadcasted_iota(jnp.int32, (tokens // QT, tokens), 0)
    token = lax.broadcasted_iota(jnp.int32, (tokens // QT, tokens), 1)
    ones = jnp.where(token // QT == query, 1.0, 0.0).astype(jnp.bfloat16)
    total = lax.dot_general(
        jnp.concatenate([ones] * 3, axis=1), parts, (((1,), (1,)), ((), ())), preferred_element_type=jnp.float32
    )
    return total * (1.0 / QT)


def best_tokens(left_of, sel, max_ref, piece):
    count, tokens = max_ref.shape
    for g in range(0, count, piece):
        dots = lax.dot_general(left_of(g, piece), sel, (((1,), (1,)), ((), ())), preferred_element_type=jnp.float32)
        max_ref[g:g + piece, :] = jnp.max(dots.reshape(piece, PT, tokens), axis=1)
    return max_ref[...]


def score_picked(sel, p_ref, max_ref):
    def left_of(g, piece):
        return p_ref[g:g + piece].reshape(piece * PT, DIM)

    return sum_tokens(best_tokens(left_of, sel, max_ref, 2 * GROUP))


def score_picked_few(sel, p_ref, wide_ref, max_ref):
    tokens, half = sel.shape[0], p_ref.shape[0] // 2
    wide_ref[...] = jnp.zeros_like(wide_ref)
    wide_ref[0:tokens, 0:DIM] = sel
    wide_ref[tokens:, DIM:] = sel

    def left_of(g, piece):
        return jnp.concatenate(
            [p_ref[h + g:h + g + piece].reshape(piece * PT, DIM) for h in (0, half)], axis=1
        )

    total = sum_tokens(best_tokens(left_of, wide_ref[...], max_ref, GROUP))
    queries = tokens // QT
    return jnp.concatenate([total[:queries], total[queries:]], axis=1)


def put(out_ref, place, total, n, slots_ref, owner):
    out_ref[place, 0:QB, :] = total[n * QB:(n + 1) * QB]
    out_ref[place, QB:QB + 1, :] = slots_ref[pl.ds(owner, 1), :]


def near_kernel(slots_ref, picks_ref, p_ref, *refs):
    q_refs, (out_ref, sel_ref, max_ref) = refs[:-3], refs[-3:]
    me = lax.axis_index("psg")
    owners = [near_owner(me, n, len(q_refs)) for n in range(len(q_refs))]
    for n, owner in enumerate(owners):
        sel_ref[n * QB * QT:(n + 1) * QB * QT, :] = picked(picks_ref, owner, q_refs[n])
    total = score_picked(sel_ref[...], p_ref, max_ref)
    for n, owner in enumerate(owners):
        put(out_ref, n, total, n, slots_ref, owner)


def some_far_kernel(steps, planes, slots_ref, p_ref, sel_ref, out_ref, wide_ref, max_ref):
    me = lax.axis_index("psg")
    total = score_picked_few(sel_ref[...], p_ref, wide_ref, max_ref)
    for n, step in enumerate(steps):
        put(out_ref, n, total, n, slots_ref, near_owner(me, step, planes) ^ 1)


def last_far_kernel(steps, planes, slots_ref, p_ref, sel_ref, near_ref, far_ref, out_ref, wide_ref, max_ref):
    me = lax.axis_index("psg")
    total = score_picked_few(sel_ref[...], p_ref, wide_ref, max_ref)
    for n, step in enumerate(steps):
        owner = near_owner(me, step, planes) ^ 1
        put(out_ref, owner, total, n, slots_ref, owner)
    others = [step for step in range(planes) if step not in steps]
    for step in range(planes):
        out_ref[near_owner(me, step, planes)] = near_ref[step]
    for n, step in enumerate(others):
        out_ref[near_owner(me, step, planes) ^ 1] = far_ref[n]


def all_kernel(slots_ref, picks_ref, p_ref, q_ref, out_ref, sel_ref, max_ref):
    some = q_ref.shape[0]
    for n in range(some):
        sel_ref[n * QB * QT:(n + 1) * QB * QT, :] = picked(picks_ref, n, q_ref.at[n])
    total = score_picked(sel_ref[...], p_ref, max_ref)
    for n in range(some):
        put(out_ref, n, total, n, slots_ref, n)


def score(kernel, tiles, some, few, passages, *more):
    count, tokens = passages.shape[0], some * QB * QT
    vmem = pl.BlockSpec(memory_space=pltpu.VMEM)
    if few:
        scratch = [pltpu.VMEM((2 * tokens, 2 * DIM), jnp.bfloat16), pltpu.VMEM((count // 2, 2 * tokens), jnp.float32)]
    else:
        scratch = [pltpu.VMEM((tokens, DIM), jnp.bfloat16), pltpu.VMEM((count, tokens), jnp.float32)]
    return pl.pallas_call(
        kernel,
        out_shape=jax.ShapeDtypeStruct((tiles, QB + 1, LANES), jnp.float32),
        in_specs=[vmem] * len(more),
        out_specs=vmem,
        scratch_shapes=scratch,
        compiler_params=pltpu.CompilerParams(vmem_limit_bytes=32 * 1024 * 1024),
        cost_estimate=pl.CostEstimate(
            flops=2 * passages.size * tokens, bytes_accessed=2 * passages.size, transcendentals=0
        ),
    )(*more)


def place_kernel(in_ref, out_ref):
    slots = out_ref.shape[-1]
    m = lax.broadcasted_iota(jnp.int32, (PBS, LANES), 0)
    for j in range(in_ref.shape[0]):
        row = in_ref[j, QB:QB + 1, :].astype(jnp.int32)
        where = jnp.minimum(row * PBS, LANES - PBS) + m
        for i in range(QB):
            tile = jnp.broadcast_to(in_ref[j, i:i + 1, :], (PBS, LANES))
            out_ref[j, i] = jnp.take_along_axis(tile, where, axis=1)[:, :slots]


def place(tiles, slots):
    vmem = pl.BlockSpec(memory_space=pltpu.VMEM)
    shards = tiles.shape[0]
    return pl.pallas_call(
        place_kernel,
        out_shape=jax.ShapeDtypeStruct((shards, QB, PBS, slots), jnp.float32),
        in_specs=[vmem],
        out_specs=vmem,
        compiler_params=pltpu.CompilerParams(vmem_limit_bytes=8 * 1024 * 1024),
    )(tiles)


def by_planes(own, shards, candidates, lengths, passages):
    planes = shards // 2

    def swap_sides(x):
        return lax.ppermute(x, "psg", [(j, j ^ 1) for j in range(shards)])

    def shift(x, step):
        return lax.ppermute(x, "psg", [(j, (j + 2 * step) % shards) for j in range(shards)])

    theirs = swap_sides(candidates)
    shifted = [shift(own, step) for step in range(1, planes)]
    slots, picks, clean = prepare(shards, candidates, lengths, passages)
    clean, *early = lax.optimization_barrier((clean, *reversed(shifted[:planes // 2 - 1])))
    early, late = [own, *reversed(early)], shifted[planes // 2 - 1:]
    steps = list(range(planes))
    first, last = steps[:planes // 2], steps[planes // 2:]
    packed = pack(first, planes, theirs, early)
    first_far = swap_sides(packed)
    *late, _ = lax.optimization_barrier((*reversed(late), packed))
    late = late[::-1]
    last_far = swap_sides(pack(last, planes, theirs, late))
    near_tiles = score(near_kernel, planes, planes, False, clean, slots, picks, clean, *early, *late)
    first_far, near_tiles = lax.optimization_barrier((first_far, near_tiles))
    far_tiles = score(
        functools.partial(some_far_kernel, first, planes), len(first), len(first), True, clean, slots, clean, first_far
    )
    last_far, far_tiles = lax.optimization_barrier((last_far, far_tiles))
    return score(
        functools.partial(last_far_kernel, last, planes), shards, len(last), True, clean,
        slots, clean, last_far, near_tiles, far_tiles,
    )


def by_gather(own, shards, candidates, lengths, passages):
    slots, picks, clean = prepare(shards, candidates, lengths, passages)
    gathered = lax.all_gather(own, "psg", axis=0)
    some = min(shards, 8)

    def score_some(items):
        return score(all_kernel, some, some, False, clean, items[0], items[1], clean, items[2])

    parts = [x.reshape(shards // some, some, *x.shape[1:]) for x in (slots, picks, gathered)]
    return lax.map(score_some, parts).reshape(shards, QB + 1, LANES)


def per_device(queries, passages, lengths, candidates):
    shards = lax.axis_size("psg")
    rows = passages.shape[0] // PBS
    form = by_planes if shards == 8 else by_gather
    tiles = form(
        queries.reshape(QBD * QB * QT, DIM), shards, candidates.reshape(rows, KB), lengths, passages
    )
    tiles = lax.all_to_all(tiles, "psg", split_axis=0, concat_axis=0, tiled=True)
    return place(tiles, rows * KB // shards).transpose(0, 3, 1, 2)[None]


def solution(mesh):
    return jax.shard_map(
        per_device,
        mesh=mesh,
        in_specs=(
            P(("grp", "psg", "qry"), None, None),
            P(("grp", "psg"), None, None),
            P(("grp", "psg")),
            P("qry", ("grp", "psg"), None),
        ),
        out_specs=P(("grp", "psg", "qry"), None, None, None, None),
        check_vma=False,
    )
```

```python
import functools

import jax
import jax.numpy as jnp
from jax import lax
from jax.experimental import pallas as pl
from jax.experimental.pallas import tpu as pltpu
from jax.sharding import PartitionSpec as P

DIM = 128
QT = 32
PT = 64
QB = 2
QBD = 4
PBS = 16
KB = 32
LANES = 128
GROUP = 8


def prepare_kernel(
    cand_hbm, len_hbm, p_hbm, slots_ref, picks_ref, clean_ref, cand_ref, len_ref, raw_ref, sems
):
    rows = cand_ref.shape[0]
    shards = slots_ref.shape[0]
    groups = p_hbm.shape[0] // GROUP

    def fetch(g):
        part = pl.ds(g * GROUP, GROUP)
        return pltpu.make_async_copy(p_hbm.at[part], raw_ref.at[part], sems.at[g])

    fetch_cand = pltpu.make_async_copy(cand_hbm, cand_ref, sems.at[groups])
    fetch_len = pltpu.make_async_copy(len_hbm, len_ref, sems.at[groups + 1])
    fetch_cand.start()
    fetch_len.start()
    for g in range(groups):
        fetch(g).start()

    fetch_cand.wait()
    cand = cand_ref[...]
    owner = cand // QBD
    block = cand - owner * QBD
    lane = lax.broadcasted_iota(jnp.int32, (rows, LANES), 1).astype(jnp.float32)
    sub = lax.broadcasted_iota(jnp.int32, (rows, LANES), 0)
    for o in range(shards):
        mine = owner == o
        named = jnp.max(jnp.where(mine, block, 0), axis=1, keepdims=True)
        picks_ref[o:o + 1, :] = jnp.broadcast_to(jnp.max(named, axis=0, keepdims=True), (1, LANES))
        named_here = jnp.sum(jnp.where(mine, 1.0, 0.0), axis=1, keepdims=True)
        upto = jnp.broadcast_to(named_here, (rows, LANES))
        step = 1
        while step < rows:
            upto = upto + jnp.where(sub >= step, pltpu.roll(upto, step, 0), 0.0)
            step *= 2
        slots_ref[o:o + 1, :] = jnp.sum(jnp.where(upto <= lane, 1.0, 0.0), axis=0, keepdims=True)

    fetch_len.wait()
    u = lax.broadcasted_iota(jnp.int32, (PT, LANES), 0)

    @pl.loop(0, groups)
    def _(g):
        fetch(g).wait()
        for i in range(GROUP):
            p = g * GROUP + i
            tokens = raw_ref[p].astype(jnp.float32)
            clean_ref[p] = jnp.where(u < len_ref[p], tokens, tokens[0:1]).astype(jnp.bfloat16)


def prepare(shards, candidates, lengths, passages):
    hbm = pl.BlockSpec(memory_space=pltpu.HBM)
    vmem = pl.BlockSpec(memory_space=pltpu.VMEM)
    operands = [pltpu.with_memory_space_constraint(x, pltpu.HBM) for x in (candidates, lengths, passages)]
    return pl.pallas_call(
        prepare_kernel,
        out_shape=[
            jax.ShapeDtypeStruct((shards, LANES), jnp.float32),
            jax.ShapeDtypeStruct((shards, LANES), jnp.int32),
            jax.ShapeDtypeStruct(passages.shape, passages.dtype),
        ],
        in_specs=[hbm] * 3,
        out_specs=[vmem] * 3,
        scratch_shapes=[
            pltpu.VMEM(candidates.shape, candidates.dtype),
            pltpu.SMEM(lengths.shape, lengths.dtype),
            pltpu.VMEM(passages.shape, passages.dtype),
            pltpu.SemaphoreType.DMA((passages.shape[0] // GROUP + 2,)),
        ],
        compiler_params=pltpu.CompilerParams(vmem_limit_bytes=24 * 1024 * 1024),
        cost_estimate=pl.CostEstimate(flops=passages.size, bytes_accessed=2 * passages.size, transcendentals=0),
    )(*operands)


def near_owner(me, step, planes):
    return lax.rem((me >> 1) + planes - step, planes) << 1 | me & 1


def picked(picks_ref, owner, q_ref):
    pick = jnp.max(picks_ref[pl.ds(owner, 1), :])
    return q_ref[pl.ds(pick * QB * QT, QB * QT), :]


def pack_kernel(steps, planes, cand_ref, *refs):
    q_refs, out_ref = refs[:-1], refs[-1]
    me = lax.axis_index("psg")
    cand = cand_ref[...]
    owner = cand // QBD
    block = cand - owner * QBD
    for n, step in enumerate(steps):
        pick = jnp.max(jnp.where(owner == near_owner(me, step, planes), block, 0))
        out_ref[n * QB * QT:(n + 1) * QB * QT, :] = q_refs[n][pl.ds(pick * QB * QT, QB * QT), :]


def pack(steps, planes, candidates, blocks):
    vmem = pl.BlockSpec(memory_space=pltpu.VMEM)
    return pl.pallas_call(
        functools.partial(pack_kernel, steps, planes),
        out_shape=jax.ShapeDtypeStruct((len(blocks) * QB * QT, DIM), blocks[0].dtype),
        in_specs=[vmem] * (1 + len(blocks)),
        out_specs=vmem,
        compiler_params=pltpu.CompilerParams(vmem_limit_bytes=4 * 1024 * 1024),
    )(candidates, *blocks)


def sum_tokens(best):
    tokens = best.shape[1]
    high = best.astype(jnp.bfloat16)
    rest = best - high.astype(jnp.float32)
    mid = rest.astype(jnp.bfloat16)
    low = (rest - mid.astype(jnp.float32)).astype(jnp.bfloat16)
    parts = jnp.concatenate([low, mid, high], axis=1)
    query = lax.broadcasted_iota(jnp.int32, (tokens // QT, tokens), 0)
    token = lax.broadcasted_iota(jnp.int32, (tokens // QT, tokens), 1)
    ones = jnp.where(token // QT == query, 1.0, 0.0).astype(jnp.bfloat16)
    total = lax.dot_general(
        jnp.concatenate([ones] * 3, axis=1), parts, (((1,), (1,)), ((), ())), preferred_element_type=jnp.float32
    )
    return total * (1.0 / QT)


def best_tokens(left_of, sel, max_ref, piece):
    count, tokens = max_ref.shape
    for g in range(0, count, piece):
        dots = lax.dot_general(left_of(g, piece), sel, (((1,), (1,)), ((), ())), preferred_element_type=jnp.float32)
        max_ref[g:g + piece, :] = jnp.max(dots.reshape(piece, PT, tokens), axis=1)
    return max_ref[...]


def score_picked(sel, p_ref, max_ref):
    def left_of(g, piece):
        return p_ref[g:g + piece].reshape(piece * PT, DIM)

    return sum_tokens(best_tokens(left_of, sel, max_ref, 2 * GROUP))


def score_picked_few(sel, p_ref, wide_ref, max_ref):
    tokens, half = sel.shape[0], p_ref.shape[0] // 2
    wide_ref[...] = jnp.zeros_like(wide_ref)
    wide_ref[0:tokens, 0:DIM] = sel
    wide_ref[tokens:, DIM:] = sel

    def left_of(g, piece):
        return jnp.concatenate(
            [p_ref[h + g:h + g + piece].reshape(piece * PT, DIM) for h in (0, half)], axis=1
        )

    total = sum_tokens(best_tokens(left_of, wide_ref[...], max_ref, GROUP))
    queries = tokens // QT
    return jnp.concatenate([total[:queries], total[queries:]], axis=1)


def put(out_ref, place, total, n, slots_ref, owner):
    out_ref[place, 0:QB, :] = total[n * QB:(n + 1) * QB]
    out_ref[place, QB:QB + 1, :] = slots_ref[pl.ds(owner, 1), :]


def near_kernel(slots_ref, picks_ref, p_ref, *refs):
    q_refs, (out_ref, sel_ref, max_ref) = refs[:-3], refs[-3:]
    me = lax.axis_index("psg")
    owners = [near_owner(me, n, len(q_refs)) for n in range(len(q_refs))]
    for n, owner in enumerate(owners):
        sel_ref[n * QB * QT:(n + 1) * QB * QT, :] = picked(picks_ref, owner, q_refs[n])
    total = score_picked(sel_ref[...], p_ref, max_ref)
    for n, owner in enumerate(owners):
        put(out_ref, n, total, n, slots_ref, owner)


def some_far_kernel(steps, planes, slots_ref, p_ref, sel_ref, out_ref, wide_ref, max_ref):
    me = lax.axis_index("psg")
    total = score_picked_few(sel_ref[...], p_ref, wide_ref, max_ref)
    for n, step in enumerate(steps):
        put(out_ref, n, total, n, slots_ref, near_owner(me, step, planes) ^ 1)


def last_far_kernel(steps, planes, slots_ref, p_ref, sel_ref, near_ref, far_ref, out_ref, wide_ref, max_ref):
    me = lax.axis_index("psg")
    total = score_picked_few(sel_ref[...], p_ref, wide_ref, max_ref)
    for n, step in enumerate(steps):
        owner = near_owner(me, step, planes) ^ 1
        put(out_ref, owner, total, n, slots_ref, owner)
    others = [step for step in range(planes) if step not in steps]
    for step in range(planes):
        out_ref[near_owner(me, step, planes)] = near_ref[step]
    for n, step in enumerate(others):
        out_ref[near_owner(me, step, planes) ^ 1] = far_ref[n]


def all_kernel(slots_ref, picks_ref, p_ref, q_ref, out_ref, sel_ref, max_ref):
    some = q_ref.shape[0]
    for n in range(some):
        sel_ref[n * QB * QT:(n + 1) * QB * QT, :] = picked(picks_ref, n, q_ref.at[n])
    total = score_picked(sel_ref[...], p_ref, max_ref)
    for n in range(some):
        put(out_ref, n, total, n, slots_ref, n)


def score(kernel, tiles, some, few, passages, *more):
    count, tokens = passages.shape[0], some * QB * QT
    vmem = pl.BlockSpec(memory_space=pltpu.VMEM)
    if few:
        scratch = [pltpu.VMEM((2 * tokens, 2 * DIM), jnp.bfloat16), pltpu.VMEM((count // 2, 2 * tokens), jnp.float32)]
    else:
        scratch = [pltpu.VMEM((tokens, DIM), jnp.bfloat16), pltpu.VMEM((count, tokens), jnp.float32)]
    return pl.pallas_call(
        kernel,
        out_shape=jax.ShapeDtypeStruct((tiles, QB + 1, LANES), jnp.float32),
        in_specs=[vmem] * len(more),
        out_specs=vmem,
        scratch_shapes=scratch,
        compiler_params=pltpu.CompilerParams(vmem_limit_bytes=32 * 1024 * 1024),
        cost_estimate=pl.CostEstimate(
            flops=2 * passages.size * tokens, bytes_accessed=2 * passages.size, transcendentals=0
        ),
    )(*more)


def place_kernel(in_ref, out_ref):
    slots = out_ref.shape[-1]
    m = lax.broadcasted_iota(jnp.int32, (PBS, LANES), 0)
    for j in range(in_ref.shape[0]):
        row = in_ref[j, QB:QB + 1, :].astype(jnp.int32)
        where = jnp.minimum(row * PBS, LANES - PBS) + m
        for i in range(QB):
            tile = jnp.broadcast_to(in_ref[j, i:i + 1, :], (PBS, LANES))
            out_ref[j, i] = jnp.take_along_axis(tile, where, axis=1)[:, :slots]


def place(tiles, slots):
    vmem = pl.BlockSpec(memory_space=pltpu.VMEM)
    shards = tiles.shape[0]
    return pl.pallas_call(
        place_kernel,
        out_shape=jax.ShapeDtypeStruct((shards, QB, PBS, slots), jnp.float32),
        in_specs=[vmem],
        out_specs=vmem,
        compiler_params=pltpu.CompilerParams(vmem_limit_bytes=8 * 1024 * 1024),
    )(tiles)


def by_planes(own, shards, candidates, lengths, passages):
    planes = shards // 2

    def swap_sides(x):
        return lax.ppermute(x, "psg", [(j, j ^ 1) for j in range(shards)])

    def shift(x, step):
        return lax.ppermute(x, "psg", [(j, (j + 2 * step) % shards) for j in range(shards)])

    theirs = swap_sides(candidates)
    shifted = [shift(own, step) for step in range(1, planes)]
    slots, picks, clean = prepare(shards, candidates, lengths, passages)
    first = [0, planes // 2]
    last = [step for step in range(planes) if step not in first]
    clean, shifted[first[1] - 1] = lax.optimization_barrier((clean, shifted[first[1] - 1]))
    blocks = [own, *shifted]
    packed = pack(first, planes, theirs, [blocks[step] for step in first])
    first_far = swap_sides(packed)
    *late, _ = lax.optimization_barrier((*[blocks[step] for step in last], packed))
    for step, block in zip(last, late):
        blocks[step] = block
    last_far = swap_sides(pack(last, planes, theirs, [blocks[step] for step in last]))
    near_tiles = score(near_kernel, planes, planes, False, clean, slots, picks, clean, *blocks)
    first_far, near_tiles = lax.optimization_barrier((first_far, near_tiles))
    far_tiles = score(
        functools.partial(some_far_kernel, first, planes), len(first), len(first), True, clean, slots, clean, first_far
    )
    last_far, far_tiles = lax.optimization_barrier((last_far, far_tiles))
    return score(
        functools.partial(last_far_kernel, last, planes), shards, len(last), True, clean,
        slots, clean, last_far, near_tiles, far_tiles,
    )


def by_gather(own, shards, candidates, lengths, passages):
    slots, picks, clean = prepare(shards, candidates, lengths, passages)
    gathered = lax.all_gather(own, "psg", axis=0)
    some = min(shards, 8)

    def score_some(items):
        return score(all_kernel, some, some, False, clean, items[0], items[1], clean, items[2])

    parts = [x.reshape(shards // some, some, *x.shape[1:]) for x in (slots, picks, gathered)]
    return lax.map(score_some, parts).reshape(shards, QB + 1, LANES)


def per_device(queries, passages, lengths, candidates):
    shards = lax.axis_size("psg")
    rows = passages.shape[0] // PBS
    form = by_planes if shards == 8 else by_gather
    tiles = form(
        queries.reshape(QBD * QB * QT, DIM), shards, candidates.reshape(rows, KB), lengths, passages
    )
    tiles = lax.all_to_all(tiles, "psg", split_axis=0, concat_axis=0, tiled=True)
    return place(tiles, rows * KB // shards).transpose(0, 3, 1, 2)[None]


def solution(mesh):
    return jax.shard_map(
        per_device,
        mesh=mesh,
        in_specs=(
            P(("grp", "psg", "qry"), None, None),
            P(("grp", "psg"), None, None),
            P(("grp", "psg")),
            P("qry", ("grp", "psg"), None),
        ),
        out_specs=P(("grp", "psg", "qry"), None, None, None, None),
        check_vma=False,
    )
```

```python
import functools

import jax
import jax.numpy as jnp
from jax import lax
from jax.experimental import pallas as pl
from jax.experimental.pallas import tpu as pltpu
from jax.sharding import PartitionSpec as P

DIM = 128
QT = 32
PT = 64
QB = 2
QBD = 4
PBS = 16
KB = 32
LANES = 128
GROUP = 8
TILE = 4


def prepare_kernel(
    cand_hbm, len_hbm, p_hbm, slots_ref, picks_ref, clean_ref, cand_ref, len_ref, raw_ref, sems
):
    rows = cand_ref.shape[0]
    shards = slots_ref.shape[0]
    groups = p_hbm.shape[0] // GROUP

    def fetch(g):
        part = pl.ds(g * GROUP, GROUP)
        return pltpu.make_async_copy(p_hbm.at[part], raw_ref.at[part], sems.at[g])

    fetch_cand = pltpu.make_async_copy(cand_hbm, cand_ref, sems.at[groups])
    fetch_len = pltpu.make_async_copy(len_hbm, len_ref, sems.at[groups + 1])
    fetch_cand.start()
    fetch_len.start()
    for g in range(groups):
        fetch(g).start()

    fetch_cand.wait()
    cand = cand_ref[...]
    owner = cand // QBD
    block = cand - owner * QBD
    lane = lax.broadcasted_iota(jnp.int32, (rows, LANES), 1).astype(jnp.float32)
    sub = lax.broadcasted_iota(jnp.int32, (rows, LANES), 0)
    for o in range(shards):
        mine = owner == o
        named = jnp.max(jnp.where(mine, block, 0), axis=1, keepdims=True)
        picks_ref[o:o + 1, :] = jnp.broadcast_to(jnp.max(named, axis=0, keepdims=True), (1, LANES))
        named_here = jnp.sum(jnp.where(mine, 1.0, 0.0), axis=1, keepdims=True)
        upto = jnp.broadcast_to(named_here, (rows, LANES))
        step = 1
        while step < rows:
            upto = upto + jnp.where(sub >= step, pltpu.roll(upto, step, 0), 0.0)
            step *= 2
        slots_ref[o:o + 1, :] = jnp.sum(jnp.where(upto <= lane, 1.0, 0.0), axis=0, keepdims=True)

    fetch_len.wait()
    u = lax.broadcasted_iota(jnp.int32, (PT, LANES), 0)

    @pl.loop(0, groups)
    def _(g):
        fetch(g).wait()
        for i in range(GROUP):
            p = g * GROUP + i
            tokens = raw_ref[p].astype(jnp.float32)
            clean_ref[p] = jnp.where(u < len_ref[p], tokens, tokens[0:1]).astype(jnp.bfloat16)


def prepare(shards, candidates, lengths, passages):
    hbm = pl.BlockSpec(memory_space=pltpu.HBM)
    vmem = pl.BlockSpec(memory_space=pltpu.VMEM)
    operands = [pltpu.with_memory_space_constraint(x, pltpu.HBM) for x in (candidates, lengths, passages)]
    return pl.pallas_call(
        prepare_kernel,
        out_shape=[
            jax.ShapeDtypeStruct((shards, LANES), jnp.float32),
            jax.ShapeDtypeStruct((shards, LANES), jnp.int32),
            jax.ShapeDtypeStruct(passages.shape, passages.dtype),
        ],
        in_specs=[hbm] * 3,
        out_specs=[vmem] * 3,
        scratch_shapes=[
            pltpu.VMEM(candidates.shape, candidates.dtype),
            pltpu.SMEM(lengths.shape, lengths.dtype),
            pltpu.VMEM(passages.shape, passages.dtype),
            pltpu.SemaphoreType.DMA((passages.shape[0] // GROUP + 2,)),
        ],
        compiler_params=pltpu.CompilerParams(vmem_limit_bytes=24 * 1024 * 1024),
        cost_estimate=pl.CostEstimate(flops=passages.size, bytes_accessed=2 * passages.size, transcendentals=0),
    )(*operands)


def near_owner(me, step, planes):
    return lax.rem((me >> 1) + planes - step, planes) << 1 | me & 1


def picked(picks_ref, owner, q_ref):
    pick = jnp.max(picks_ref[pl.ds(owner, 1), :])
    return q_ref[pl.ds(pick * QB * QT, QB * QT), :]


def pack_kernel(steps, planes, cand_ref, *refs):
    q_refs, out_ref = refs[:-1], refs[-1]
    me = lax.axis_index("psg")
    cand = cand_ref[...]
    owner = cand // QBD
    block = cand - owner * QBD
    for n, step in enumerate(steps):
        pick = jnp.max(jnp.where(owner == near_owner(me, step, planes), block, 0))
        out_ref[n * QB * QT:(n + 1) * QB * QT, :] = q_refs[n][pl.ds(pick * QB * QT, QB * QT), :]


def pack(steps, planes, candidates, blocks):
    vmem = pl.BlockSpec(memory_space=pltpu.VMEM)
    return pl.pallas_call(
        functools.partial(pack_kernel, steps, planes),
        out_shape=jax.ShapeDtypeStruct((len(blocks) * QB * QT, DIM), blocks[0].dtype),
        in_specs=[vmem] * (1 + len(blocks)),
        out_specs=vmem,
        compiler_params=pltpu.CompilerParams(vmem_limit_bytes=4 * 1024 * 1024),
    )(candidates, *blocks)


def sum_tokens(best):
    tokens = best.shape[1]
    high = best.astype(jnp.bfloat16)
    rest = best - high.astype(jnp.float32)
    mid = rest.astype(jnp.bfloat16)
    low = (rest - mid.astype(jnp.float32)).astype(jnp.bfloat16)
    parts = jnp.concatenate([low, mid, high], axis=1)
    query = lax.broadcasted_iota(jnp.int32, (tokens // QT, tokens), 0)
    token = lax.broadcasted_iota(jnp.int32, (tokens // QT, tokens), 1)
    ones = jnp.where(token // QT == query, 1.0, 0.0).astype(jnp.bfloat16)
    total = lax.dot_general(
        jnp.concatenate([ones] * 3, axis=1), parts, (((1,), (1,)), ((), ())), preferred_element_type=jnp.float32
    )
    return total * (1.0 / QT)


def best_tokens(left_of, sel, max_ref, piece):
    count, tokens = max_ref.shape
    for g in range(0, count, piece):
        dots = lax.dot_general(left_of(g, piece), sel, (((1,), (1,)), ((), ())), preferred_element_type=jnp.float32)
        max_ref[g:g + piece, :] = jnp.max(dots.reshape(piece, PT, tokens), axis=1)
    return max_ref[...]


def score_picked(sel, p_ref, max_ref):
    def left_of(g, piece):
        return p_ref[g:g + piece].reshape(piece * PT, DIM)

    return sum_tokens(best_tokens(left_of, sel, max_ref, 2 * GROUP))


def score_picked_few(sel, p_ref, wide_ref, max_ref):
    tokens, half = sel.shape[0], p_ref.shape[0] // 2
    wide_ref[...] = jnp.zeros_like(wide_ref)
    wide_ref[0:tokens, 0:DIM] = sel
    wide_ref[tokens:, DIM:] = sel

    def left_of(g, piece):
        return jnp.concatenate(
            [p_ref[h + g:h + g + piece].reshape(piece * PT, DIM) for h in (0, half)], axis=1
        )

    total = sum_tokens(best_tokens(left_of, wide_ref[...], max_ref, GROUP))
    queries = tokens // QT
    return jnp.concatenate([total[:queries], total[queries:]], axis=1)


def put(out_ref, place, total, n, slots_ref, owner):
    out_ref[place, 0:QB, :] = total[n * QB:(n + 1) * QB]
    out_ref[place, QB:QB + 1, :] = slots_ref[pl.ds(owner, 1), :]


def near_kernel(slots_ref, picks_ref, p_ref, *refs):
    q_refs, (out_ref, sel_ref, max_ref) = refs[:-3], refs[-3:]
    me = lax.axis_index("psg")
    owners = [near_owner(me, n, len(q_refs)) for n in range(len(q_refs))]
    for n, owner in enumerate(owners):
        sel_ref[n * QB * QT:(n + 1) * QB * QT, :] = picked(picks_ref, owner, q_refs[n])
    total = score_picked(sel_ref[...], p_ref, max_ref)
    for n, owner in enumerate(owners):
        put(out_ref, n, total, n, slots_ref, owner)


def some_far_kernel(steps, planes, slots_ref, p_ref, sel_ref, out_ref, wide_ref, max_ref):
    me = lax.axis_index("psg")
    total = score_picked_few(sel_ref[...], p_ref, wide_ref, max_ref)
    for n, step in enumerate(steps):
        put(out_ref, n, total, n, slots_ref, near_owner(me, step, planes) ^ 1)


def last_far_kernel(steps, planes, slots_ref, p_ref, sel_ref, near_ref, far_ref, out_ref, wide_ref, max_ref):
    me = lax.axis_index("psg")
    total = score_picked_few(sel_ref[...], p_ref, wide_ref, max_ref)
    for n, step in enumerate(steps):
        owner = near_owner(me, step, planes) ^ 1
        put(out_ref, owner, total, n, slots_ref, owner)
    others = [step for step in range(planes) if step not in steps]
    for step in range(planes):
        out_ref[near_owner(me, step, planes), 0:QB + 1, :] = near_ref[step]
    for n, step in enumerate(others):
        out_ref[near_owner(me, step, planes) ^ 1, 0:QB + 1, :] = far_ref[n]


def all_kernel(slots_ref, picks_ref, p_ref, q_ref, out_ref, sel_ref, max_ref):
    some = q_ref.shape[0]
    for n in range(some):
        sel_ref[n * QB * QT:(n + 1) * QB * QT, :] = picked(picks_ref, n, q_ref.at[n])
    total = score_picked(sel_ref[...], p_ref, max_ref)
    for n in range(some):
        put(out_ref, n, total, n, slots_ref, n)


def score(kernel, tiles, some, few, passages, *more, tile_rows=QB + 1):
    count, tokens = passages.shape[0], some * QB * QT
    vmem = pl.BlockSpec(memory_space=pltpu.VMEM)
    if few:
        scratch = [pltpu.VMEM((2 * tokens, 2 * DIM), jnp.bfloat16), pltpu.VMEM((count // 2, 2 * tokens), jnp.float32)]
    else:
        scratch = [pltpu.VMEM((tokens, DIM), jnp.bfloat16), pltpu.VMEM((count, tokens), jnp.float32)]
    return pl.pallas_call(
        kernel,
        out_shape=jax.ShapeDtypeStruct((tiles, tile_rows, LANES), jnp.float32),
        in_specs=[vmem] * len(more),
        out_specs=vmem,
        scratch_shapes=scratch,
        compiler_params=pltpu.CompilerParams(vmem_limit_bytes=32 * 1024 * 1024),
        cost_estimate=pl.CostEstimate(
            flops=2 * passages.size * tokens, bytes_accessed=2 * passages.size, transcendentals=0
        ),
    )(*more)


def place_kernel(in_ref, out_ref):
    slots = out_ref.shape[-1]
    m = lax.broadcasted_iota(jnp.int32, (PBS, LANES), 0)
    for j in range(in_ref.shape[0]):
        tile_ref = in_ref.at[j, lax.axis_index("psg")] if len(in_ref.shape) == 4 else in_ref.at[j]
        row = tile_ref[QB:QB + 1, :].astype(jnp.int32)
        where = jnp.minimum(row * PBS, LANES - PBS) + m
        for i in range(QB):
            tile = jnp.broadcast_to(tile_ref[i:i + 1, :], (PBS, LANES))
            out_ref[j, i] = jnp.take_along_axis(tile, where, axis=1)[:, :slots]


def place(tiles, slots):
    vmem = pl.BlockSpec(memory_space=pltpu.VMEM)
    shards = tiles.shape[0]
    return pl.pallas_call(
        place_kernel,
        out_shape=jax.ShapeDtypeStruct((shards, QB, PBS, slots), jnp.float32),
        in_specs=[vmem],
        out_specs=vmem,
        compiler_params=pltpu.CompilerParams(vmem_limit_bytes=8 * 1024 * 1024),
    )(tiles)


def by_planes(own, shards, slot_count, candidates, lengths, passages):
    planes = shards // 2

    def swap_sides(x):
        return lax.ppermute(x, "psg", [(j, j ^ 1) for j in range(shards)])

    def shift(x, step):
        return lax.ppermute(x, "psg", [(j, (j + 2 * step) % shards) for j in range(shards)])

    theirs = swap_sides(candidates)
    shifted = [shift(own, step) for step in range(1, planes)]
    slots, picks, clean = prepare(shards, candidates, lengths, passages)
    clean, *early = lax.optimization_barrier((clean, *reversed(shifted[:planes // 2 - 1])))
    early, late = [own, *reversed(early)], shifted[planes // 2 - 1:]
    steps = list(range(planes))
    first, last = steps[:planes // 2], steps[planes // 2:]
    packed = pack(first, planes, theirs, early)
    first_far = swap_sides(packed)
    *late, _ = lax.optimization_barrier((*reversed(late), packed))
    late = late[::-1]
    last_far = swap_sides(pack(last, planes, theirs, late))
    near_tiles = score(near_kernel, planes, planes, False, clean, slots, picks, clean, *early, *late)
    first_far, near_tiles = lax.optimization_barrier((first_far, near_tiles))
    far_tiles = score(
        functools.partial(some_far_kernel, first, planes), len(first), len(first), True, clean, slots, clean, first_far
    )
    last_far, far_tiles = lax.optimization_barrier((last_far, far_tiles))
    tiles = score(
        functools.partial(last_far_kernel, last, planes), shards, len(last), True, clean,
        slots, clean, last_far, near_tiles, far_tiles, tile_rows=TILE,
    )
    tiles = lax.all_gather(tiles.reshape(shards * TILE, LANES), "psg", axis=0, tiled=True)
    return place(tiles.reshape(shards, shards, TILE, LANES), slot_count)


def by_gather(own, shards, slot_count, candidates, lengths, passages):
    slots, picks, clean = prepare(shards, candidates, lengths, passages)
    gathered = lax.all_gather(own, "psg", axis=0)
    some = min(shards, 8)

    def score_some(items):
        return score(all_kernel, some, some, False, clean, items[0], items[1], clean, items[2])

    parts = [x.reshape(shards // some, some, *x.shape[1:]) for x in (slots, picks, gathered)]
    tiles = lax.map(score_some, parts).reshape(shards, QB + 1, LANES)
    return place(lax.all_to_all(tiles, "psg", split_axis=0, concat_axis=0, tiled=True), slot_count)


def per_device(queries, passages, lengths, candidates):
    shards = lax.axis_size("psg")
    rows = passages.shape[0] // PBS
    form = by_planes if shards == 8 else by_gather
    placed = form(
        queries.reshape(QBD * QB * QT, DIM), shards, rows * KB // shards,
        candidates.reshape(rows, KB), lengths, passages,
    )
    return placed.transpose(0, 3, 1, 2)[None]


def solution(mesh):
    return jax.shard_map(
        per_device,
        mesh=mesh,
        in_specs=(
            P(("grp", "psg", "qry"), None, None),
            P(("grp", "psg"), None, None),
            P(("grp", "psg")),
            P("qry", ("grp", "psg"), None),
        ),
        out_specs=P(("grp", "psg", "qry"), None, None, None, None),
        check_vma=False,
    )
```

```python
import functools

import jax
import jax.numpy as jnp
from jax import lax
from jax.experimental import pallas as pl
from jax.experimental.pallas import tpu as pltpu
from jax.sharding import PartitionSpec as P

DIM = 128
QT = 32
PT = 64
QB = 2
QBD = 4
PBS = 16
KB = 32
LANES = 128
GROUP = 8


def clean_passages(len_hbm, p_hbm, clean_ref, len_ref, raw_ref, sems, meanwhile=lambda: None):
    groups = p_hbm.shape[0] // GROUP

    def fetch(g):
        part = pl.ds(g * GROUP, GROUP)
        return pltpu.make_async_copy(p_hbm.at[part], raw_ref.at[part], sems.at[g])

    fetch_len = pltpu.make_async_copy(len_hbm, len_ref, sems.at[groups])
    fetch_len.start()
    for g in range(groups):
        fetch(g).start()
    meanwhile()
    fetch_len.wait()
    u = lax.broadcasted_iota(jnp.int32, (PT, LANES), 0)

    @pl.loop(0, groups)
    def _(g):
        fetch(g).wait()
        for i in range(GROUP):
            p = g * GROUP + i
            tokens = raw_ref[p].astype(jnp.float32)
            clean_ref[p] = jnp.where(u < len_ref[p], tokens, tokens[0:1]).astype(jnp.bfloat16)


def read_candidates(cand_ref, slots_ref, picks_ref):
    rows = cand_ref.shape[0]
    cand = cand_ref[...]
    owner = cand // QBD
    block = cand - owner * QBD
    lane = lax.broadcasted_iota(jnp.int32, (rows, LANES), 1).astype(jnp.float32)
    sub = lax.broadcasted_iota(jnp.int32, (rows, LANES), 0)
    for o in range(slots_ref.shape[0]):
        mine = owner == o
        named = jnp.max(jnp.where(mine, block, 0), axis=1, keepdims=True)
        picks_ref[o:o + 1, :] = jnp.broadcast_to(jnp.max(named, axis=0, keepdims=True), (1, LANES))
        named_here = jnp.sum(jnp.where(mine, 1.0, 0.0), axis=1, keepdims=True)
        upto = jnp.broadcast_to(named_here, (rows, LANES))
        step = 1
        while step < rows:
            upto = upto + jnp.where(sub >= step, pltpu.roll(upto, step, 0), 0.0)
            step *= 2
        slots_ref[o:o + 1, :] = jnp.sum(jnp.where(upto <= lane, 1.0, 0.0), axis=0, keepdims=True)


def prepare_early_kernel(len_hbm, p_hbm, clean_ref, *scratch):
    @pl.when(lax.axis_index("qry") % 2 == 1)
    def _():
        clean_passages(len_hbm, p_hbm, clean_ref, *scratch)


def prepare_kernel(early, cand_hbm, len_hbm, p_hbm, *refs):
    early_refs, (slots_ref, picks_ref, clean_ref, len_ref, raw_ref, sems, cand_ref) = refs[:early], refs[early:]
    fetch_cand = pltpu.make_async_copy(cand_hbm, cand_ref, sems.at[sems.shape[0] - 1])
    fetch_cand.start()

    def candidates():
        fetch_cand.wait()
        read_candidates(cand_ref, slots_ref, picks_ref)

    def now():
        clean_passages(len_hbm, p_hbm, clean_ref, len_ref, raw_ref, sems, candidates)

    if not early:
        now()
        return
    odd = lax.axis_index("qry") % 2 == 1
    pl.when(jnp.logical_not(odd))(now)

    @pl.when(odd)
    def _():
        candidates()

        @pl.loop(0, clean_ref.shape[0] // GROUP)
        def _(g):
            part = pl.ds(g * GROUP, GROUP)
            clean_ref[part] = early_refs[0][part]


def prepare_scratch(lengths, passages):
    return [
        pltpu.SMEM(lengths.shape, lengths.dtype),
        pltpu.VMEM(passages.shape, passages.dtype),
        pltpu.SemaphoreType.DMA((passages.shape[0] // GROUP + 2,)),
    ]


def prepare_early(lengths, passages):
    hbm = pl.BlockSpec(memory_space=pltpu.HBM)
    return pl.pallas_call(
        prepare_early_kernel,
        out_shape=jax.ShapeDtypeStruct(passages.shape, passages.dtype),
        in_specs=[hbm] * 2,
        out_specs=pl.BlockSpec(memory_space=pltpu.VMEM),
        scratch_shapes=prepare_scratch(lengths, passages),
        compiler_params=pltpu.CompilerParams(vmem_limit_bytes=24 * 1024 * 1024),
    )(*[pltpu.with_memory_space_constraint(x, pltpu.HBM) for x in (lengths, passages)])


def prepare(shards, candidates, lengths, passages, *early):
    hbm = pl.BlockSpec(memory_space=pltpu.HBM)
    vmem = pl.BlockSpec(memory_space=pltpu.VMEM)
    operands = [pltpu.with_memory_space_constraint(x, pltpu.HBM) for x in (candidates, lengths, passages)]
    return pl.pallas_call(
        functools.partial(prepare_kernel, len(early)),
        out_shape=[
            jax.ShapeDtypeStruct((shards, LANES), jnp.float32),
            jax.ShapeDtypeStruct((shards, LANES), jnp.int32),
            jax.ShapeDtypeStruct(passages.shape, passages.dtype),
        ],
        in_specs=[hbm] * 3 + [vmem] * len(early),
        out_specs=[vmem] * 3,
        scratch_shapes=prepare_scratch(lengths, passages) + [pltpu.VMEM(candidates.shape, candidates.dtype)],
        compiler_params=pltpu.CompilerParams(vmem_limit_bytes=24 * 1024 * 1024),
        cost_estimate=pl.CostEstimate(flops=passages.size, bytes_accessed=2 * passages.size, transcendentals=0),
    )(*operands, *early)


def near_owner(me, step, planes):
    return lax.rem((me >> 1) + planes - step, planes) << 1 | me & 1


def picked(picks_ref, owner, q_ref):
    pick = jnp.max(picks_ref[pl.ds(owner, 1), :])
    return q_ref[pl.ds(pick * QB * QT, QB * QT), :]


def pack_kernel(steps, planes, cand_ref, *refs):
    q_refs, out_ref = refs[:-1], refs[-1]
    me = lax.axis_index("psg")
    cand = cand_ref[...]
    owner = cand // QBD
    block = cand - owner * QBD
    for n, step in enumerate(steps):
        pick = jnp.max(jnp.where(owner == near_owner(me, step, planes), block, 0))
        out_ref[n * QB * QT:(n + 1) * QB * QT, :] = q_refs[n][pl.ds(pick * QB * QT, QB * QT), :]


def pack(steps, planes, candidates, blocks):
    vmem = pl.BlockSpec(memory_space=pltpu.VMEM)
    return pl.pallas_call(
        functools.partial(pack_kernel, steps, planes),
        out_shape=jax.ShapeDtypeStruct((len(blocks) * QB * QT, DIM), blocks[0].dtype),
        in_specs=[vmem] * (1 + len(blocks)),
        out_specs=vmem,
        compiler_params=pltpu.CompilerParams(vmem_limit_bytes=4 * 1024 * 1024),
    )(candidates, *blocks)


def sum_tokens(best):
    tokens = best.shape[1]
    high = best.astype(jnp.bfloat16)
    rest = best - high.astype(jnp.float32)
    mid = rest.astype(jnp.bfloat16)
    low = (rest - mid.astype(jnp.float32)).astype(jnp.bfloat16)
    parts = jnp.concatenate([low, mid, high], axis=1)
    query = lax.broadcasted_iota(jnp.int32, (tokens // QT, tokens), 0)
    token = lax.broadcasted_iota(jnp.int32, (tokens // QT, tokens), 1)
    ones = jnp.where(token // QT == query, 1.0, 0.0).astype(jnp.bfloat16)
    total = lax.dot_general(
        jnp.concatenate([ones] * 3, axis=1), parts, (((1,), (1,)), ((), ())), preferred_element_type=jnp.float32
    )
    return total * (1.0 / QT)


def best_tokens(left_of, sel, max_ref, piece):
    count, tokens = max_ref.shape
    for g in range(0, count, piece):
        dots = lax.dot_general(left_of(g, piece), sel, (((1,), (1,)), ((), ())), preferred_element_type=jnp.float32)
        max_ref[g:g + piece, :] = jnp.max(dots.reshape(piece, PT, tokens), axis=1)
    return max_ref[...]


def score_picked(sel, p_ref, max_ref):
    def left_of(g, piece):
        return p_ref[g:g + piece].reshape(piece * PT, DIM)

    return sum_tokens(best_tokens(left_of, sel, max_ref, 2 * GROUP))


def score_picked_few(sel, p_ref, wide_ref, max_ref):
    tokens, half = sel.shape[0], p_ref.shape[0] // 2
    wide_ref[...] = jnp.zeros_like(wide_ref)
    wide_ref[0:tokens, 0:DIM] = sel
    wide_ref[tokens:, DIM:] = sel

    def left_of(g, piece):
        return jnp.concatenate(
            [p_ref[h + g:h + g + piece].reshape(piece * PT, DIM) for h in (0, half)], axis=1
        )

    total = sum_tokens(best_tokens(left_of, wide_ref[...], max_ref, GROUP))
    queries = tokens // QT
    return jnp.concatenate([total[:queries], total[queries:]], axis=1)


def put(out_ref, place, total, n, slots_ref, owner):
    out_ref[place, 0:QB, :] = total[n * QB:(n + 1) * QB]
    out_ref[place, QB:QB + 1, :] = slots_ref[pl.ds(owner, 1), :]


def near_kernel(slots_ref, picks_ref, p_ref, *refs):
    q_refs, (out_ref, sel_ref, max_ref) = refs[:-3], refs[-3:]
    me = lax.axis_index("psg")
    owners = [near_owner(me, n, len(q_refs)) for n in range(len(q_refs))]
    for n, owner in enumerate(owners):
        sel_ref[n * QB * QT:(n + 1) * QB * QT, :] = picked(picks_ref, owner, q_refs[n])
    total = score_picked(sel_ref[...], p_ref, max_ref)
    for n, owner in enumerate(owners):
        put(out_ref, n, total, n, slots_ref, owner)


def some_far_kernel(steps, planes, slots_ref, p_ref, sel_ref, out_ref, wide_ref, max_ref):
    me = lax.axis_index("psg")
    total = score_picked_few(sel_ref[...], p_ref, wide_ref, max_ref)
    for n, step in enumerate(steps):
        put(out_ref, n, total, n, slots_ref, near_owner(me, step, planes) ^ 1)


def last_far_kernel(steps, planes, slots_ref, p_ref, sel_ref, near_ref, far_ref, out_ref, wide_ref, max_ref):
    me = lax.axis_index("psg")
    total = score_picked_few(sel_ref[...], p_ref, wide_ref, max_ref)
    for n, step in enumerate(steps):
        owner = near_owner(me, step, planes) ^ 1
        put(out_ref, owner, total, n, slots_ref, owner)
    others = [step for step in range(planes) if step not in steps]
    for step in range(planes):
        out_ref[near_owner(me, step, planes)] = near_ref[step]
    for n, step in enumerate(others):
        out_ref[near_owner(me, step, planes) ^ 1] = far_ref[n]


def all_kernel(slots_ref, picks_ref, p_ref, q_ref, out_ref, sel_ref, max_ref):
    some = q_ref.shape[0]
    for n in range(some):
        sel_ref[n * QB * QT:(n + 1) * QB * QT, :] = picked(picks_ref, n, q_ref.at[n])
    total = score_picked(sel_ref[...], p_ref, max_ref)
    for n in range(some):
        put(out_ref, n, total, n, slots_ref, n)


def score(kernel, tiles, some, few, passages, *more):
    count, tokens = passages.shape[0], some * QB * QT
    vmem = pl.BlockSpec(memory_space=pltpu.VMEM)
    if few:
        scratch = [pltpu.VMEM((2 * tokens, 2 * DIM), jnp.bfloat16), pltpu.VMEM((count // 2, 2 * tokens), jnp.float32)]
    else:
        scratch = [pltpu.VMEM((tokens, DIM), jnp.bfloat16), pltpu.VMEM((count, tokens), jnp.float32)]
    return pl.pallas_call(
        kernel,
        out_shape=jax.ShapeDtypeStruct((tiles, QB + 1, LANES), jnp.float32),
        in_specs=[vmem] * len(more),
        out_specs=vmem,
        scratch_shapes=scratch,
        compiler_params=pltpu.CompilerParams(vmem_limit_bytes=32 * 1024 * 1024),
        cost_estimate=pl.CostEstimate(
            flops=2 * passages.size * tokens, bytes_accessed=2 * passages.size, transcendentals=0
        ),
    )(*more)


def place_kernel(in_ref, out_ref):
    slots = out_ref.shape[-1]
    m = lax.broadcasted_iota(jnp.int32, (PBS, LANES), 0)
    for j in range(in_ref.shape[0]):
        row = in_ref[j, QB:QB + 1, :].astype(jnp.int32)
        where = jnp.minimum(row * PBS, LANES - PBS) + m
        for i in range(QB):
            tile = jnp.broadcast_to(in_ref[j, i:i + 1, :], (PBS, LANES))
            out_ref[j, i] = jnp.take_along_axis(tile, where, axis=1)[:, :slots]


def place(tiles, slots):
    vmem = pl.BlockSpec(memory_space=pltpu.VMEM)
    shards = tiles.shape[0]
    return pl.pallas_call(
        place_kernel,
        out_shape=jax.ShapeDtypeStruct((shards, QB, PBS, slots), jnp.float32),
        in_specs=[vmem],
        out_specs=vmem,
        compiler_params=pltpu.CompilerParams(vmem_limit_bytes=8 * 1024 * 1024),
    )(tiles)


def by_planes(own, shards, candidates, lengths, passages):
    planes = shards // 2

    def swap_sides(x):
        return lax.ppermute(x, "psg", [(j, j ^ 1) for j in range(shards)])

    def shift(x, step):
        return lax.ppermute(x, "psg", [(j, (j + 2 * step) % shards) for j in range(shards)])

    theirs = swap_sides(candidates)
    sent, prepared = lax.optimization_barrier((own, prepare_early(lengths, passages)))
    shifted = [shift(own if step == 1 else sent, step) for step in range(1, planes)]
    slots, picks, clean = prepare(shards, candidates, lengths, passages, prepared)
    clean, *early = lax.optimization_barrier((clean, *reversed(shifted[:planes // 2 - 1])))
    early, late = [own, *reversed(early)], shifted[planes // 2 - 1:]
    steps = list(range(planes))
    first, last = steps[:planes // 2], steps[planes // 2:]
    packed = pack(first, planes, theirs, early)
    first_far = swap_sides(packed)
    *late, _ = lax.optimization_barrier((*late, packed))
    last_far = swap_sides(pack(last, planes, theirs, late))
    near_tiles = score(near_kernel, planes, planes, False, clean, slots, picks, clean, *early, *late)
    first_far, near_tiles = lax.optimization_barrier((first_far, near_tiles))
    far_tiles = score(
        functools.partial(some_far_kernel, first, planes), len(first), len(first), True, clean, slots, clean, first_far
    )
    last_far, far_tiles = lax.optimization_barrier((last_far, far_tiles))
    return score(
        functools.partial(last_far_kernel, last, planes), shards, len(last), True, clean,
        slots, clean, last_far, near_tiles, far_tiles,
    )


def by_gather(own, shards, candidates, lengths, passages):
    slots, picks, clean = prepare(shards, candidates, lengths, passages)
    gathered = lax.all_gather(own, "psg", axis=0)
    some = min(shards, 8)

    def score_some(items):
        return score(all_kernel, some, some, False, clean, items[0], items[1], clean, items[2])

    parts = [x.reshape(shards // some, some, *x.shape[1:]) for x in (slots, picks, gathered)]
    return lax.map(score_some, parts).reshape(shards, QB + 1, LANES)


def per_device(queries, passages, lengths, candidates):
    shards = lax.axis_size("psg")
    rows = passages.shape[0] // PBS
    form = by_planes if shards == 8 else by_gather
    tiles = form(
        queries.reshape(QBD * QB * QT, DIM), shards, candidates.reshape(rows, KB), lengths, passages
    )
    tiles = lax.all_to_all(tiles, "psg", split_axis=0, concat_axis=0, tiled=True)
    return place(tiles, rows * KB // shards).transpose(0, 3, 1, 2)[None]


def solution(mesh):
    return jax.shard_map(
        per_device,
        mesh=mesh,
        in_specs=(
            P(("grp", "psg", "qry"), None, None),
            P(("grp", "psg"), None, None),
            P(("grp", "psg")),
            P("qry", ("grp", "psg"), None),
        ),
        out_specs=P(("grp", "psg", "qry"), None, None, None, None),
        check_vma=False,
    )
```

```python
import functools

import jax
import jax.numpy as jnp
from jax import lax
from jax.experimental import pallas as pl
from jax.experimental.pallas import tpu as pltpu
from jax.sharding import PartitionSpec as P

DIM = 128
QT = 32
PT = 64
QB = 2
QBD = 4
PBS = 16
KB = 32
LANES = 128
GROUP = 8


def prepare_kernel(
    cand_hbm, len_hbm, p_hbm, slots_ref, picks_ref, clean_ref, cand_ref, len_ref, raw_ref, sems
):
    rows = cand_ref.shape[0]
    shards = slots_ref.shape[0]
    groups = p_hbm.shape[0] // GROUP

    def fetch(g):
        part = pl.ds(g * GROUP, GROUP)
        return pltpu.make_async_copy(p_hbm.at[part], raw_ref.at[part], sems.at[g])

    fetch_cand = pltpu.make_async_copy(cand_hbm, cand_ref, sems.at[groups])
    fetch_len = pltpu.make_async_copy(len_hbm, len_ref, sems.at[groups + 1])
    fetch_cand.start()
    fetch_len.start()
    for g in range(groups):
        fetch(g).start()

    fetch_cand.wait()
    cand = cand_ref[...]
    owner = cand // QBD
    block = cand - owner * QBD
    lane = lax.broadcasted_iota(jnp.int32, (rows, LANES), 1).astype(jnp.float32)
    sub = lax.broadcasted_iota(jnp.int32, (rows, LANES), 0)
    for o in range(shards):
        mine = owner == o
        named = jnp.max(jnp.where(mine, block, 0), axis=1, keepdims=True)
        picks_ref[o:o + 1, :] = jnp.broadcast_to(jnp.max(named, axis=0, keepdims=True), (1, LANES))
        named_here = jnp.sum(jnp.where(mine, 1.0, 0.0), axis=1, keepdims=True)
        upto = jnp.broadcast_to(named_here, (rows, LANES))
        step = 1
        while step < rows:
            upto = upto + jnp.where(sub >= step, pltpu.roll(upto, step, 0), 0.0)
            step *= 2
        slots_ref[o:o + 1, :] = jnp.sum(jnp.where(upto <= lane, 1.0, 0.0), axis=0, keepdims=True)

    fetch_len.wait()
    u = lax.broadcasted_iota(jnp.int32, (PT, LANES), 0)

    @pl.loop(0, groups)
    def _(g):
        fetch(g).wait()
        for i in range(GROUP):
            p = g * GROUP + i
            tokens = raw_ref[p].astype(jnp.float32)
            clean_ref[p] = jnp.where(u < len_ref[p], tokens, tokens[0:1]).astype(jnp.bfloat16)


def prepare(shards, candidates, lengths, passages):
    hbm = pl.BlockSpec(memory_space=pltpu.HBM)
    vmem = pl.BlockSpec(memory_space=pltpu.VMEM)
    operands = [pltpu.with_memory_space_constraint(x, pltpu.HBM) for x in (candidates, lengths, passages)]
    return pl.pallas_call(
        prepare_kernel,
        out_shape=[
            jax.ShapeDtypeStruct((shards, LANES), jnp.float32),
            jax.ShapeDtypeStruct((shards, LANES), jnp.int32),
            jax.ShapeDtypeStruct(passages.shape, passages.dtype),
        ],
        in_specs=[hbm] * 3,
        out_specs=[vmem] * 3,
        scratch_shapes=[
            pltpu.VMEM(candidates.shape, candidates.dtype),
            pltpu.SMEM(lengths.shape, lengths.dtype),
            pltpu.VMEM(passages.shape, passages.dtype),
            pltpu.SemaphoreType.DMA((passages.shape[0] // GROUP + 2,)),
        ],
        compiler_params=pltpu.CompilerParams(vmem_limit_bytes=24 * 1024 * 1024),
        cost_estimate=pl.CostEstimate(flops=passages.size, bytes_accessed=2 * passages.size, transcendentals=0),
    )(*operands)


def near_owner(me, step, planes):
    return me ^ 2 * step


def picked(picks_ref, owner, q_ref):
    pick = jnp.max(picks_ref[pl.ds(owner, 1), :])
    return q_ref[pl.ds(pick * QB * QT, QB * QT), :]


def pack_kernel(steps, planes, cand_ref, *refs):
    q_refs, out_ref = refs[:-1], refs[-1]
    me = lax.axis_index("psg")
    cand = cand_ref[...]
    owner = cand // QBD
    block = cand - owner * QBD
    for n, step in enumerate(steps):
        pick = jnp.max(jnp.where(owner == near_owner(me, step, planes), block, 0))
        out_ref[n * QB * QT:(n + 1) * QB * QT, :] = q_refs[n][pl.ds(pick * QB * QT, QB * QT), :]


def pack(steps, planes, candidates, blocks):
    vmem = pl.BlockSpec(memory_space=pltpu.VMEM)
    return pl.pallas_call(
        functools.partial(pack_kernel, steps, planes),
        out_shape=jax.ShapeDtypeStruct((len(blocks) * QB * QT, DIM), blocks[0].dtype),
        in_specs=[vmem] * (1 + len(blocks)),
        out_specs=vmem,
        compiler_params=pltpu.CompilerParams(vmem_limit_bytes=4 * 1024 * 1024),
    )(candidates, *blocks)


def sum_tokens(best):
    tokens = best.shape[1]
    high = best.astype(jnp.bfloat16)
    rest = best - high.astype(jnp.float32)
    mid = rest.astype(jnp.bfloat16)
    low = (rest - mid.astype(jnp.float32)).astype(jnp.bfloat16)
    parts = jnp.concatenate([low, mid, high], axis=1)
    query = lax.broadcasted_iota(jnp.int32, (tokens // QT, tokens), 0)
    token = lax.broadcasted_iota(jnp.int32, (tokens // QT, tokens), 1)
    ones = jnp.where(token // QT == query, 1.0, 0.0).astype(jnp.bfloat16)
    total = lax.dot_general(
        jnp.concatenate([ones] * 3, axis=1), parts, (((1,), (1,)), ((), ())), preferred_element_type=jnp.float32
    )
    return total * (1.0 / QT)


def best_tokens(left_of, sel, max_ref, piece):
    count, tokens = max_ref.shape
    for g in range(0, count, piece):
        dots = lax.dot_general(left_of(g, piece), sel, (((1,), (1,)), ((), ())), preferred_element_type=jnp.float32)
        max_ref[g:g + piece, :] = jnp.max(dots.reshape(piece, PT, tokens), axis=1)
    return max_ref[...]


def score_picked(sel, p_ref, max_ref):
    def left_of(g, piece):
        return p_ref[g:g + piece].reshape(piece * PT, DIM)

    return sum_tokens(best_tokens(left_of, sel, max_ref, 2 * GROUP))


def score_picked_few(sel, p_ref, wide_ref, max_ref):
    tokens, half = sel.shape[0], p_ref.shape[0] // 2
    wide_ref[...] = jnp.zeros_like(wide_ref)
    wide_ref[0:tokens, 0:DIM] = sel
    wide_ref[tokens:, DIM:] = sel

    def left_of(g, piece):
        return jnp.concatenate(
            [p_ref[h + g:h + g + piece].reshape(piece * PT, DIM) for h in (0, half)], axis=1
        )

    total = sum_tokens(best_tokens(left_of, wide_ref[...], max_ref, GROUP))
    queries = tokens // QT
    return jnp.concatenate([total[:queries], total[queries:]], axis=1)


def put(out_ref, place, total, n, slots_ref, owner):
    out_ref[place, 0:QB, :] = total[n * QB:(n + 1) * QB]
    out_ref[place, QB:QB + 1, :] = slots_ref[pl.ds(owner, 1), :]


def near_kernel(slots_ref, picks_ref, p_ref, *refs):
    q_refs, (out_ref, sel_ref, max_ref) = refs[:-3], refs[-3:]
    me = lax.axis_index("psg")
    owners = [near_owner(me, n, len(q_refs)) for n in range(len(q_refs))]
    for n, owner in enumerate(owners):
        sel_ref[n * QB * QT:(n + 1) * QB * QT, :] = picked(picks_ref, owner, q_refs[n])
    total = score_picked(sel_ref[...], p_ref, max_ref)
    for n, owner in enumerate(owners):
        put(out_ref, n, total, n, slots_ref, owner)


def some_far_kernel(steps, planes, slots_ref, p_ref, sel_ref, out_ref, wide_ref, max_ref):
    me = lax.axis_index("psg")
    total = score_picked_few(sel_ref[...], p_ref, wide_ref, max_ref)
    for n, step in enumerate(steps):
        put(out_ref, n, total, n, slots_ref, near_owner(me, step, planes) ^ 1)


def last_far_kernel(steps, planes, slots_ref, p_ref, sel_ref, near_ref, far_ref, out_ref, wide_ref, max_ref):
    me = lax.axis_index("psg")
    total = score_picked_few(sel_ref[...], p_ref, wide_ref, max_ref)
    for n, step in enumerate(steps):
        owner = near_owner(me, step, planes) ^ 1
        put(out_ref, owner, total, n, slots_ref, owner)
    others = [step for step in range(planes) if step not in steps]
    for step in range(planes):
        out_ref[near_owner(me, step, planes)] = near_ref[step]
    for n, step in enumerate(others):
        out_ref[near_owner(me, step, planes) ^ 1] = far_ref[n]


def all_kernel(slots_ref, picks_ref, p_ref, q_ref, out_ref, sel_ref, max_ref):
    some = q_ref.shape[0]
    for n in range(some):
        sel_ref[n * QB * QT:(n + 1) * QB * QT, :] = picked(picks_ref, n, q_ref.at[n])
    total = score_picked(sel_ref[...], p_ref, max_ref)
    for n in range(some):
        put(out_ref, n, total, n, slots_ref, n)


def score(kernel, tiles, some, few, passages, *more):
    count, tokens = passages.shape[0], some * QB * QT
    vmem = pl.BlockSpec(memory_space=pltpu.VMEM)
    if few:
        scratch = [pltpu.VMEM((2 * tokens, 2 * DIM), jnp.bfloat16), pltpu.VMEM((count // 2, 2 * tokens), jnp.float32)]
    else:
        scratch = [pltpu.VMEM((tokens, DIM), jnp.bfloat16), pltpu.VMEM((count, tokens), jnp.float32)]
    return pl.pallas_call(
        kernel,
        out_shape=jax.ShapeDtypeStruct((tiles, QB + 1, LANES), jnp.float32),
        in_specs=[vmem] * len(more),
        out_specs=vmem,
        scratch_shapes=scratch,
        compiler_params=pltpu.CompilerParams(vmem_limit_bytes=32 * 1024 * 1024),
        cost_estimate=pl.CostEstimate(
            flops=2 * passages.size * tokens, bytes_accessed=2 * passages.size, transcendentals=0
        ),
    )(*more)


def place_kernel(in_ref, out_ref):
    slots = out_ref.shape[-1]
    m = lax.broadcasted_iota(jnp.int32, (PBS, LANES), 0)
    for j in range(in_ref.shape[0]):
        row = in_ref[j, QB:QB + 1, :].astype(jnp.int32)
        where = jnp.minimum(row * PBS, LANES - PBS) + m
        for i in range(QB):
            tile = jnp.broadcast_to(in_ref[j, i:i + 1, :], (PBS, LANES))
            out_ref[j, i] = jnp.take_along_axis(tile, where, axis=1)[:, :slots]


def place(tiles, slots):
    vmem = pl.BlockSpec(memory_space=pltpu.VMEM)
    shards = tiles.shape[0]
    return pl.pallas_call(
        place_kernel,
        out_shape=jax.ShapeDtypeStruct((shards, QB, PBS, slots), jnp.float32),
        in_specs=[vmem],
        out_specs=vmem,
        compiler_params=pltpu.CompilerParams(vmem_limit_bytes=8 * 1024 * 1024),
    )(tiles)


def by_planes(own, shards, candidates, lengths, passages):
    planes = shards // 2

    def swap_sides(x):
        return lax.ppermute(x, "psg", [(j, j ^ 1) for j in range(shards)])

    def shift(x, step):
        return lax.ppermute(x, "psg", [(j, j ^ 2 * step) for j in range(shards)])

    theirs = swap_sides(candidates)
    shifted = [shift(own, step) for step in range(1, planes)]
    slots, picks, clean = prepare(shards, candidates, lengths, passages)
    first = [0, planes // 2]
    last = [step for step in range(planes) if step not in first]
    clean, shifted[first[1] - 1] = lax.optimization_barrier((clean, shifted[first[1] - 1]))
    blocks = [own, *shifted]
    packed = pack(first, planes, theirs, [blocks[step] for step in first])
    first_far = swap_sides(packed)
    *late, _ = lax.optimization_barrier((*[blocks[step] for step in last], packed))
    for step, block in zip(last, late):
        blocks[step] = block
    last_far = swap_sides(pack(last, planes, theirs, [blocks[step] for step in last]))
    near_tiles = score(near_kernel, planes, planes, False, clean, slots, picks, clean, *blocks)
    first_far, near_tiles = lax.optimization_barrier((first_far, near_tiles))
    far_tiles = score(
        functools.partial(some_far_kernel, first, planes), len(first), len(first), True, clean, slots, clean, first_far
    )
    last_far, far_tiles = lax.optimization_barrier((last_far, far_tiles))
    return score(
        functools.partial(last_far_kernel, last, planes), shards, len(last), True, clean,
        slots, clean, last_far, near_tiles, far_tiles,
    )


def by_gather(own, shards, candidates, lengths, passages):
    slots, picks, clean = prepare(shards, candidates, lengths, passages)
    gathered = lax.all_gather(own, "psg", axis=0)
    some = min(shards, 8)

    def score_some(items):
        return score(all_kernel, some, some, False, clean, items[0], items[1], clean, items[2])

    parts = [x.reshape(shards // some, some, *x.shape[1:]) for x in (slots, picks, gathered)]
    return lax.map(score_some, parts).reshape(shards, QB + 1, LANES)


def per_device(queries, passages, lengths, candidates):
    shards = lax.axis_size("psg")
    rows = passages.shape[0] // PBS
    form = by_planes if shards == 8 else by_gather
    tiles = form(
        queries.reshape(QBD * QB * QT, DIM), shards, candidates.reshape(rows, KB), lengths, passages
    )
    tiles = lax.all_to_all(tiles, "psg", split_axis=0, concat_axis=0, tiled=True)
    return place(tiles, rows * KB // shards).transpose(0, 3, 1, 2)[None]


def solution(mesh):
    return jax.shard_map(
        per_device,
        mesh=mesh,
        in_specs=(
            P(("grp", "psg", "qry"), None, None),
            P(("grp", "psg"), None, None),
            P(("grp", "psg")),
            P("qry", ("grp", "psg"), None),
        ),
        out_specs=P(("grp", "psg", "qry"), None, None, None, None),
        check_vma=False,
    )
```

```python
import functools

import jax
import jax.numpy as jnp
from jax import lax
from jax.experimental import pallas as pl
from jax.experimental.pallas import tpu as pltpu
from jax.sharding import PartitionSpec as P

DIM = 128
QT = 32
PT = 64
QB = 2
QBD = 4
PBS = 16
KB = 32
LANES = 128
GROUP = 8


def prepare_kernel(
    cand_hbm, len_hbm, p_hbm, slots_ref, picks_ref, clean_ref, cand_ref, len_ref, raw_ref, sems
):
    rows = cand_ref.shape[0]
    shards = slots_ref.shape[0]
    groups = p_hbm.shape[0] // GROUP

    def fetch(g):
        part = pl.ds(g * GROUP, GROUP)
        return pltpu.make_async_copy(p_hbm.at[part], raw_ref.at[part], sems.at[g])

    fetch_cand = pltpu.make_async_copy(cand_hbm, cand_ref, sems.at[groups])
    fetch_len = pltpu.make_async_copy(len_hbm, len_ref, sems.at[groups + 1])
    fetch_cand.start()
    fetch_len.start()
    for g in range(groups):
        fetch(g).start()

    fetch_cand.wait()
    cand = cand_ref[...]
    owner = cand // QBD
    block = cand - owner * QBD
    lane = lax.broadcasted_iota(jnp.int32, (rows, LANES), 1).astype(jnp.float32)
    sub = lax.broadcasted_iota(jnp.int32, (rows, LANES), 0)
    for o in range(shards):
        mine = owner == o
        named = jnp.max(jnp.where(mine, block, 0), axis=1, keepdims=True)
        picks_ref[o:o + 1, :] = jnp.broadcast_to(jnp.max(named, axis=0, keepdims=True), (1, LANES))
        named_here = jnp.sum(jnp.where(mine, 1.0, 0.0), axis=1, keepdims=True)
        upto = jnp.broadcast_to(named_here, (rows, LANES))
        step = 1
        while step < rows:
            upto = upto + jnp.where(sub >= step, pltpu.roll(upto, step, 0), 0.0)
            step *= 2
        slots_ref[o:o + 1, :] = jnp.sum(jnp.where(upto <= lane, 1.0, 0.0), axis=0, keepdims=True)

    fetch_len.wait()
    u = lax.broadcasted_iota(jnp.int32, (PT, LANES), 0)

    @pl.loop(0, groups)
    def _(g):
        fetch(g).wait()
        for i in range(GROUP):
            p = g * GROUP + i
            tokens = raw_ref[p].astype(jnp.float32)
            clean_ref[p] = jnp.where(u < len_ref[p], tokens, tokens[0:1]).astype(jnp.bfloat16)


def prepare(shards, candidates, lengths, passages):
    hbm = pl.BlockSpec(memory_space=pltpu.HBM)
    vmem = pl.BlockSpec(memory_space=pltpu.VMEM)
    operands = [pltpu.with_memory_space_constraint(x, pltpu.HBM) for x in (candidates, lengths, passages)]
    return pl.pallas_call(
        prepare_kernel,
        out_shape=[
            jax.ShapeDtypeStruct((shards, LANES), jnp.float32),
            jax.ShapeDtypeStruct((shards, LANES), jnp.int32),
            jax.ShapeDtypeStruct(passages.shape, passages.dtype),
        ],
        in_specs=[hbm] * 3,
        out_specs=[vmem] * 3,
        scratch_shapes=[
            pltpu.VMEM(candidates.shape, candidates.dtype),
            pltpu.SMEM(lengths.shape, lengths.dtype),
            pltpu.VMEM(passages.shape, passages.dtype),
            pltpu.SemaphoreType.DMA((passages.shape[0] // GROUP + 2,)),
        ],
        compiler_params=pltpu.CompilerParams(vmem_limit_bytes=24 * 1024 * 1024),
        cost_estimate=pl.CostEstimate(flops=passages.size, bytes_accessed=2 * passages.size, transcendentals=0),
    )(*operands)


def near_owner(me, step, planes):
    return me ^ 2 * step


def picked(picks_ref, owner, q_ref):
    pick = jnp.max(picks_ref[pl.ds(owner, 1), :])
    return q_ref[pl.ds(pick * QB * QT, QB * QT), :]


def pack_kernel(steps, planes, cand_ref, *refs):
    q_refs, out_ref = refs[:-1], refs[-1]
    me = lax.axis_index("psg")
    cand = cand_ref[...]
    owner = cand // QBD
    block = cand - owner * QBD
    for n, step in enumerate(steps):
        pick = jnp.max(jnp.where(owner == near_owner(me, step, planes), block, 0))
        out_ref[n * QB * QT:(n + 1) * QB * QT, :] = q_refs[n][pl.ds(pick * QB * QT, QB * QT), :]


def pack(steps, planes, candidates, blocks):
    vmem = pl.BlockSpec(memory_space=pltpu.VMEM)
    return pl.pallas_call(
        functools.partial(pack_kernel, steps, planes),
        out_shape=jax.ShapeDtypeStruct((len(blocks) * QB * QT, DIM), blocks[0].dtype),
        in_specs=[vmem] * (1 + len(blocks)),
        out_specs=vmem,
        compiler_params=pltpu.CompilerParams(vmem_limit_bytes=4 * 1024 * 1024),
    )(candidates, *blocks)


def sum_tokens(best):
    tokens = best.shape[1]
    high = best.astype(jnp.bfloat16)
    rest = best - high.astype(jnp.float32)
    mid = rest.astype(jnp.bfloat16)
    low = (rest - mid.astype(jnp.float32)).astype(jnp.bfloat16)
    parts = jnp.concatenate([low, mid, high], axis=1)
    query = lax.broadcasted_iota(jnp.int32, (tokens // QT, tokens), 0)
    token = lax.broadcasted_iota(jnp.int32, (tokens // QT, tokens), 1)
    ones = jnp.where(token // QT == query, 1.0, 0.0).astype(jnp.bfloat16)
    total = lax.dot_general(
        jnp.concatenate([ones] * 3, axis=1), parts, (((1,), (1,)), ((), ())), preferred_element_type=jnp.float32
    )
    return total * (1.0 / QT)


def best_tokens(left_of, sel, max_ref, piece):
    count, tokens = max_ref.shape
    for g in range(0, count, piece):
        dots = lax.dot_general(left_of(g, piece), sel, (((1,), (1,)), ((), ())), preferred_element_type=jnp.float32)
        max_ref[g:g + piece, :] = jnp.max(dots.reshape(piece, PT, tokens), axis=1)
    return max_ref[...]


def score_picked(sel, p_ref, max_ref):
    def left_of(g, piece):
        return p_ref[g:g + piece].reshape(piece * PT, DIM)

    return sum_tokens(best_tokens(left_of, sel, max_ref, 2 * GROUP))


def score_picked_few(sel, p_ref, wide_ref, max_ref):
    tokens, half = sel.shape[0], p_ref.shape[0] // 2
    wide_ref[...] = jnp.zeros_like(wide_ref)
    wide_ref[0:tokens, 0:DIM] = sel
    wide_ref[tokens:, DIM:] = sel

    def left_of(g, piece):
        return jnp.concatenate(
            [p_ref[h + g:h + g + piece].reshape(piece * PT, DIM) for h in (0, half)], axis=1
        )

    total = sum_tokens(best_tokens(left_of, wide_ref[...], max_ref, GROUP))
    queries = tokens // QT
    return jnp.concatenate([total[:queries], total[queries:]], axis=1)


def put(out_ref, place, total, n, slots_ref, owner):
    out_ref[place, 0:QB, :] = total[n * QB:(n + 1) * QB]
    out_ref[place, QB:QB + 1, :] = slots_ref[pl.ds(owner, 1), :]


def near_kernel(slots_ref, picks_ref, p_ref, *refs):
    q_refs, (out_ref, sel_ref, max_ref) = refs[:-3], refs[-3:]
    me = lax.axis_index("psg")
    owners = [near_owner(me, n, len(q_refs)) for n in range(len(q_refs))]
    for n, owner in enumerate(owners):
        sel_ref[n * QB * QT:(n + 1) * QB * QT, :] = picked(picks_ref, owner, q_refs[n])
    total = score_picked(sel_ref[...], p_ref, max_ref)
    for n, owner in enumerate(owners):
        put(out_ref, n, total, n, slots_ref, owner)


def some_far_kernel(steps, planes, slots_ref, p_ref, sel_ref, out_ref, wide_ref, max_ref):
    me = lax.axis_index("psg")
    total = score_picked_few(sel_ref[...], p_ref, wide_ref, max_ref)
    for n, step in enumerate(steps):
        put(out_ref, n, total, n, slots_ref, near_owner(me, step, planes) ^ 1)


def last_far_kernel(steps, planes, slots_ref, p_ref, sel_ref, near_ref, far_ref, out_ref, wide_ref, max_ref):
    me = lax.axis_index("psg")
    total = score_picked_few(sel_ref[...], p_ref, wide_ref, max_ref)
    for n, step in enumerate(steps):
        owner = near_owner(me, step, planes) ^ 1
        put(out_ref, owner, total, n, slots_ref, owner)
    others = [step for step in range(planes) if step not in steps]
    for step in range(planes):
        out_ref[near_owner(me, step, planes)] = near_ref[step]
    for n, step in enumerate(others):
        out_ref[near_owner(me, step, planes) ^ 1] = far_ref[n]


def all_kernel(slots_ref, picks_ref, p_ref, q_ref, out_ref, sel_ref, max_ref):
    some = q_ref.shape[0]
    for n in range(some):
        sel_ref[n * QB * QT:(n + 1) * QB * QT, :] = picked(picks_ref, n, q_ref.at[n])
    total = score_picked(sel_ref[...], p_ref, max_ref)
    for n in range(some):
        put(out_ref, n, total, n, slots_ref, n)


def score(kernel, tiles, some, few, passages, *more):
    count, tokens = passages.shape[0], some * QB * QT
    vmem = pl.BlockSpec(memory_space=pltpu.VMEM)
    if few:
        scratch = [pltpu.VMEM((2 * tokens, 2 * DIM), jnp.bfloat16), pltpu.VMEM((count // 2, 2 * tokens), jnp.float32)]
    else:
        scratch = [pltpu.VMEM((tokens, DIM), jnp.bfloat16), pltpu.VMEM((count, tokens), jnp.float32)]
    return pl.pallas_call(
        kernel,
        out_shape=jax.ShapeDtypeStruct((tiles, QB + 1, LANES), jnp.float32),
        in_specs=[vmem] * len(more),
        out_specs=vmem,
        scratch_shapes=scratch,
        compiler_params=pltpu.CompilerParams(vmem_limit_bytes=32 * 1024 * 1024),
        cost_estimate=pl.CostEstimate(
            flops=2 * passages.size * tokens, bytes_accessed=2 * passages.size, transcendentals=0
        ),
    )(*more)


def place_kernel(in_ref, out_ref):
    slots = out_ref.shape[-1]
    m = lax.broadcasted_iota(jnp.int32, (PBS, LANES), 0)
    for j in range(in_ref.shape[0]):
        row = in_ref[j, QB:QB + 1, :].astype(jnp.int32)
        where = jnp.minimum(row * PBS, LANES - PBS) + m
        for i in range(QB):
            tile = jnp.broadcast_to(in_ref[j, i:i + 1, :], (PBS, LANES))
            out_ref[j, i] = jnp.take_along_axis(tile, where, axis=1)[:, :slots]


def place(tiles, slots):
    vmem = pl.BlockSpec(memory_space=pltpu.VMEM)
    shards = tiles.shape[0]
    return pl.pallas_call(
        place_kernel,
        out_shape=jax.ShapeDtypeStruct((shards, QB, PBS, slots), jnp.float32),
        in_specs=[vmem],
        out_specs=vmem,
        compiler_params=pltpu.CompilerParams(vmem_limit_bytes=8 * 1024 * 1024),
    )(tiles)


def by_planes(own, shards, candidates, lengths, passages):
    planes = shards // 2

    def swap_sides(x):
        return lax.ppermute(x, "psg", [(j, j ^ 1) for j in range(shards)])

    def shift(x, step):
        return lax.ppermute(x, "psg", [(j, j ^ 2 * step) for j in range(shards)])

    theirs = swap_sides(candidates)
    shifted = [shift(own, step) for step in range(1, planes)]
    slots, picks, clean = prepare(shards, candidates, lengths, passages)
    first = [0, planes // 2]
    last = [step for step in range(planes) if step not in first]
    clean, shifted[first[1] - 1] = lax.optimization_barrier((clean, shifted[first[1] - 1]))
    blocks = [own, *shifted]
    packed = pack(first, planes, theirs, [blocks[step] for step in first])
    first_far = swap_sides(packed)
    *late, _ = lax.optimization_barrier((*[blocks[step] for step in reversed(last)], packed))
    for step, block in zip(reversed(last), late):
        blocks[step] = block
    last_far = swap_sides(pack(last, planes, theirs, [blocks[step] for step in last]))
    near_tiles = score(near_kernel, planes, planes, False, clean, slots, picks, clean, *blocks)
    first_far, near_tiles = lax.optimization_barrier((first_far, near_tiles))
    far_tiles = score(
        functools.partial(some_far_kernel, first, planes), len(first), len(first), True, clean, slots, clean, first_far
    )
    last_far, far_tiles = lax.optimization_barrier((last_far, far_tiles))
    return score(
        functools.partial(last_far_kernel, last, planes), shards, len(last), True, clean,
        slots, clean, last_far, near_tiles, far_tiles,
    )


def by_gather(own, shards, candidates, lengths, passages):
    slots, picks, clean = prepare(shards, candidates, lengths, passages)
    gathered = lax.all_gather(own, "psg", axis=0)
    some = min(shards, 8)

    def score_some(items):
        return score(all_kernel, some, some, False, clean, items[0], items[1], clean, items[2])

    parts = [x.reshape(shards // some, some, *x.shape[1:]) for x in (slots, picks, gathered)]
    return lax.map(score_some, parts).reshape(shards, QB + 1, LANES)


def per_device(queries, passages, lengths, candidates):
    shards = lax.axis_size("psg")
    rows = passages.shape[0] // PBS
    form = by_planes if shards == 8 else by_gather
    tiles = form(
        queries.reshape(QBD * QB * QT, DIM), shards, candidates.reshape(rows, KB), lengths, passages
    )
    tiles = lax.all_to_all(tiles, "psg", split_axis=0, concat_axis=0, tiled=True)
    return place(tiles, rows * KB // shards).transpose(0, 3, 1, 2)[None]


def solution(mesh):
    return jax.shard_map(
        per_device,
        mesh=mesh,
        in_specs=(
            P(("grp", "psg", "qry"), None, None),
            P(("grp", "psg"), None, None),
            P(("grp", "psg")),
            P("qry", ("grp", "psg"), None),
        ),
        out_specs=P(("grp", "psg", "qry"), None, None, None, None),
        check_vma=False,
    )
```

```python
import functools

import jax
import jax.numpy as jnp
from jax import lax
from jax.experimental import pallas as pl
from jax.experimental.pallas import tpu as pltpu
from jax.sharding import PartitionSpec as P

DIM = 128
QT = 32
PT = 64
QB = 2
QBD = 4
PBS = 16
KB = 32
LANES = 128
GROUP = 8


def prepare_kernel(
    cand_hbm, len_hbm, p_hbm, slots_ref, picks_ref, clean_ref, cand_ref, len_ref, raw_ref, sems
):
    rows = cand_ref.shape[0]
    shards = slots_ref.shape[0]
    groups = p_hbm.shape[0] // GROUP

    def fetch(g):
        part = pl.ds(g * GROUP, GROUP)
        return pltpu.make_async_copy(p_hbm.at[part], raw_ref.at[part], sems.at[g])

    fetch_cand = pltpu.make_async_copy(cand_hbm, cand_ref, sems.at[groups])
    fetch_len = pltpu.make_async_copy(len_hbm, len_ref, sems.at[groups + 1])
    fetch_cand.start()
    fetch_len.start()
    for g in range(groups):
        fetch(g).start()

    fetch_cand.wait()
    cand = cand_ref[...]
    owner = cand // QBD
    block = cand - owner * QBD
    lane = lax.broadcasted_iota(jnp.int32, (rows, LANES), 1).astype(jnp.float32)
    sub = lax.broadcasted_iota(jnp.int32, (rows, LANES), 0)
    for o in range(shards):
        mine = owner == o
        named = jnp.max(jnp.where(mine, block, 0), axis=1, keepdims=True)
        picks_ref[o:o + 1, :] = jnp.broadcast_to(jnp.max(named, axis=0, keepdims=True), (1, LANES))
        named_here = jnp.sum(jnp.where(mine, 1.0, 0.0), axis=1, keepdims=True)
        upto = jnp.broadcast_to(named_here, (rows, LANES))
        step = 1
        while step < rows:
            upto = upto + jnp.where(sub >= step, pltpu.roll(upto, step, 0), 0.0)
            step *= 2
        slots_ref[o:o + 1, :] = jnp.sum(jnp.where(upto <= lane, 1.0, 0.0), axis=0, keepdims=True)

    fetch_len.wait()
    u = lax.broadcasted_iota(jnp.int32, (PT, LANES), 0)

    @pl.loop(0, groups)
    def _(g):
        fetch(g).wait()
        for i in range(GROUP):
            p = g * GROUP + i
            tokens = raw_ref[p].astype(jnp.float32)
            clean_ref[p] = jnp.where(u < len_ref[p], tokens, tokens[0:1]).astype(jnp.bfloat16)


def prepare(shards, candidates, lengths, passages):
    hbm = pl.BlockSpec(memory_space=pltpu.HBM)
    vmem = pl.BlockSpec(memory_space=pltpu.VMEM)
    operands = [pltpu.with_memory_space_constraint(x, pltpu.HBM) for x in (candidates, lengths, passages)]
    return pl.pallas_call(
        prepare_kernel,
        out_shape=[
            jax.ShapeDtypeStruct((shards, LANES), jnp.float32),
            jax.ShapeDtypeStruct((shards, LANES), jnp.int32),
            jax.ShapeDtypeStruct(passages.shape, passages.dtype),
        ],
        in_specs=[hbm] * 3,
        out_specs=[vmem] * 3,
        scratch_shapes=[
            pltpu.VMEM(candidates.shape, candidates.dtype),
            pltpu.SMEM(lengths.shape, lengths.dtype),
            pltpu.VMEM(passages.shape, passages.dtype),
            pltpu.SemaphoreType.DMA((passages.shape[0] // GROUP + 2,)),
        ],
        compiler_params=pltpu.CompilerParams(vmem_limit_bytes=24 * 1024 * 1024),
        cost_estimate=pl.CostEstimate(flops=passages.size, bytes_accessed=2 * passages.size, transcendentals=0),
    )(*operands)


def near_owner(me, step, planes):
    return me ^ 2 * step


def picked(picks_ref, owner, q_ref):
    pick = jnp.max(picks_ref[pl.ds(owner, 1), :])
    return q_ref[pl.ds(pick * QB * QT, QB * QT), :]


def pack_kernel(steps, planes, cand_ref, *refs):
    q_refs, out_ref = refs[:-1], refs[-1]
    me = lax.axis_index("psg")
    cand = cand_ref[...]
    owner = cand // QBD
    block = cand - owner * QBD
    for n, step in enumerate(steps):
        pick = jnp.max(jnp.where(owner == near_owner(me, step, planes), block, 0))
        out_ref[n * QB * QT:(n + 1) * QB * QT, :] = q_refs[n][pl.ds(pick * QB * QT, QB * QT), :]


def pack(steps, planes, candidates, blocks):
    vmem = pl.BlockSpec(memory_space=pltpu.VMEM)
    return pl.pallas_call(
        functools.partial(pack_kernel, steps, planes),
        out_shape=jax.ShapeDtypeStruct((len(blocks) * QB * QT, DIM), blocks[0].dtype),
        in_specs=[vmem] * (1 + len(blocks)),
        out_specs=vmem,
        compiler_params=pltpu.CompilerParams(vmem_limit_bytes=4 * 1024 * 1024),
    )(candidates, *blocks)


def sum_tokens(best):
    tokens = best.shape[1]
    high = best.astype(jnp.bfloat16)
    rest = best - high.astype(jnp.float32)
    mid = rest.astype(jnp.bfloat16)
    low = (rest - mid.astype(jnp.float32)).astype(jnp.bfloat16)
    parts = jnp.concatenate([low, mid, high], axis=1)
    query = lax.broadcasted_iota(jnp.int32, (tokens // QT, tokens), 0)
    token = lax.broadcasted_iota(jnp.int32, (tokens // QT, tokens), 1)
    ones = jnp.where(token // QT == query, 1.0, 0.0).astype(jnp.bfloat16)
    total = lax.dot_general(
        jnp.concatenate([ones] * 3, axis=1), parts, (((1,), (1,)), ((), ())), preferred_element_type=jnp.float32
    )
    return total * (1.0 / QT)


def best_tokens(left_of, sel, max_ref, piece):
    count, tokens = max_ref.shape
    for g in range(0, count, piece):
        dots = lax.dot_general(left_of(g, piece), sel, (((1,), (1,)), ((), ())), preferred_element_type=jnp.float32)
        max_ref[g:g + piece, :] = jnp.max(dots.reshape(piece, PT, tokens), axis=1)
    return max_ref[...]


def score_picked(sel, p_ref, max_ref):
    def left_of(g, piece):
        return p_ref[g:g + piece].reshape(piece * PT, DIM)

    return sum_tokens(best_tokens(left_of, sel, max_ref, 2 * GROUP))


def score_picked_few(sel, p_ref, wide_ref, max_ref):
    tokens, half = sel.shape[0], p_ref.shape[0] // 2
    wide_ref[...] = jnp.zeros_like(wide_ref)
    wide_ref[0:tokens, 0:DIM] = sel
    wide_ref[tokens:, DIM:] = sel

    def left_of(g, piece):
        return jnp.concatenate(
            [p_ref[h + g:h + g + piece].reshape(piece * PT, DIM) for h in (0, half)], axis=1
        )

    total = sum_tokens(best_tokens(left_of, wide_ref[...], max_ref, GROUP))
    queries = tokens // QT
    return jnp.concatenate([total[:queries], total[queries:]], axis=1)


def put(out_ref, place, total, n, slots_ref, owner):
    out_ref[place, 0:QB, :] = total[n * QB:(n + 1) * QB]
    out_ref[place, QB:QB + 1, :] = slots_ref[pl.ds(owner, 1), :]


def near_kernel(slots_ref, picks_ref, p_ref, *refs):
    q_refs, (out_ref, sel_ref, max_ref) = refs[:-3], refs[-3:]
    me = lax.axis_index("psg")
    owners = [near_owner(me, n, len(q_refs)) for n in range(len(q_refs))]
    for n, owner in enumerate(owners):
        sel_ref[n * QB * QT:(n + 1) * QB * QT, :] = picked(picks_ref, owner, q_refs[n])
    total = score_picked(sel_ref[...], p_ref, max_ref)
    for n, owner in enumerate(owners):
        put(out_ref, n, total, n, slots_ref, owner)


def some_far_kernel(steps, planes, slots_ref, p_ref, sel_ref, out_ref, wide_ref, max_ref):
    me = lax.axis_index("psg")
    total = score_picked_few(sel_ref[...], p_ref, wide_ref, max_ref)
    for n, step in enumerate(steps):
        put(out_ref, n, total, n, slots_ref, near_owner(me, step, planes) ^ 1)


def last_far_kernel(steps, planes, slots_ref, p_ref, sel_ref, near_ref, far_ref, out_ref, wide_ref, max_ref):
    me = lax.axis_index("psg")
    total = score_picked_few(sel_ref[...], p_ref, wide_ref, max_ref)
    for n, step in enumerate(steps):
        owner = near_owner(me, step, planes) ^ 1
        put(out_ref, owner, total, n, slots_ref, owner)
    others = [step for step in range(planes) if step not in steps]
    for step in range(planes):
        out_ref[near_owner(me, step, planes)] = near_ref[step]
    for n, step in enumerate(others):
        out_ref[near_owner(me, step, planes) ^ 1] = far_ref[n]


def all_kernel(slots_ref, picks_ref, p_ref, q_ref, out_ref, sel_ref, max_ref):
    some = q_ref.shape[0]
    for n in range(some):
        sel_ref[n * QB * QT:(n + 1) * QB * QT, :] = picked(picks_ref, n, q_ref.at[n])
    total = score_picked(sel_ref[...], p_ref, max_ref)
    for n in range(some):
        put(out_ref, n, total, n, slots_ref, n)


def score(kernel, tiles, some, few, passages, *more):
    count, tokens = passages.shape[0], some * QB * QT
    vmem = pl.BlockSpec(memory_space=pltpu.VMEM)
    if few:
        scratch = [pltpu.VMEM((2 * tokens, 2 * DIM), jnp.bfloat16), pltpu.VMEM((count // 2, 2 * tokens), jnp.float32)]
    else:
        scratch = [pltpu.VMEM((tokens, DIM), jnp.bfloat16), pltpu.VMEM((count, tokens), jnp.float32)]
    return pl.pallas_call(
        kernel,
        out_shape=jax.ShapeDtypeStruct((tiles, QB + 1, LANES), jnp.float32),
        in_specs=[vmem] * len(more),
        out_specs=vmem,
        scratch_shapes=scratch,
        compiler_params=pltpu.CompilerParams(vmem_limit_bytes=32 * 1024 * 1024),
        cost_estimate=pl.CostEstimate(
            flops=2 * passages.size * tokens, bytes_accessed=2 * passages.size, transcendentals=0
        ),
    )(*more)


def place_kernel(in_ref, out_ref):
    slots = out_ref.shape[-1]
    m = lax.broadcasted_iota(jnp.int32, (PBS, LANES), 0)
    for j in range(in_ref.shape[0]):
        row = in_ref[j, QB:QB + 1, :].astype(jnp.int32)
        where = jnp.minimum(row * PBS, LANES - PBS) + m
        for i in range(QB):
            tile = jnp.broadcast_to(in_ref[j, i:i + 1, :], (PBS, LANES))
            out_ref[j, i] = jnp.take_along_axis(tile, where, axis=1)[:, :slots]


def place(tiles, slots):
    vmem = pl.BlockSpec(memory_space=pltpu.VMEM)
    shards = tiles.shape[0]
    return pl.pallas_call(
        place_kernel,
        out_shape=jax.ShapeDtypeStruct((shards, QB, PBS, slots), jnp.float32),
        in_specs=[vmem],
        out_specs=vmem,
        compiler_params=pltpu.CompilerParams(vmem_limit_bytes=8 * 1024 * 1024),
    )(tiles)


def by_planes(own, shards, candidates, lengths, passages):
    planes = shards // 2

    def swap_sides(x):
        return lax.ppermute(x, "psg", [(j, j ^ 1) for j in range(shards)])

    def shift(x, step):
        return lax.ppermute(x, "psg", [(j, j ^ 2 * step) for j in range(shards)])

    theirs = swap_sides(candidates)
    shifted = [shift(own, step) for step in range(1, planes)]
    slots, picks, clean = prepare(shards, candidates, lengths, passages)
    first, last = [0], [2, 3, 1]
    theirs, clean = lax.optimization_barrier((theirs, clean))
    packed = pack(first, planes, theirs, [own])
    first_far = swap_sides(packed)
    blocks = [own, *shifted]
    *late, _ = lax.optimization_barrier((*[blocks[step] for step in last], packed))
    for step, block in zip(last, late):
        blocks[step] = block
    last_far = swap_sides(pack(last, planes, theirs, [blocks[step] for step in last]))
    near_tiles = score(near_kernel, planes, planes, False, clean, slots, picks, clean, *blocks)
    first_far, near_tiles = lax.optimization_barrier((first_far, near_tiles))
    far_tiles = score(
        functools.partial(some_far_kernel, first, planes), len(first), len(first), True, clean, slots, clean, first_far
    )
    last_far, far_tiles = lax.optimization_barrier((last_far, far_tiles))
    return score(
        functools.partial(last_far_kernel, last, planes), shards, len(last), True, clean,
        slots, clean, last_far, near_tiles, far_tiles,
    )


def by_gather(own, shards, candidates, lengths, passages):
    slots, picks, clean = prepare(shards, candidates, lengths, passages)
    gathered = lax.all_gather(own, "psg", axis=0)
    some = min(shards, 8)

    def score_some(items):
        return score(all_kernel, some, some, False, clean, items[0], items[1], clean, items[2])

    parts = [x.reshape(shards // some, some, *x.shape[1:]) for x in (slots, picks, gathered)]
    return lax.map(score_some, parts).reshape(shards, QB + 1, LANES)


def per_device(queries, passages, lengths, candidates):
    shards = lax.axis_size("psg")
    rows = passages.shape[0] // PBS
    form = by_planes if shards == 8 else by_gather
    tiles = form(
        queries.reshape(QBD * QB * QT, DIM), shards, candidates.reshape(rows, KB), lengths, passages
    )
    tiles = lax.all_to_all(tiles, "psg", split_axis=0, concat_axis=0, tiled=True)
    return place(tiles, rows * KB // shards).transpose(0, 3, 1, 2)[None]


def solution(mesh):
    return jax.shard_map(
        per_device,
        mesh=mesh,
        in_specs=(
            P(("grp", "psg", "qry"), None, None),
            P(("grp", "psg"), None, None),
            P(("grp", "psg")),
            P("qry", ("grp", "psg"), None),
        ),
        out_specs=P(("grp", "psg", "qry"), None, None, None, None),
        check_vma=False,
    )
```

```python
import functools

import jax
import jax.numpy as jnp
from jax import lax
from jax.experimental import pallas as pl
from jax.experimental.pallas import tpu as pltpu
from jax.sharding import PartitionSpec as P

DIM = 128
QT = 32
PT = 64
QB = 2
QBD = 4
PBS = 16
KB = 32
LANES = 128
GROUP = 8


def prepare_kernel(
    cand_hbm, len_hbm, p_hbm, slots_ref, picks_ref, clean_ref, cand_ref, len_ref, raw_ref, sems
):
    rows = cand_ref.shape[0]
    shards = slots_ref.shape[0]
    groups = p_hbm.shape[0] // GROUP

    def fetch(g):
        part = pl.ds(g * GROUP, GROUP)
        return pltpu.make_async_copy(p_hbm.at[part], raw_ref.at[part], sems.at[g])

    fetch_cand = pltpu.make_async_copy(cand_hbm, cand_ref, sems.at[groups])
    fetch_len = pltpu.make_async_copy(len_hbm, len_ref, sems.at[groups + 1])
    fetch_cand.start()
    fetch_len.start()
    for g in range(groups):
        fetch(g).start()

    fetch_cand.wait()
    cand = cand_ref[...]
    owner = cand // QBD
    block = cand - owner * QBD
    lane = lax.broadcasted_iota(jnp.int32, (rows, LANES), 1).astype(jnp.float32)
    sub = lax.broadcasted_iota(jnp.int32, (rows, LANES), 0)
    for o in range(shards):
        mine = owner == o
        named = jnp.max(jnp.where(mine, block, 0), axis=1, keepdims=True)
        picks_ref[o:o + 1, :] = jnp.broadcast_to(jnp.max(named, axis=0, keepdims=True), (1, LANES))
        named_here = jnp.sum(jnp.where(mine, 1.0, 0.0), axis=1, keepdims=True)
        upto = jnp.broadcast_to(named_here, (rows, LANES))
        step = 1
        while step < rows:
            upto = upto + jnp.where(sub >= step, pltpu.roll(upto, step, 0), 0.0)
            step *= 2
        slots_ref[o:o + 1, :] = jnp.sum(jnp.where(upto <= lane, 1.0, 0.0), axis=0, keepdims=True)

    fetch_len.wait()
    u = lax.broadcasted_iota(jnp.int32, (PT, LANES), 0)

    @pl.loop(0, groups)
    def _(g):
        fetch(g).wait()
        for i in range(GROUP):
            p = g * GROUP + i
            tokens = raw_ref[p].astype(jnp.float32)
            clean_ref[p] = jnp.where(u < len_ref[p], tokens, tokens[0:1]).astype(jnp.bfloat16)


def prepare(shards, candidates, lengths, passages):
    hbm = pl.BlockSpec(memory_space=pltpu.HBM)
    vmem = pl.BlockSpec(memory_space=pltpu.VMEM)
    operands = [pltpu.with_memory_space_constraint(x, pltpu.HBM) for x in (candidates, lengths, passages)]
    return pl.pallas_call(
        prepare_kernel,
        out_shape=[
            jax.ShapeDtypeStruct((shards, LANES), jnp.float32),
            jax.ShapeDtypeStruct((shards, LANES), jnp.int32),
            jax.ShapeDtypeStruct(passages.shape, passages.dtype),
        ],
        in_specs=[hbm] * 3,
        out_specs=[vmem] * 3,
        scratch_shapes=[
            pltpu.VMEM(candidates.shape, candidates.dtype),
            pltpu.SMEM(lengths.shape, lengths.dtype),
            pltpu.VMEM(passages.shape, passages.dtype),
            pltpu.SemaphoreType.DMA((passages.shape[0] // GROUP + 2,)),
        ],
        compiler_params=pltpu.CompilerParams(vmem_limit_bytes=24 * 1024 * 1024),
        cost_estimate=pl.CostEstimate(flops=passages.size, bytes_accessed=2 * passages.size, transcendentals=0),
    )(*operands)


def near_owner(me, step, planes):
    return me ^ 2 * step


def picked(picks_ref, owner, q_ref):
    pick = jnp.max(picks_ref[pl.ds(owner, 1), :])
    return q_ref[pl.ds(pick * QB * QT, QB * QT), :]


def pack_kernel(steps, planes, cand_ref, *refs):
    q_refs, out_ref = refs[:-1], refs[-1]
    me = lax.axis_index("psg")
    cand = cand_ref[...]
    owner = cand // QBD
    block = cand - owner * QBD
    for n, step in enumerate(steps):
        pick = jnp.max(jnp.where(owner == near_owner(me, step, planes), block, 0))
        out_ref[n * QB * QT:(n + 1) * QB * QT, :] = q_refs[n][pl.ds(pick * QB * QT, QB * QT), :]


def pack(steps, planes, candidates, blocks):
    vmem = pl.BlockSpec(memory_space=pltpu.VMEM)
    return pl.pallas_call(
        functools.partial(pack_kernel, steps, planes),
        out_shape=jax.ShapeDtypeStruct((len(blocks) * QB * QT, DIM), blocks[0].dtype),
        in_specs=[vmem] * (1 + len(blocks)),
        out_specs=vmem,
        compiler_params=pltpu.CompilerParams(vmem_limit_bytes=4 * 1024 * 1024),
    )(candidates, *blocks)


def sum_tokens(best):
    tokens = best.shape[1]
    high = best.astype(jnp.bfloat16)
    rest = best - high.astype(jnp.float32)
    mid = rest.astype(jnp.bfloat16)
    low = (rest - mid.astype(jnp.float32)).astype(jnp.bfloat16)
    parts = jnp.concatenate([low, mid, high], axis=1)
    query = lax.broadcasted_iota(jnp.int32, (tokens // QT, tokens), 0)
    token = lax.broadcasted_iota(jnp.int32, (tokens // QT, tokens), 1)
    ones = jnp.where(token // QT == query, 1.0, 0.0).astype(jnp.bfloat16)
    total = lax.dot_general(
        jnp.concatenate([ones] * 3, axis=1), parts, (((1,), (1,)), ((), ())), preferred_element_type=jnp.float32
    )
    return total * (1.0 / QT)


def best_tokens(left_of, sel, max_ref, piece):
    count, tokens = max_ref.shape
    for g in range(0, count, piece):
        dots = lax.dot_general(left_of(g, piece), sel, (((1,), (1,)), ((), ())), preferred_element_type=jnp.float32)
        max_ref[g:g + piece, :] = jnp.max(dots.reshape(piece, PT, tokens), axis=1)
    return max_ref[...]


def score_picked(sel, p_ref, max_ref):
    def left_of(g, piece):
        return p_ref[g:g + piece].reshape(piece * PT, DIM)

    return sum_tokens(best_tokens(left_of, sel, max_ref, 2 * GROUP))


def score_picked_few(sel, p_ref, wide_ref, max_ref):
    tokens, half = sel.shape[0], p_ref.shape[0] // 2
    wide_ref[...] = jnp.zeros_like(wide_ref)
    wide_ref[0:tokens, 0:DIM] = sel
    wide_ref[tokens:, DIM:] = sel

    def left_of(g, piece):
        return jnp.concatenate(
            [p_ref[h + g:h + g + piece].reshape(piece * PT, DIM) for h in (0, half)], axis=1
        )

    total = sum_tokens(best_tokens(left_of, wide_ref[...], max_ref, GROUP))
    queries = tokens // QT
    return jnp.concatenate([total[:queries], total[queries:]], axis=1)


def put(out_ref, place, total, n, slots_ref, owner):
    out_ref[place, 0:QB, :] = total[n * QB:(n + 1) * QB]
    out_ref[place, QB:QB + 1, :] = slots_ref[pl.ds(owner, 1), :]


def near_kernel(slots_ref, picks_ref, p_ref, *refs):
    q_refs, (out_ref, sel_ref, max_ref) = refs[:-3], refs[-3:]
    me = lax.axis_index("psg")
    owners = [near_owner(me, n, len(q_refs)) for n in range(len(q_refs))]
    for n, owner in enumerate(owners):
        sel_ref[n * QB * QT:(n + 1) * QB * QT, :] = picked(picks_ref, owner, q_refs[n])
    total = score_picked(sel_ref[...], p_ref, max_ref)
    for n, owner in enumerate(owners):
        put(out_ref, n, total, n, slots_ref, owner)


def some_far_kernel(steps, planes, slots_ref, p_ref, sel_ref, out_ref, wide_ref, max_ref):
    me = lax.axis_index("psg")
    total = score_picked_few(sel_ref[...], p_ref, wide_ref, max_ref)
    for n, step in enumerate(steps):
        put(out_ref, n, total, n, slots_ref, near_owner(me, step, planes) ^ 1)


def last_far_kernel(steps, planes, slots_ref, p_ref, sel_ref, near_ref, far_ref, out_ref, wide_ref, max_ref):
    me = lax.axis_index("psg")
    total = score_picked_few(sel_ref[...], p_ref, wide_ref, max_ref)
    for n, step in enumerate(steps):
        owner = near_owner(me, step, planes) ^ 1
        put(out_ref, owner, total, n, slots_ref, owner)
    others = [step for step in range(planes) if step not in steps]
    for step in range(planes):
        out_ref[near_owner(me, step, planes)] = near_ref[step]
    for n, step in enumerate(others):
        out_ref[near_owner(me, step, planes) ^ 1] = far_ref[n]


def all_kernel(slots_ref, picks_ref, p_ref, q_ref, out_ref, sel_ref, max_ref):
    some = q_ref.shape[0]
    for n in range(some):
        sel_ref[n * QB * QT:(n + 1) * QB * QT, :] = picked(picks_ref, n, q_ref.at[n])
    total = score_picked(sel_ref[...], p_ref, max_ref)
    for n in range(some):
        put(out_ref, n, total, n, slots_ref, n)


def score(kernel, tiles, some, few, passages, *more):
    count, tokens = passages.shape[0], some * QB * QT
    vmem = pl.BlockSpec(memory_space=pltpu.VMEM)
    if few:
        scratch = [pltpu.VMEM((2 * tokens, 2 * DIM), jnp.bfloat16), pltpu.VMEM((count // 2, 2 * tokens), jnp.float32)]
    else:
        scratch = [pltpu.VMEM((tokens, DIM), jnp.bfloat16), pltpu.VMEM((count, tokens), jnp.float32)]
    return pl.pallas_call(
        kernel,
        out_shape=jax.ShapeDtypeStruct((tiles, QB + 1, LANES), jnp.float32),
        in_specs=[vmem] * len(more),
        out_specs=vmem,
        scratch_shapes=scratch,
        compiler_params=pltpu.CompilerParams(vmem_limit_bytes=32 * 1024 * 1024),
        cost_estimate=pl.CostEstimate(
            flops=2 * passages.size * tokens, bytes_accessed=2 * passages.size, transcendentals=0
        ),
    )(*more)


def place_kernel(in_ref, out_ref):
    slots = out_ref.shape[-1]
    m = lax.broadcasted_iota(jnp.int32, (PBS, LANES), 0)
    for j in range(in_ref.shape[0]):
        row = in_ref[j, QB:QB + 1, :].astype(jnp.int32)
        where = jnp.minimum(row * PBS, LANES - PBS) + m
        for i in range(QB):
            tile = jnp.broadcast_to(in_ref[j, i:i + 1, :], (PBS, LANES))
            out_ref[j, i] = jnp.take_along_axis(tile, where, axis=1)[:, :slots]


def place(tiles, slots):
    vmem = pl.BlockSpec(memory_space=pltpu.VMEM)
    shards = tiles.shape[0]
    return pl.pallas_call(
        place_kernel,
        out_shape=jax.ShapeDtypeStruct((shards, QB, PBS, slots), jnp.float32),
        in_specs=[vmem],
        out_specs=vmem,
        compiler_params=pltpu.CompilerParams(vmem_limit_bytes=8 * 1024 * 1024),
    )(tiles)


def by_planes(own, shards, candidates, lengths, passages):
    planes = shards // 2

    def swap_sides(x):
        return lax.ppermute(x, "psg", [(j, j ^ 1) for j in range(shards)])

    def shift(x, step):
        return lax.ppermute(x, "psg", [(j, j ^ 2 * step) for j in range(shards)])

    theirs = swap_sides(candidates)
    shifted = [shift(own, step) for step in range(1, planes)]
    slots, picks, clean = prepare(shards, candidates, lengths, passages)
    clean, *early = lax.optimization_barrier((clean, *reversed(shifted[:planes // 2 - 1])))
    early, late = [own, *reversed(early)], shifted[planes // 2 - 1:]
    steps = list(range(planes))
    first, last = steps[:planes // 2], steps[planes // 2:]
    packed = pack(first, planes, theirs, early)
    first_far = swap_sides(packed)
    *late, _ = lax.optimization_barrier((*late, packed))
    last_far = swap_sides(pack(last, planes, theirs, late))
    near_tiles = score(near_kernel, planes, planes, False, clean, slots, picks, clean, *early, *late)
    first_far, near_tiles = lax.optimization_barrier((first_far, near_tiles))
    far_tiles = score(
        functools.partial(some_far_kernel, first, planes), len(first), len(first), True, clean, slots, clean, first_far
    )
    last_far, far_tiles = lax.optimization_barrier((last_far, far_tiles))
    return score(
        functools.partial(last_far_kernel, last, planes), shards, len(last), True, clean,
        slots, clean, last_far, near_tiles, far_tiles,
    )


def by_gather(own, shards, candidates, lengths, passages):
    slots, picks, clean = prepare(shards, candidates, lengths, passages)
    gathered = lax.all_gather(own, "psg", axis=0)
    some = min(shards, 8)

    def score_some(items):
        return score(all_kernel, some, some, False, clean, items[0], items[1], clean, items[2])

    parts = [x.reshape(shards // some, some, *x.shape[1:]) for x in (slots, picks, gathered)]
    return lax.map(score_some, parts).reshape(shards, QB + 1, LANES)


def per_device(queries, passages, lengths, candidates):
    shards = lax.axis_size("psg")
    rows = passages.shape[0] // PBS
    form = by_planes if shards == 8 else by_gather
    tiles = form(
        queries.reshape(QBD * QB * QT, DIM), shards, candidates.reshape(rows, KB), lengths, passages
    )
    tiles = lax.all_to_all(tiles, "psg", split_axis=0, concat_axis=0, tiled=True)
    return place(tiles, rows * KB // shards).transpose(0, 3, 1, 2)[None]


def solution(mesh):
    return jax.shard_map(
        per_device,
        mesh=mesh,
        in_specs=(
            P(("grp", "psg", "qry"), None, None),
            P(("grp", "psg"), None, None),
            P(("grp", "psg")),
            P("qry", ("grp", "psg"), None),
        ),
        out_specs=P(("grp", "psg", "qry"), None, None, None, None),
        check_vma=False,
    )
```

```python
import functools

import jax
import jax.numpy as jnp
from jax import lax
from jax.experimental import pallas as pl
from jax.experimental.pallas import tpu as pltpu
from jax.sharding import PartitionSpec as P

DIM = 128
QT = 32
PT = 64
QB = 2
QBD = 4
PBS = 16
KB = 32
LANES = 128
GROUP = 8


def prepare_kernel(
    cand_hbm, len_hbm, p_hbm, slots_ref, picks_ref, clean_ref, cand_ref, len_ref, raw_ref, sems
):
    rows = cand_ref.shape[0]
    shards = slots_ref.shape[0]
    groups = p_hbm.shape[0] // GROUP

    def fetch(g):
        part = pl.ds(g * GROUP, GROUP)
        return pltpu.make_async_copy(p_hbm.at[part], raw_ref.at[part], sems.at[g])

    fetch_cand = pltpu.make_async_copy(cand_hbm, cand_ref, sems.at[groups])
    fetch_len = pltpu.make_async_copy(len_hbm, len_ref, sems.at[groups + 1])
    fetch_cand.start()
    fetch_len.start()
    for g in range(groups):
        fetch(g).start()

    fetch_cand.wait()
    cand = cand_ref[...]
    owner = cand // QBD
    block = cand - owner * QBD
    lane = lax.broadcasted_iota(jnp.int32, (rows, LANES), 1).astype(jnp.float32)
    sub = lax.broadcasted_iota(jnp.int32, (rows, LANES), 0)
    for o in range(shards):
        mine = owner == o
        named = jnp.max(jnp.where(mine, block, 0), axis=1, keepdims=True)
        picks_ref[o:o + 1, :] = jnp.broadcast_to(jnp.max(named, axis=0, keepdims=True), (1, LANES))
        named_here = jnp.sum(jnp.where(mine, 1.0, 0.0), axis=1, keepdims=True)
        upto = jnp.broadcast_to(named_here, (rows, LANES))
        step = 1
        while step < rows:
            upto = upto + jnp.where(sub >= step, pltpu.roll(upto, step, 0), 0.0)
            step *= 2
        slots_ref[o:o + 1, :] = jnp.sum(jnp.where(upto <= lane, 1.0, 0.0), axis=0, keepdims=True)

    fetch_len.wait()
    u = lax.broadcasted_iota(jnp.int32, (PT, LANES), 0)

    @pl.loop(0, groups)
    def _(g):
        fetch(g).wait()
        for i in range(GROUP):
            p = g * GROUP + i
            tokens = raw_ref[p].astype(jnp.float32)
            clean_ref[p] = jnp.where(u < len_ref[p], tokens, tokens[0:1]).astype(jnp.bfloat16)


def prepare(shards, candidates, lengths, passages):
    hbm = pl.BlockSpec(memory_space=pltpu.HBM)
    vmem = pl.BlockSpec(memory_space=pltpu.VMEM)
    operands = [pltpu.with_memory_space_constraint(x, pltpu.HBM) for x in (candidates, lengths, passages)]
    return pl.pallas_call(
        prepare_kernel,
        out_shape=[
            jax.ShapeDtypeStruct((shards, LANES), jnp.float32),
            jax.ShapeDtypeStruct((shards, LANES), jnp.int32),
            jax.ShapeDtypeStruct(passages.shape, passages.dtype),
        ],
        in_specs=[hbm] * 3,
        out_specs=[vmem] * 3,
        scratch_shapes=[
            pltpu.VMEM(candidates.shape, candidates.dtype),
            pltpu.SMEM(lengths.shape, lengths.dtype),
            pltpu.VMEM(passages.shape, passages.dtype),
            pltpu.SemaphoreType.DMA((passages.shape[0] // GROUP + 2,)),
        ],
        compiler_params=pltpu.CompilerParams(vmem_limit_bytes=24 * 1024 * 1024),
        cost_estimate=pl.CostEstimate(flops=passages.size, bytes_accessed=2 * passages.size, transcendentals=0),
    )(*operands)


def near_owner(me, step, planes):
    return lax.rem((me >> 1) + planes - step, planes) << 1 | me & 1


def picked(picks_ref, owner, q_ref):
    pick = jnp.max(picks_ref[pl.ds(owner, 1), :])
    return q_ref[pl.ds(pick * QB * QT, QB * QT), :]


def pack_kernel(steps, planes, cand_ref, *refs):
    q_refs, out_ref = refs[:-1], refs[-1]
    me = lax.axis_index("psg")
    cand = cand_ref[...]
    owner = cand // QBD
    block = cand - owner * QBD
    for n, step in enumerate(steps):
        pick = jnp.max(jnp.where(owner == near_owner(me, step, planes), block, 0))
        out_ref[n * QB * QT:(n + 1) * QB * QT, :] = q_refs[n][pl.ds(pick * QB * QT, QB * QT), :]


def pack(steps, planes, candidates, blocks):
    vmem = pl.BlockSpec(memory_space=pltpu.VMEM)
    return pl.pallas_call(
        functools.partial(pack_kernel, steps, planes),
        out_shape=jax.ShapeDtypeStruct((len(blocks) * QB * QT, DIM), blocks[0].dtype),
        in_specs=[vmem] * (1 + len(blocks)),
        out_specs=vmem,
        compiler_params=pltpu.CompilerParams(vmem_limit_bytes=4 * 1024 * 1024),
    )(candidates, *blocks)


def sum_tokens(best):
    tokens = best.shape[1]
    high = best.astype(jnp.bfloat16)
    rest = best - high.astype(jnp.float32)
    mid = rest.astype(jnp.bfloat16)
    low = (rest - mid.astype(jnp.float32)).astype(jnp.bfloat16)
    parts = jnp.concatenate([low, mid, high], axis=1)
    query = lax.broadcasted_iota(jnp.int32, (tokens // QT, tokens), 0)
    token = lax.broadcasted_iota(jnp.int32, (tokens // QT, tokens), 1)
    ones = jnp.where(token // QT == query, 1.0, 0.0).astype(jnp.bfloat16)
    total = lax.dot_general(
        jnp.concatenate([ones] * 3, axis=1), parts, (((1,), (1,)), ((), ())), preferred_element_type=jnp.float32
    )
    return total * (1.0 / QT)


def best_tokens(left_of, sel, max_ref, piece):
    count, tokens = max_ref.shape
    for g in range(0, count, piece):
        dots = lax.dot_general(left_of(g, piece), sel, (((1,), (1,)), ((), ())), preferred_element_type=jnp.float32)
        max_ref[g:g + piece, :] = jnp.max(dots.reshape(piece, PT, tokens), axis=1)
    return max_ref[...]


def score_picked(sel, p_ref, max_ref):
    def left_of(g, piece):
        return p_ref[g:g + piece].reshape(piece * PT, DIM)

    return sum_tokens(best_tokens(left_of, sel, max_ref, 2 * GROUP))


def score_picked_few(sel, p_ref, wide_ref, max_ref):
    tokens, half = sel.shape[0], p_ref.shape[0] // 2
    wide_ref[...] = jnp.zeros_like(wide_ref)
    wide_ref[0:tokens, 0:DIM] = sel
    wide_ref[tokens:, DIM:] = sel

    def left_of(g, piece):
        return jnp.concatenate(
            [p_ref[h + g:h + g + piece].reshape(piece * PT, DIM) for h in (0, half)], axis=1
        )

    total = sum_tokens(best_tokens(left_of, wide_ref[...], max_ref, 2 * GROUP))
    queries = tokens // QT
    return jnp.concatenate([total[:queries], total[queries:]], axis=1)


def put(out_ref, place, total, n, slots_ref, owner):
    out_ref[place, 0:QB, :] = total[n * QB:(n + 1) * QB]
    out_ref[place, QB:QB + 1, :] = slots_ref[pl.ds(owner, 1), :]


def near_kernel(slots_ref, picks_ref, p_ref, *refs):
    q_refs, (out_ref, sel_ref, max_ref) = refs[:-3], refs[-3:]
    me = lax.axis_index("psg")
    owners = [near_owner(me, n, len(q_refs)) for n in range(len(q_refs))]
    for n, owner in enumerate(owners):
        sel_ref[n * QB * QT:(n + 1) * QB * QT, :] = picked(picks_ref, owner, q_refs[n])
    total = score_picked(sel_ref[...], p_ref, max_ref)
    for n, owner in enumerate(owners):
        put(out_ref, n, total, n, slots_ref, owner)


def some_far_kernel(steps, planes, slots_ref, p_ref, sel_ref, out_ref, wide_ref, max_ref):
    me = lax.axis_index("psg")
    total = score_picked_few(sel_ref[...], p_ref, wide_ref, max_ref)
    for n, step in enumerate(steps):
        put(out_ref, n, total, n, slots_ref, near_owner(me, step, planes) ^ 1)


def last_far_kernel(steps, planes, slots_ref, p_ref, sel_ref, near_ref, far_ref, out_ref, wide_ref, max_ref):
    me = lax.axis_index("psg")
    total = score_picked_few(sel_ref[...], p_ref, wide_ref, max_ref)
    for n, step in enumerate(steps):
        owner = near_owner(me, step, planes) ^ 1
        put(out_ref, owner, total, n, slots_ref, owner)
    others = [step for step in range(planes) if step not in steps]
    for step in range(planes):
        out_ref[near_owner(me, step, planes)] = near_ref[step]
    for n, step in enumerate(others):
        out_ref[near_owner(me, step, planes) ^ 1] = far_ref[n]


def all_kernel(slots_ref, picks_ref, p_ref, q_ref, out_ref, sel_ref, max_ref):
    some = q_ref.shape[0]
    for n in range(some):
        sel_ref[n * QB * QT:(n + 1) * QB * QT, :] = picked(picks_ref, n, q_ref.at[n])
    total = score_picked(sel_ref[...], p_ref, max_ref)
    for n in range(some):
        put(out_ref, n, total, n, slots_ref, n)


def score(kernel, tiles, some, few, passages, *more):
    count, tokens = passages.shape[0], some * QB * QT
    vmem = pl.BlockSpec(memory_space=pltpu.VMEM)
    if few:
        scratch = [pltpu.VMEM((2 * tokens, 2 * DIM), jnp.bfloat16), pltpu.VMEM((count // 2, 2 * tokens), jnp.float32)]
    else:
        scratch = [pltpu.VMEM((tokens, DIM), jnp.bfloat16), pltpu.VMEM((count, tokens), jnp.float32)]
    return pl.pallas_call(
        kernel,
        out_shape=jax.ShapeDtypeStruct((tiles, QB + 1, LANES), jnp.float32),
        in_specs=[vmem] * len(more),
        out_specs=vmem,
        scratch_shapes=scratch,
        compiler_params=pltpu.CompilerParams(vmem_limit_bytes=32 * 1024 * 1024),
        cost_estimate=pl.CostEstimate(
            flops=2 * passages.size * tokens, bytes_accessed=2 * passages.size, transcendentals=0
        ),
    )(*more)


def place_kernel(in_ref, out_ref):
    slots = out_ref.shape[-1]
    m = lax.broadcasted_iota(jnp.int32, (PBS, LANES), 0)
    for j in range(in_ref.shape[0]):
        row = in_ref[j, QB:QB + 1, :].astype(jnp.int32)
        where = jnp.minimum(row * PBS, LANES - PBS) + m
        for i in range(QB):
            tile = jnp.broadcast_to(in_ref[j, i:i + 1, :], (PBS, LANES))
            out_ref[j, i] = jnp.take_along_axis(tile, where, axis=1)[:, :slots]


def place(tiles, slots):
    vmem = pl.BlockSpec(memory_space=pltpu.VMEM)
    shards = tiles.shape[0]
    return pl.pallas_call(
        place_kernel,
        out_shape=jax.ShapeDtypeStruct((shards, QB, PBS, slots), jnp.float32),
        in_specs=[vmem],
        out_specs=vmem,
        compiler_params=pltpu.CompilerParams(vmem_limit_bytes=8 * 1024 * 1024),
    )(tiles)


def by_planes(own, shards, candidates, lengths, passages):
    planes = shards // 2

    def swap_sides(x):
        return lax.ppermute(x, "psg", [(j, j ^ 1) for j in range(shards)])

    def shift(x, step):
        return lax.ppermute(x, "psg", [(j, (j + 2 * step) % shards) for j in range(shards)])

    theirs = swap_sides(candidates)
    shifted = [shift(own, step) for step in range(1, planes)]
    slots, picks, clean = prepare(shards, candidates, lengths, passages)
    clean, *early = lax.optimization_barrier((clean, *reversed(shifted[:planes // 2 - 1])))
    early, late = [own, *reversed(early)], shifted[planes // 2 - 1:]
    steps = list(range(planes))
    first, last = steps[:planes // 2], steps[planes // 2:]
    packed = pack(first, planes, theirs, early)
    first_far = swap_sides(packed)
    *late, _ = lax.optimization_barrier((*reversed(late), packed))
    late = late[::-1]
    last_far = swap_sides(pack(last, planes, theirs, late))
    near_tiles = score(near_kernel, planes, planes, False, clean, slots, picks, clean, *early, *late)
    first_far, near_tiles = lax.optimization_barrier((first_far, near_tiles))
    far_tiles = score(
        functools.partial(some_far_kernel, first, planes), len(first), len(first), True, clean, slots, clean, first_far
    )
    last_far, far_tiles = lax.optimization_barrier((last_far, far_tiles))
    return score(
        functools.partial(last_far_kernel, last, planes), shards, len(last), True, clean,
        slots, clean, last_far, near_tiles, far_tiles,
    )


def by_gather(own, shards, candidates, lengths, passages):
    slots, picks, clean = prepare(shards, candidates, lengths, passages)
    gathered = lax.all_gather(own, "psg", axis=0)
    some = min(shards, 8)

    def score_some(items):
        return score(all_kernel, some, some, False, clean, items[0], items[1], clean, items[2])

    parts = [x.reshape(shards // some, some, *x.shape[1:]) for x in (slots, picks, gathered)]
    return lax.map(score_some, parts).reshape(shards, QB + 1, LANES)


def per_device(queries, passages, lengths, candidates):
    shards = lax.axis_size("psg")
    rows = passages.shape[0] // PBS
    form = by_planes if shards == 8 else by_gather
    tiles = form(
        queries.reshape(QBD * QB * QT, DIM), shards, candidates.reshape(rows, KB), lengths, passages
    )
    tiles = lax.all_to_all(tiles, "psg", split_axis=0, concat_axis=0, tiled=True)
    return place(tiles, rows * KB // shards).transpose(0, 3, 1, 2)[None]


def solution(mesh):
    return jax.shard_map(
        per_device,
        mesh=mesh,
        in_specs=(
            P(("grp", "psg", "qry"), None, None),
            P(("grp", "psg"), None, None),
            P(("grp", "psg")),
            P("qry", ("grp", "psg"), None),
        ),
        out_specs=P(("grp", "psg", "qry"), None, None, None, None),
        check_vma=False,
    )
```
